32 devices in a mesh: seq: 8 (over z, x), head: 4 (over y, core).
Axes of the slice: x: 2, y: 2, z: 4, core: 2. Of those that a mesh axis runs over, the one named last changes fastest.
Arguments:
- inputs: float32 [8192, 4096], P('seq', 'head'), may hold values from -6 to 6
- cotangent: float32 [8192, 4096], P('seq', 'head'), may hold values from -1.5 to 1.5
- b_proj: float32 [8192, 128], P('seq'), may hold values from -1.8 to 1.8
- c_proj: float32 [8192, 128], P('seq'), may hold values from -1.8 to 1.8
- decay_rate: float32 [64], P('head'), may hold values from 1e-06 to 0.0001
- level_weight: float32 [8, 64, 8192], P(None, 'head', 'seq'), may hold values from 0 to 2, as said below
- starts: int32 [128], P('seq'), may hold values from 0 to 1, as said below
Outputs:
- grad_x: float32 [8192, 4096], P('seq', 'head')
- grad_b: float32 [8192, 128], P(('seq', 'head'))
- grad_c: float32 [8192, 128], P(('seq', 'head'))
- grad_level: float32 [8, 64, 8192], P(None, 'head', 'seq')
The draws below stay inside these ranges and needn't reach their ends.
Inputs may be any that keep to these rules, and one draw needn't show every extreme that they name: `starts`: exactly two of the 128 stretches carry 1. `level_weight`: positive.
All inputs are finite; a program needn't handle non-finite values.
Results may differ from the reference program's by a relative error of at most 0.0001.
Values sent between devices are 32-bit elements; how exact they have to be, the bound alone decides.
No kernel may reach another device: no remote copies, remote signals or barrier semaphores. Data moves between devices by JAX's collectives and lax.ppermute only.
A program may use at most 128 MiB of HBM per device.

```python
import math
import jax
import jax.numpy as jnp
from jax import lax

HEADS = 64
HEAD_DIM = 64
STATE = 128
STRETCH = 64
TOK_DEV = 1024
TOKENS = 8192
STRETCHES = 128
CH_BITS = 4
SEQ_BITS = 3
LEVELS = 8
N_SEQ = 8


def draw_level_weight(key, part):
    key_spread = jax.random.fold_in(key, 11)
    key_forget = jax.random.fold_in(key, 12)
    level_ids = jnp.arange(LEVELS, dtype=jnp.float32)[:, None, None]
    spread = jnp.exp(jax.random.uniform(key_spread, (LEVELS, HEADS, TOKENS), jnp.float32, math.log(0.5), math.log(2.0)))
    forget = jax.random.uniform(key_forget, (HEADS,), jnp.float32, 0.0, 0.6)
    return spread * jnp.exp(-forget[None, :, None] * level_ids)


def draw_starts(key, part):
    shuffled = jax.random.permutation(jax.random.fold_in(key, 21), STRETCHES)
    return (shuffled < 2).astype(jnp.int32)


def levels(key, shape, cuts, smallest, largest):
    gain = 1.0
    for axis_at, parts in cuts:
        draws = jax.random.uniform(jax.random.fold_in(jax.random.fold_in(key, 6), axis_at), (parts,), jnp.float32, smallest / len(cuts), largest / len(cuts))
        gain = gain * jnp.repeat(jnp.exp(draws), shape[axis_at] // parts).reshape((-1,) + (1,) * (len(shape) - 1 - axis_at))
    return gain


def normal_values(stream_key, shape, scale, most, split=(), held_as=jnp.bfloat16):
    result = jax.random.normal(stream_key, shape, jnp.float32) * scale
    if len(split) > 0:
        result = levels(stream_key, shape, split, -0.22, 0.18) * result
    return jnp.clip(result, min=-most, max=most).astype(held_as)


def setup_inputs(seed: int = 0) -> dict:
    key_of = jax.random.split(jax.random.key(seed), 8)
    return {
        "inputs": normal_values(key_of[0], (TOKENS, HEADS * HEAD_DIM), 1.0, 6.0, ((0, 8), (1, 4)), jnp.float32),
        "cotangent": normal_values(key_of[1], (TOKENS, HEADS * HEAD_DIM), 0.25, 1.5, ((0, 8), (1, 4)), jnp.float32),
        "b_proj": normal_values(key_of[2], (TOKENS, STATE), 0.3, 1.8, ((0, 8),), jnp.float32),
        "c_proj": normal_values(key_of[3], (TOKENS, STATE), 0.3, 1.8, ((0, 8),), jnp.float32),
        "decay_rate": jnp.clip(jnp.exp(math.log(0.0001) - 4.6051702 * jax.random.uniform(key_of[4], (HEADS,), jnp.float32) ** levels(key_of[4], (HEADS,), ((0, 4),), -0.2, 0.2)), 9.999999974752427e-07, 0.0001),
        "level_weight": draw_level_weight(jax.random.fold_in(key_of[7], 71), 0),
        "starts": draw_starts(jax.random.fold_in(key_of[7], 71), 0),
    }


def reference(inputs, cotangent, b_proj, c_proj, decay_rate, level_weight, starts):
    highest = lax.Precision.HIGHEST
    total = TOKENS
    width = HEAD_DIM
    state_dim = STATE
    blocks = N_SEQ
    block_len = TOK_DEV
    level_scale = (STRETCH * 2.0 ** jnp.arange(LEVELS, dtype=jnp.float32)) ** -0.5
    level_vals = level_weight * level_scale[:, None, None]
    doc_ids = jnp.cumsum(starts).astype(jnp.int32)
    doc_rows = doc_ids[(jnp.arange(total) // STRETCH).astype(jnp.int32)]
    position = jnp.arange(total).astype(jnp.float32)
    local_stretch = (jnp.arange(block_len) // STRETCH).astype(jnp.int32)
    differ = local_stretch[:, None] ^ local_stretch[None, :]
    local_level = jnp.zeros_like(differ)
    for level_bit in range(CH_BITS):
        local_level = local_level + (differ >= 2 ** level_bit).astype(jnp.int32)
    rows_idx = jnp.arange(block_len)
    causal = rows_idx[:, None] >= rows_idx[None, :]
    doc_block = doc_rows.reshape(blocks, block_len)
    valid = causal[None] & (doc_block[:, :, None] == doc_block[:, None, :])
    distance = (rows_idx[:, None] - rows_idx[None, :]).astype(jnp.float32)
    c_blocks = c_proj.reshape(blocks, block_len, state_dim)
    b_blocks = b_proj.reshape(blocks, block_len, state_dim)
    scores = jnp.einsum('btn,bsn->bts', c_blocks, b_blocks, precision=highest)
    x_heads = inputs.reshape(total, HEADS, width)
    cot_heads = cotangent.reshape(total, HEADS, width)

    def head_step(carry, pieces):
        acc_b, acc_c = carry
        x_one, cot_one, rate, lam_one = pieces
        x_blk = x_one.reshape(blocks, block_len, width)
        cot_blk = cot_one.reshape(blocks, block_len, width)
        decayed = jnp.where(valid, jnp.exp(-rate * distance)[None], 0.0)
        lam_rows = lam_one.reshape(LEVELS, blocks, block_len)
        lam_pair = jnp.zeros((blocks, block_len, block_len), jnp.float32)
        for level in range(CH_BITS + 1):
            lam_pair = jnp.where(local_level[None] == level, lam_rows[level][:, :, None], lam_pair)
        inner = jnp.einsum('btp,bsp->bts', cot_blk, x_blk, precision=highest)
        kernel = decayed * lam_pair
        weighted = kernel * scores
        mixed = kernel * inner
        plain = decayed * scores * inner
        grad_x_one = jnp.einsum('bts,btp->bsp', weighted, cot_blk, precision=highest).reshape(total, width)
        grad_c_one = jnp.einsum('bts,bsn->btn', mixed, b_blocks, precision=highest).reshape(total, state_dim)
        grad_b_one = jnp.einsum('bts,btn->bsn', mixed, c_blocks, precision=highest).reshape(total, state_dim)
        local_grads = jnp.stack([jnp.sum(jnp.where(local_level[None] == level, plain, 0.0), axis=2) for level in range(CH_BITS + 1)])
        level_rows = [local_grads.reshape(CH_BITS + 1, total)]
        for level_bit in range(SEQ_BITS):
            span = block_len * 2 ** level_bit
            groups = total // (2 * span)
            level = CH_BITS + 1 + level_bit
            pos_grp = position.reshape(groups, 2, span)
            bound = pos_grp[:, 1, 0]
            key_off = bound[:, None] - pos_grp[:, 0]
            query_off = pos_grp[:, 1] - bound[:, None]
            doc_grp = doc_rows.reshape(groups, 2, span)
            doc_end = doc_grp[:, 0, span - 1]
            key_wt = jnp.where(doc_grp[:, 0] == doc_end[:, None], jnp.exp(-rate * key_off), 0.0)
            query_wt = jnp.where(doc_grp[:, 1] == doc_end[:, None], jnp.exp(-rate * query_off), 0.0)
            lam_query = lam_one[level].reshape(groups, 2, span)[:, 1] * query_wt
            b_grp = b_proj.reshape(groups, 2, span, state_dim)
            c_grp = c_proj.reshape(groups, 2, span, state_dim)
            x_grp = x_one.reshape(groups, 2, span, width)
            cot_grp = cot_one.reshape(groups, 2, span, width)
            key_state = jnp.einsum('gsn,gsp->gnp', b_grp[:, 0] * key_wt[..., None], x_grp[:, 0], precision=highest)
            applied = jnp.einsum('gnp,gtp->gtn', key_state, cot_grp[:, 1], precision=highest)
            grad_c_up = lam_query[..., None] * applied
            grad_lam_up = query_wt * jnp.sum(c_grp[:, 1] * applied, axis=-1)
            query_state = jnp.einsum('gtn,gtp->gnp', c_grp[:, 1] * lam_query[..., None], cot_grp[:, 1], precision=highest)
            grad_x_low = key_wt[..., None] * jnp.einsum('gsn,gnp->gsp', b_grp[:, 0], query_state, precision=highest)
            grad_b_low = key_wt[..., None] * jnp.einsum('gnp,gsp->gsn', query_state, x_grp[:, 0], precision=highest)
            grad_x_one = grad_x_one + jnp.stack([grad_x_low, jnp.zeros_like(grad_x_low)], 1).reshape(total, width)
            grad_c_one = grad_c_one + jnp.stack([jnp.zeros_like(grad_c_up), grad_c_up], 1).reshape(total, state_dim)
            grad_b_one = grad_b_one + jnp.stack([grad_b_low, jnp.zeros_like(grad_b_low)], 1).reshape(total, state_dim)
            level_rows.append(jnp.stack([jnp.zeros_like(grad_lam_up), grad_lam_up], 1).reshape(1, total))
        grad_lam_one = jnp.concatenate(level_rows, 0) * level_scale[:, None]
        return (acc_b + grad_b_one, acc_c + grad_c_one), (grad_x_one, grad_lam_one)

    start_acc = (jnp.zeros((total, state_dim), jnp.float32), jnp.zeros((total, state_dim), jnp.float32))
    pieces = (jnp.transpose(x_heads, (1, 0, 2)), jnp.transpose(cot_heads, (1, 0, 2)), decay_rate, jnp.transpose(level_vals, (1, 0, 2)))
    (grad_b, grad_c), (grad_x_all, grad_lam_all) = lax.scan(head_step, start_acc, pieces)
    grad_x = jnp.transpose(grad_x_all, (1, 0, 2)).reshape(total, HEADS * width)
    grad_level = jnp.transpose(grad_lam_all, (1, 0, 2))
    return grad_x, grad_b, grad_c, grad_level
```

```python
import jax
import jax.numpy as jnp
from jax import lax
from jax.sharding import PartitionSpec as P

STRETCH = 64
HIGH = lax.Precision.HIGH


def partner(x, apart):
    return lax.ppermute(x, "seq", [(i, i ^ apart) for i in range(lax.axis_size("seq"))])


def all_clean_flags(own, me):
    held = own.reshape(1)
    apart = 1
    while apart < lax.axis_size("seq"):
        other = partner(held, apart)
        high = (me & apart) != 0
        held = jnp.where(
            high, jnp.concatenate([other, held]), jnp.concatenate([held, other])
        )
        apart *= 2
    return held


def gate_of(flags, device, level_bit):
    ids = jnp.arange(flags.shape[0])
    first = (device >> level_bit) << level_bit
    last = first + (1 << level_bit) - 1
    upper = ((device >> level_bit) & 1) == 1
    between = jnp.where(upper, (ids >= first) & (ids < device), (ids > device) & (ids <= last))
    return jnp.min(jnp.where(between, flags, 1.0))


def swap_block_sums(v, flags, me, level_bit):
    gated = False
    for bit in reversed(range(level_bit)):
        half = v.shape[0] // 2
        high = (me >> bit) & 1
        away = lax.dynamic_slice_in_dim(v, (1 - high) * half, half)
        kept = lax.dynamic_slice_in_dim(v, high * half, half)
        came = partner(away, 1 << bit)
        if gated:
            v = kept + came
        else:
            v = gate_of(flags, me, level_bit) * kept + gate_of(flags, me ^ (1 << bit), level_bit) * came
            gated = True
    v = partner(v, 1 << level_bit)
    for bit in range(level_bit):
        came = partner(v, 1 << bit)
        high = ((me >> bit) & 1) == 1
        v = jnp.where(high, jnp.concatenate([came, v]), jnp.concatenate([v, came]))
    return v


def scatter_heads(x):
    count = lax.axis_size("head")
    me = lax.axis_index("head")
    bits = count.bit_length() - 1
    x = x.reshape((2,) * bits + (x.shape[0] // count,) + x.shape[1:])
    for bit in range(bits):
        axis = x.ndim - 3 - bit if False else bits - 1 - bit
        high = (me >> bit) & 1
        away = lax.dynamic_index_in_dim(x, 1 - high, axis, keepdims=False)
        kept = lax.dynamic_index_in_dim(x, high, axis, keepdims=False)
        came = lax.ppermute(away, "head", [(i, i ^ (1 << bit)) for i in range(count)])
        x = kept + came
    return x


def local(inputs, cotangent, b_proj, c_proj, decay_rate, level_weight, starts):
    rows = inputs.shape[0]
    heads = decay_rate.shape[0]
    width = inputs.shape[1] // heads
    stretches = rows // STRETCH
    local_bits = stretches.bit_length() - 1
    seq_count = lax.axis_size("seq")
    seq_bits = seq_count.bit_length() - 1
    me = lax.axis_index("seq")
    level_count = level_weight.shape[0]
    scale = (STRETCH * 2.0 ** jnp.arange(level_count, dtype=jnp.float32)) ** (-0.5)
    lam = jnp.transpose(level_weight * scale[:, None, None], (0, 2, 1))
    lam = jnp.repeat(lam, width, axis=2)
    position = (me * rows + jnp.arange(rows) - seq_count * rows // 2).astype(jnp.float32)
    rate = jnp.repeat(decay_rate, width)
    x = inputs * jnp.exp(position[:, None] * rate[None, :])
    cot = cotangent * jnp.exp(-position[:, None] * rate[None, :])

    ids = jnp.arange(stretches)
    opened = starts.astype(jnp.float32)
    doc = jnp.sum(jnp.where(ids[None, :] <= ids[:, None], opened[None, :], 0.0), 1)
    total = jnp.sum(opened)
    prefix = jnp.repeat(jnp.where(doc == 0.0, 1.0, 0.0), STRETCH)
    suffix = jnp.repeat(jnp.where(doc == total, 1.0, 0.0), STRETCH)
    doc_rows = jnp.repeat(doc, STRETCH)
    flags = all_clean_flags(jnp.where(total == 0.0, 1.0, 0.0), me)

    uppers = [((me >> b) & 1) == 1 for b in range(seq_bits)]
    c_open = c_proj * prefix[:, None]
    b_open = b_proj * suffix[:, None]
    sent = []
    for b in range(seq_bits):
        z = jnp.where(uppers[b], cot * lam[local_bits + 1 + b], x)
        w = jnp.where(uppers[b], c_open, b_open)
        sent.append(jnp.einsum("tn,td->nd", w, z, precision=HIGH))
    states = [swap_block_sums(sent[b], flags, me, b) for b in range(seq_bits)]

    segment = jnp.repeat(jnp.eye(heads, dtype=jnp.float32), width, axis=0)
    grad_x = jnp.zeros((rows, heads * width), jnp.float32)
    grad_b = jnp.zeros_like(b_proj)
    grad_c = jnp.zeros_like(c_proj)
    grad_lam = []

    def put(low, high):
        low = jnp.zeros_like(high) if low is None else low
        high = jnp.zeros_like(low) if high is None else high
        return jnp.stack([low, high], 1).reshape((rows,) + low.shape[2:])

    for level in range(local_bits + 1):
        z = cot * lam[level]
        if level == 0:
            def split(a, upper):
                return a.reshape((stretches, STRETCH) + a.shape[1:])
            span = STRETCH
        else:
            span = STRETCH << (level - 1)

            def split(a, upper, span=span):
                return a.reshape((rows // (2 * span), 2, span) + a.shape[1:])[:, int(upper)]
        valid = split(doc_rows, True)[:, :, None] == split(doc_rows, False)[:, None, :]
        if level == 0:
            valid = valid & (jnp.arange(span)[:, None] >= jnp.arange(span)[None, :])
        s = jnp.einsum("gtn,gsn->gts", split(c_proj, True), split(b_proj, False), precision=HIGH)
        s = jnp.where(valid, s, 0.0)
        y = jnp.einsum("gts,gsd->gtd", s, split(x, False), precision=HIGH)
        gl = jnp.dot(split(cot, True) * y, segment, precision=HIGH)
        gx = jnp.einsum("gts,gtd->gsd", s, split(z, True), precision=HIGH)
        m = jnp.einsum("gtd,gsd->gts", split(z, True), split(x, False), precision=HIGH)
        m = jnp.where(valid, m, 0.0)
        gc = jnp.einsum("gts,gsn->gtn", m, split(b_proj, False), precision=HIGH)
        gb = jnp.einsum("gts,gtn->gsn", m, split(c_proj, True), precision=HIGH)
        if level == 0:
            grad_x = grad_x + gx.reshape(grad_x.shape)
            grad_b = grad_b + gb.reshape(grad_b.shape)
            grad_c = grad_c + gc.reshape(grad_c.shape)
            grad_lam.append(gl.reshape(rows, heads))
        else:
            grad_x = grad_x + put(gx, None)
            grad_b = grad_b + put(gb, None)
            grad_c = grad_c + put(None, gc)
            grad_lam.append(put(None, gl))
    for b in range(seq_bits):
        gate = gate_of(flags, me, b)
        state = states[b] * gate
        up = jnp.where(uppers[b], 1.0, 0.0)
        p = jnp.where(uppers[b], c_open, b_open)
        z = jnp.where(uppers[b], cot * lam[local_bits + 1 + b], x)
        g = jnp.dot(p, state, precision=HIGH)
        h = jnp.einsum("td,nd->tn", z, state, precision=HIGH)
        grad_x = grad_x + (1.0 - up) * g
        grad_lam.append(jnp.dot(cot * g, segment, precision=HIGH) * up)
        grad_c = grad_c + up * h * prefix[:, None]
        grad_b = grad_b + (1.0 - up) * h * suffix[:, None]
    grad_x = grad_x * jnp.exp(position[:, None] * rate[None, :])
    grad_level = jnp.transpose(jnp.stack(grad_lam), (0, 2, 1)) * scale[:, None, None]
    return (grad_x, scatter_heads(grad_b), scatter_heads(grad_c), grad_level)


def solution(mesh):
    return jax.shard_map(
        local,
        mesh=mesh,
        in_specs=(
            P("seq", "head"),
            P("seq", "head"),
            P("seq", None),
            P("seq", None),
            P("head"),
            P(None, "head", "seq"),
            P("seq"),
        ),
        out_specs=(
            P("seq", "head"),
            P(("seq", "head"), None),
            P(("seq", "head"), None),
            P(None, "head", "seq"),
        ),
        check_vma=False,
    )
```

```python
import functools

import jax
import jax.numpy as jnp
from jax import lax
from jax.experimental import pallas as pl
from jax.experimental.pallas import tpu as pltpu
from jax.sharding import PartitionSpec as P

KERNELS = True
STRETCH = 64
WIDTH = 64
CHUNK = 256
LANES = 128
F32 = jnp.float32
BF16 = jnp.bfloat16


def partner(x, apart):
    return lax.ppermute(x, "seq", [(i, i ^ apart) for i in range(lax.axis_size("seq"))])


def all_clean_flags(own, me):
    held = own.reshape(1)
    apart = 1
    while apart < lax.axis_size("seq"):
        other = partner(held, apart)
        high = (me & apart) != 0
        held = jnp.where(
            high, jnp.concatenate([other, held]), jnp.concatenate([held, other])
        )
        apart *= 2
    return held


def gate_of(flags, device, level_bit):
    ids = jnp.arange(flags.shape[0])
    first = (device >> level_bit) << level_bit
    last = first + (1 << level_bit) - 1
    upper = ((device >> level_bit) & 1) == 1
    between = jnp.where(upper, (ids >= first) & (ids < device), (ids > device) & (ids <= last))
    return jnp.min(jnp.where(between, flags, 1.0))


def swap_block_sums(v, flags, me, level_bit):
    gated = False
    for bit in reversed(range(level_bit)):
        half = v.shape[0] // 2
        high = (me >> bit) & 1
        away = lax.dynamic_slice_in_dim(v, (1 - high) * half, half)
        kept = lax.dynamic_slice_in_dim(v, high * half, half)
        came = partner(away, 1 << bit)
        if gated:
            v = kept + came
        else:
            v = gate_of(flags, me, level_bit) * kept + gate_of(flags, me ^ (1 << bit), level_bit) * came
            gated = True
    v = partner(v, 1 << level_bit)
    for bit in range(level_bit):
        came = partner(v, 1 << bit)
        high = ((me >> bit) & 1) == 1
        v = jnp.where(high, jnp.concatenate([came, v]), jnp.concatenate([v, came]))
    return v


def scatter_heads(x):
    count = lax.axis_size("head")
    me = lax.axis_index("head")
    bits = count.bit_length() - 1
    x = x.reshape((2,) * bits + (x.shape[0] // count,) + x.shape[1:])
    for bit in range(bits):
        axis = bits - 1 - bit
        high = (me >> bit) & 1
        away = lax.dynamic_index_in_dim(x, 1 - high, axis, keepdims=False)
        kept = lax.dynamic_index_in_dim(x, high, axis, keepdims=False)
        came = lax.ppermute(away, "head", [(i, i ^ (1 << bit)) for i in range(count)])
        x = kept + came
    return x


def split(a):
    hi = a.astype(BF16)
    return hi, (a - hi.astype(F32)).astype(BF16)


def dot(a, b):
    return lax.dot_general(a, b, (((1,), (0,)), ((), ())), preferred_element_type=F32)


def dot_nt(a, b):
    return lax.dot_general(a, b, (((1,), (1,)), ((), ())), preferred_element_type=F32)


def open_product(info, first, last):
    r = jnp.float32(1.0)
    for k in range(first, last + 1):
        r = r * (1 - info[1 + k]).astype(F32)
    return r


def query_open(info, level, i):
    mid = ((i >> level) << level) + (1 << (level - 1))
    return open_product(info, mid, i)


def key_open(info, level, j):
    mid = ((j >> level) << level) + (1 << (level - 1))
    return open_product(info, j + 1, mid - 1)


def scaled_rows(a, factors):
    return jnp.concatenate(
        [a[STRETCH * k : STRETCH * (k + 1)] * f for k, f in enumerate(factors)], 0
    )


def decays(rate_ref, chunk, base, sign, stretches):
    per = CHUNK // WIDTH
    lane_head = lax.broadcasted_iota(jnp.int32, (1, CHUNK), 1) // WIDTH
    row = jnp.zeros((1, CHUNK), F32)
    for k in range(per):
        row = jnp.where(lane_head == k, rate_ref[chunk * per + k], row)
    within = lax.broadcasted_iota(jnp.int32, (STRETCH, CHUNK), 0).astype(F32)
    across = lax.broadcasted_iota(jnp.int32, (stretches, CHUNK), 0).astype(F32) * STRETCH + base
    return jnp.exp(sign * within * row), jnp.exp(sign * across * row)


def decayed(a, tables, i, first=0):
    inner, outer = tables
    return a[STRETCH * i : STRETCH * (i + 1), :] * (inner * outer[first + i : first + i + 1, :])


def weight_of(lam, level, chunk, heads):
    rows = lam.shape[0]
    per = LANES // WIDTH
    lane = lax.broadcasted_iota(jnp.int32, (rows, LANES), 1) // WIDTH
    out = []
    for piece in range(CHUNK // LANES):
        at = lane + (level * heads + piece * per + chunk * (CHUNK // WIDTH))
        out.append(jnp.take_along_axis(lam, at, axis=1))
    return jnp.concatenate(out, 1)


def head_sums(level, chunk, heads):
    d = lax.broadcasted_iota(jnp.int32, (CHUNK, LANES), 0) // WIDTH
    lane = lax.broadcasted_iota(jnp.int32, (CHUNK, LANES), 1)
    return jnp.where(lane == d + (level * heads + chunk * (CHUNK // WIDTH)), 1.0, 0.0).astype(BF16)


def level_scales(shape, axis, heads):
    shift = heads.bit_length() - 1
    level = (lax.broadcasted_iota(jnp.int32, shape, axis) >> shift).astype(F32)
    return jnp.exp2(-0.5 * level - 0.5 * (STRETCH.bit_length() - 1))


def send_kernel(heads, level, level_bit, half, first, info, rate_ref, x_ref, cot_ref, b_ref, c_ref, lam_ref, *rest):
    if first:
        v_ref, lam_out, wt, zh, zl = rest
    else:
        v_ref, wt, zh, zl = rest
    chunk = pl.program_id(0)
    rows = x_ref.shape[0]
    stretches = rows // STRETCH
    me = info[0]
    upper = ((me >> level_bit) & 1) == 1
    base = (me * rows - half).astype(F32)

    if first:

        @pl.when(chunk == 0)
        def _():
            w = lam_ref[...] * level_scales(lam_ref.shape, 0, heads)
            lam_out[...] = w.T

        lam = lam_out
    else:
        lam = lam_ref

    @pl.when(chunk == 0)
    def _():
        def put(w):
            t = w.T
            hi, lo = split(t)
            wt[: t.shape[0]] = hi
            wt[t.shape[0] :] = lo

        @pl.when(upper)
        def _():
            put(scaled_rows(c_ref[...], [open_product(info, 0, i) for i in range(stretches)]))

        @pl.when(jnp.logical_not(upper))
        def _():
            put(scaled_rows(b_ref[...], [open_product(info, i + 1, stretches - 1) for i in range(stretches)]))

    @pl.when(upper)
    def _():
        tables = decays(rate_ref, chunk, base, -1.0, stretches)
        for i in range(stretches):
            at = slice(STRETCH * i, STRETCH * (i + 1))
            z = decayed(cot_ref, tables, i) * weight_of(lam[at, :], level, chunk, heads)
            zh[at], zl[at] = split(z)

    @pl.when(jnp.logical_not(upper))
    def _():
        tables = decays(rate_ref, chunk, base, 1.0, stretches)
        for i in range(stretches):
            at = slice(STRETCH * i, STRETCH * (i + 1))
            zh[at], zl[at] = split(decayed(x_ref, tables, i))

    n = v_ref.shape[0]
    r = dot(wt[...], zh[...])
    v_ref[...] = r[:n] + r[n:] + dot(wt[:n], zl[...])


def send_state(info, rate, x, cot, b, c, lam, level, level_bit, half, first):
    rows, columns = x.shape
    heads = rate.shape[0]
    n = b.shape[1]
    upper = lambda info: (info[0] >> level_bit) & 1
    whole = lambda a: pl.BlockSpec(a.shape, lambda j, info: (0, 0))
    out_shape = [jax.ShapeDtypeStruct((n, columns), F32)]
    out_specs = [pl.BlockSpec((n, CHUNK), lambda j, info: (0, j))]
    if first:
        out_shape.append(jax.ShapeDtypeStruct((rows, LANES), F32))
        out_specs.append(pl.BlockSpec((rows, LANES), lambda j, info: (0, 0)))
    out = pl.pallas_call(
        functools.partial(send_kernel, heads, level, level_bit, half, first),
        out_shape=out_shape,
        grid_spec=pltpu.PrefetchScalarGridSpec(
            num_scalar_prefetch=1,
            grid=(columns // CHUNK,),
            in_specs=[
                pl.BlockSpec(memory_space=pltpu.SMEM),
                pl.BlockSpec((rows, CHUNK), lambda j, info: (0, j * (1 - upper(info)))),
                pl.BlockSpec((rows, CHUNK), lambda j, info: (0, j * upper(info))),
                whole(b),
                whole(c),
                whole(lam),
            ],
            out_specs=out_specs,
            scratch_shapes=[
                pltpu.VMEM((2 * n, rows), BF16),
                pltpu.VMEM((rows, CHUNK), BF16),
                pltpu.VMEM((rows, CHUNK), BF16),
            ],
        ),
        compiler_params=pltpu.CompilerParams(vmem_limit_bytes=40 * 2**20),
        cost_estimate=pl.CostEstimate(
            flops=6 * rows * n * columns, bytes_accessed=6 * 2**20, transcendentals=0
        ),
        name=f"send_level_{level}",
    )(info, rate, x, cot, b, c, lam)
    return out if first else out[0]


def local_kernel(heads, half, info_off, info, rate_ref, x_ref, cot_ref, b_ref, c_ref, lam_ref,
                 gx_ref, gl_ref, gb_ref, gc_ref,
                 p0, p0t, p1, p1t, p2, p2t, s3, s3t, xh, xl, zh, zl, m0, m1, m2, m3, y):
    chunk = pl.program_id(0)
    last = pl.num_programs(0) - 1
    rows = x_ref.shape[0]
    n = b_ref.shape[1]
    stretches = rows // STRETCH
    total = 2 * rows
    me = info[0]
    base = (me * total - half).astype(F32) + info_off * STRETCH

    def rs(a, count=1):
        return slice(STRETCH * a, STRETCH * (a + count))

    def level_rows(level):
        span = 1 << (level - 1)
        for g in range(stretches >> level):
            yield g, (g << level), (g << level) + span, span

    @pl.when(chunk == 0)
    def _():
        def product(q, k):
            qh, ql = split(q)
            kh, kl = split(k)
            return dot_nt(jnp.concatenate([qh, ql], 1), jnp.concatenate([kh, kh], 1)) + dot_nt(qh, kl)

        for i in range(stretches):
            cq, bk = c_ref[rs(i), :], b_ref[rs(i), :]
            t = lax.broadcasted_iota(jnp.int32, (STRETCH, STRETCH), 0)
            s = lax.broadcasted_iota(jnp.int32, (STRETCH, STRETCH), 1)
            h, l = split(jnp.where(t >= s, product(cq, bk), 0.0))
            p0[i] = jnp.concatenate([h, l, h], 1)
            h, l = split(jnp.where(s >= t, product(bk, cq), 0.0))
            p0t[i] = jnp.concatenate([h, l, h], 1)
        for level, ps in ((1, (p1, p1t)), (2, (p2, p2t)), (3, (s3, s3t))):
            for g, k0, q0, span in level_rows(level):
                cq = scaled_rows(c_ref[rs(q0, span), :], [query_open(info, level, info_off + q0 + a) for a in range(span)])
                bk = scaled_rows(b_ref[rs(k0, span), :], [key_open(info, level, info_off + k0 + a) for a in range(span)])
                for ref, (u, w) in zip(ps, ((cq, bk), (bk, cq))):
                    h, l = split(product(u, w))
                    ref[g] = jnp.concatenate([h, l, h] if level == 1 else [h, l], 1)
        gl_ref[...] = jnp.zeros_like(gl_ref)
        m0[...] = jnp.zeros_like(m0)
        m1[...] = jnp.zeros_like(m1)
        m2[...] = jnp.zeros_like(m2)
        m3[...] = jnp.zeros_like(m3)

    key_tables = decays(rate_ref, chunk, base, 1.0, stretches)
    query_tables = decays(rate_ref, chunk, base, -1.0, stretches)
    for i in range(stretches):
        xh[rs(i)], xl[rs(i)] = split(decayed(x_ref, key_tables, i))

    def weighted(level, i):
        return decayed(cot_ref, query_tables, i) * weight_of(lam_ref[rs(i), :], level, chunk, heads)

    def apply3(p, k, span, h, l):
        hi, lo = h[rs(k, span)], l[rs(k, span)]
        if span == 1:
            return dot(p, jnp.concatenate([hi, hi, lo], 0))
        wide = span * STRETCH
        if span == 2:
            return dot(p, jnp.concatenate([hi, hi], 0)) + dot(p[:, :wide], lo)
        return dot(p[:, :wide], hi) + dot(p[:, wide:], hi) + dot(p[:, :wide], lo)

    def level_gradient(level, q0, span):
        prod = jnp.concatenate(
            [y[rs(q0 + a)] * decayed(cot_ref, query_tables, q0 + a) for a in range(span)], 0
        )
        h, l = split(prod)
        e = head_sums(level, chunk, heads)
        gl_ref[rs(q0, span), :] += dot(h, e) + dot(l, e)

    def mixed(q0, span, k0, kspan):
        kh, kl = xh[rs(k0, kspan)], xl[rs(k0, kspan)]
        qh, ql = zh[rs(q0, span)], zl[rs(q0, span)]
        if kspan == 2:
            r = dot_nt(qh, jnp.concatenate([kh, kl], 0))
            return r[:, :LANES] + r[:, LANES:] + dot_nt(ql, kh)
        return dot_nt(qh, kh) + dot_nt(qh, kl) + dot_nt(ql, kh)

    for i in range(stretches):
        zh[rs(i)], zl[rs(i)] = split(weighted(0, i))
    for i in range(stretches):
        y[rs(i)] = apply3(p0[i], i, 1, xh, xl)
        gx_ref[rs(i), :] = apply3(p0t[i], i, 1, zh, zl)
    level_gradient(0, 0, stretches)
    for g in range(stretches // 2):
        m0[g] += mixed(2 * g, 2, 2 * g, 2)
    for level, ps, psT in ((1, p1, p1t), (2, p2, p2t), (3, s3, s3t)):
        for g, k0, q0, span in level_rows(level):
            for a in range(span):
                zh[rs(q0 + a)], zl[rs(q0 + a)] = split(weighted(level, q0 + a))
            y[rs(q0, span)] = apply3(ps[g], k0, span, xh, xl)
            level_gradient(level, q0, span)
            gx_ref[rs(k0, span), :] += apply3(psT[g], q0, span, zh, zl)
            if level == 1:
                m1[g] += mixed(q0, 1, k0, 2)
            elif level == 2:
                m2[g] += mixed(q0, 2, k0, 2)
            else:
                m3[...] += mixed(q0, 4, k0, 4)

    @pl.when(chunk == last)
    def _():
        def times(m, w):
            mh, ml = split(m)
            wh, wl = split(w)
            r = dot(mh, jnp.concatenate([wh, wl], 1))
            return r[:, :n] + r[:, n:] + dot(ml, wh)

        wide = 2 * STRETCH
        t = lax.broadcasted_iota(jnp.int32, (wide, wide), 0)
        s = lax.broadcasted_iota(jnp.int32, (wide, wide), 1)
        for g in range(stretches // 4):
            rows4 = rs(4 * g, 4)
            blocks = []
            for d in range(2):
                at = 2 * g + d
                own = jnp.where((t >= s) & (t // STRETCH == s // STRETCH), m0[at], 0.0)
                valid = open_product(info, info_off + 2 * at + 1, info_off + 2 * at + 1)
                low = jnp.concatenate([jnp.zeros((STRETCH, wide), F32), m1[at] * valid], 0)
                blocks.append(own + jnp.where(s < STRETCH, low, 0.0))
            q = [query_open(info, 2, info_off + 4 * g + 2 + a) for a in range(2)]
            k = [key_open(info, 2, info_off + 4 * g + a) for a in range(2)]
            m_two = scaled_rows(m2[g], q)
            m_two = jnp.where(s < STRETCH, m_two * k[0], m_two * k[1])
            m = jnp.concatenate(
                [
                    jnp.concatenate([blocks[0], jnp.zeros((wide, wide), F32)], 1),
                    jnp.concatenate([m_two, blocks[1]], 1),
                ],
                0,
            )
            gc_ref[rows4, :] = times(m, b_ref[rows4, :])
            gb_ref[rows4, :] = times(m.T, c_ref[rows4, :])
        q = [query_open(info, 3, info_off + 4 + a) for a in range(4)]
        k = [key_open(info, 3, info_off + a) for a in range(4)]
        m = m3[...]
        gc_ref[rs(4, 4), :] += scaled_rows(times(m, scaled_rows(b_ref[rs(0, 4), :], k)), q)
        gb_ref[rs(0, 4), :] += scaled_rows(times(m.T, scaled_rows(c_ref[rs(4, 4), :], q)), k)


def local_levels(info, rate, x, cot, b, c, lam, half, part):
    rows, columns = x.shape[0] // 2, x.shape[1]
    heads = rate.shape[0]
    n = b.shape[1]
    stretches = rows // STRETCH
    own = lambda wide: pl.BlockSpec((rows, wide), lambda j, info: (part, 0))
    fixed = lambda wide: pl.BlockSpec((rows, wide), lambda j, info: (0, 0))
    cut = lambda at: pl.BlockSpec((rows, CHUNK), lambda j, info: (at, j))
    three, wide = 3 * STRETCH, 2 * STRETCH
    return pl.pallas_call(
        functools.partial(local_kernel, heads, half, part * stretches),
        out_shape=[
            jax.ShapeDtypeStruct((rows, columns), F32),
            jax.ShapeDtypeStruct((rows, LANES), F32),
            jax.ShapeDtypeStruct((rows, n), F32),
            jax.ShapeDtypeStruct((rows, n), F32),
        ],
        grid_spec=pltpu.PrefetchScalarGridSpec(
            num_scalar_prefetch=1,
            grid=(columns // CHUNK,),
            in_specs=[
                pl.BlockSpec(memory_space=pltpu.SMEM),
                cut(part),
                cut(part),
                own(n),
                own(n),
                own(LANES),
            ],
            out_specs=[cut(0), fixed(LANES), fixed(n), fixed(n)],
            scratch_shapes=[
                pltpu.VMEM((stretches, STRETCH, three), BF16),
                pltpu.VMEM((stretches, STRETCH, three), BF16),
                pltpu.VMEM((stretches // 2, STRETCH, three), BF16),
                pltpu.VMEM((stretches // 2, STRETCH, three), BF16),
                pltpu.VMEM((stretches // 4, wide, 2 * wide), BF16),
                pltpu.VMEM((stretches // 4, wide, 2 * wide), BF16),
                pltpu.VMEM((1, 2 * wide, 4 * wide), BF16),
                pltpu.VMEM((1, 2 * wide, 4 * wide), BF16),
                pltpu.VMEM((rows, CHUNK), BF16),
                pltpu.VMEM((rows, CHUNK), BF16),
                pltpu.VMEM((rows, CHUNK), BF16),
                pltpu.VMEM((rows, CHUNK), BF16),
                pltpu.VMEM((stretches // 2, wide, wide), F32),
                pltpu.VMEM((stretches // 2, STRETCH, wide), F32),
                pltpu.VMEM((stretches // 4, wide, wide), F32),
                pltpu.VMEM((2 * wide, 2 * wide), F32),
                pltpu.VMEM((rows, CHUNK), F32),
            ],
        ),
        compiler_params=pltpu.CompilerParams(vmem_limit_bytes=40 * 2**20),
        cost_estimate=pl.CostEstimate(
            flops=9 * 10**9, bytes_accessed=6 * 2**20, transcendentals=0
        ),
        name=f"local_levels_{part}",
    )(info, rate, x, cot, b, c, lam)


def apply_kernel(heads, half, middle, bits, level0, final, info, rate_ref, x_ref, cot_ref, b_ref, c_ref, lam_ref,
                 gxa_ref, gxb_ref, gl_in, gb_in, gc_in, *rest):
    count = len(bits)
    r_refs, (gx_ref, gl_ref, gb_ref, gc_ref, pw, xh, xl, zh, zl, gls, rt) = rest[:count], rest[count:]
    chunk = pl.program_id(0)
    last = pl.num_programs(0) - 1
    rows = x_ref.shape[0]
    n = b_ref.shape[1]
    stretches = rows // STRETCH
    me = info[0]
    base = (me * rows - half).astype(F32)
    gates = 1 + stretches

    def rs(a, count=1):
        return slice(STRETCH * a, STRETCH * (a + count))

    prefix = [open_product(info, 0, i) for i in range(stretches)]
    suffix = [open_product(info, i + 1, stretches - 1) for i in range(stretches)]
    uppers = [((me >> bit) & 1) == 1 for bit in bits]
    gate = [info[gates + bit].astype(F32) for bit in bits]

    @pl.when(chunk == 0)
    def _():
        gls[...] = gl_in[...]
        gb_ref[...] = gb_in[...]
        gc_ref[...] = gc_in[...]
        pw[0] = jnp.concatenate(split(scaled_rows(c_ref[...], prefix)), 1)
        pw[1] = jnp.concatenate(split(scaled_rows(b_ref[...], suffix)), 1)
        if middle:
            mid = stretches // 2
            level = stretches.bit_length() - 1
            pw[2] = jnp.concatenate(
                split(
                    jnp.concatenate(
                        [
                            scaled_rows(b_ref[rs(0, mid), :], [key_open(info, level, j) for j in range(mid)]),
                            scaled_rows(c_ref[rs(mid, mid), :], [query_open(info, level, mid + j) for j in range(mid)]),
                        ],
                        0,
                    )
                ),
                1,
            )
            t = jnp.concatenate(
                [
                    scaled_rows(b_ref[rs(0, mid), :], [key_open(info, level, j) for j in range(mid)]).T,
                    scaled_rows(c_ref[rs(mid, mid), :], [query_open(info, level, mid + j) for j in range(mid)]).T,
                ],
                0,
            )
            rt[0], rt[1] = split(t)

    key_tables = decays(rate_ref, chunk, base, 1.0, stretches)
    query_tables = decays(rate_ref, chunk, base, -1.0, stretches)
    mid = stretches // 2
    gx_ref[rs(0, mid), :] = gxa_ref[...]
    gx_ref[rs(mid, mid), :] = gxb_ref[...]
    for i in range(stretches):
        xh[rs(i)], xl[rs(i)] = split(decayed(x_ref, key_tables, i))

    def spread(p, r):
        hi, lo = split(r)
        return dot(p, jnp.concatenate([hi, hi], 0)) + dot(p[:, :n], lo)

    def gather(h, l, r):
        hi, lo = split(r)
        both = dot_nt(h, jnp.concatenate([hi, lo], 0))
        return both[:, :n] + both[:, n:] + dot_nt(l, hi)

    def query_side(level, first, count, p, r, factors):
        for a in range(first, first + count):
            z = decayed(cot_ref, query_tables, a) * weight_of(lam_ref[rs(a), :], level, chunk, heads)
            zh[rs(a)], zl[rs(a)] = split(z)
        at = rs(first, count)
        gc_ref[at, :] += scaled_rows(gather(zh[at], zl[at], r), factors)
        g = spread(p[at], r)
        prod = jnp.concatenate(
            [g[rs(a)] * decayed(cot_ref, query_tables, first + a) for a in range(count)], 0
        )
        h, l = split(prod)
        e = head_sums(level, chunk, heads)
        gls[at, :] += dot(h, e) + dot(l, e)

    def key_side(first, count, p, r, factors):
        at = rs(first, count)
        gb_ref[at, :] += scaled_rows(gather(xh[at], xl[at], r), factors)
        gx_ref[at, :] += spread(p[at], r)

    if middle:
        level = stretches.bit_length() - 1
        for a in range(mid, stretches):
            z = decayed(cot_ref, query_tables, a) * weight_of(lam_ref[rs(a), :], level, chunk, heads)
            zh[rs(a)], zl[rs(a)] = split(z)

        def state(h, l, w):
            wh, wl = rt[0, w * n : (w + 1) * n], rt[1, w * n : (w + 1) * n]
            r = dot(jnp.concatenate([wh, wl], 0), h)
            return r[:n] + r[n:] + dot(wh, l)

        low, high = rs(0, mid), rs(mid, mid)
        keys = state(xh[low], xl[low], 0)
        queries = state(zh[high], zl[high], 1)
        key_side(0, mid, pw.at[2], queries, [key_open(info, level, j) for j in range(mid)])
        query_side(level, mid, mid, pw.at[2], keys, [query_open(info, level, mid + j) for j in range(mid)])
    for k, bit in enumerate(bits):

        @pl.when(uppers[k])
        def _():
            query_side(level0 + bit, 0, stretches, pw.at[0], r_refs[k][...] * gate[k], prefix)

        @pl.when(jnp.logical_not(uppers[k]))
        def _():
            key_side(0, stretches, pw.at[1], r_refs[k][...] * gate[k], suffix)

    if final:
        for i in range(stretches):
            gx_ref[rs(i), :] = decayed(gx_ref, key_tables, i)

    @pl.when(chunk == last)
    def _():
        if final:
            lanes = gl_ref.shape[0]
            gl_ref[...] = gls[...].T[:lanes] * level_scales((lanes, 1), 0, heads)
        else:
            gl_ref[...] = gls[...]


def apply_states(info, rate, x, cot, b, c, lam, gx, gl, gb, gc, states, bits, half, middle, level0, lanes, final):
    rows, columns = x.shape
    heads = rate.shape[0]
    n = b.shape[1]
    cut = pl.BlockSpec((rows, CHUNK), lambda j, info: (0, j))
    whole = lambda a: pl.BlockSpec(a.shape, lambda j, info: (0, 0))
    gxa, gxb = gx
    off = 0 if gxa.shape[0] == rows // 2 else 1
    gl_shape = (lanes, rows) if final else (rows, LANES)
    return pl.pallas_call(
        functools.partial(apply_kernel, heads, half, middle, bits, level0, final),
        out_shape=[
            jax.ShapeDtypeStruct((rows, columns), F32),
            jax.ShapeDtypeStruct(gl_shape, F32),
            jax.ShapeDtypeStruct((rows, n), F32),
            jax.ShapeDtypeStruct((rows, n), F32),
        ],
        grid_spec=pltpu.PrefetchScalarGridSpec(
            num_scalar_prefetch=1,
            grid=(columns // CHUNK,),
            in_specs=[
                pl.BlockSpec(memory_space=pltpu.SMEM),
                cut,
                cut,
                whole(b),
                whole(c),
                whole(lam),
                pl.BlockSpec((rows // 2, CHUNK), lambda j, info: (0, j)),
                pl.BlockSpec((rows // 2, CHUNK), lambda j, info: (off, j)),
                whole(gl),
                whole(gb),
                whole(gc),
            ]
            + [pl.BlockSpec((n, CHUNK), lambda j, info: (0, j))] * len(bits),
            out_specs=[
                cut,
                pl.BlockSpec(gl_shape, lambda j, info: (0, 0)),
                pl.BlockSpec((rows, n), lambda j, info: (0, 0)),
                pl.BlockSpec((rows, n), lambda j, info: (0, 0)),
            ],
            scratch_shapes=[
                pltpu.VMEM((3, rows, 2 * n), BF16),
                pltpu.VMEM((rows, CHUNK), BF16),
                pltpu.VMEM((rows, CHUNK), BF16),
                pltpu.VMEM((rows, CHUNK), BF16),
                pltpu.VMEM((rows, CHUNK), BF16),
                pltpu.VMEM((rows, LANES), F32),
                pltpu.VMEM((2, 2 * n, rows // 2), BF16),
            ],
        ),
        compiler_params=pltpu.CompilerParams(vmem_limit_bytes=56 * 2**20),
        cost_estimate=pl.CostEstimate(
            flops=len(bits) * 2 * 10**9, bytes_accessed=16 * 2**20, transcendentals=0
        ),
        name="apply_" + "_".join(str(level0 + b) for b in bits),
    )(info, rate, x, cot, b, c, lam, gxa, gxb, gl, gb, gc, *states)


def local(inputs, cotangent, b_proj, c_proj, decay_rate, level_weight, starts):
    rows = inputs.shape[0]
    heads = decay_rate.shape[0]
    stretches = rows // STRETCH
    local_bits = stretches.bit_length() - 1
    seq_count = lax.axis_size("seq")
    seq_bits = seq_count.bit_length() - 1
    half = seq_count * rows // 2
    me = lax.axis_index("seq")
    lanes = level_weight.shape[0] * heads
    info = jnp.concatenate([me.astype(jnp.int32).reshape(1), starts])
    raw_lam = level_weight.reshape(lanes, rows)
    if lanes < LANES:
        raw_lam = jnp.pad(raw_lam, ((0, LANES - lanes), (0, 0)))
    args = (info, decay_rate, inputs, cotangent, b_proj, c_proj)
    flags = all_clean_flags(jnp.where(jnp.sum(starts) == 0, 1.0, 0.0), me)
    states = [None] * seq_bits
    lam = None
    for b in reversed(range(seq_bits)):
        level = local_bits + 1 + b
        if lam is None:
            v, lam = send_state(*args, raw_lam, level, b, half, True)
        else:
            v = send_state(*args, lam, level, b, half, False)
        states[b] = swap_block_sums(v, flags, me, b)
    parts = [local_levels(*args, lam, half, part) for part in range(2)]
    gates = jnp.stack([gate_of(flags, me, b) for b in range(seq_bits)]).astype(jnp.int32)
    info = jnp.concatenate([info, gates])
    args = (info,) + args[1:]
    gx = [p[0] for p in parts]
    gl, gb, gc = (jnp.concatenate([p[k] for p in parts], 0) for k in (1, 2, 3))
    early = tuple(range(seq_bits - 1))
    gx_all, gl, gb, gc = apply_states(
        *args, lam, gx, gl, gb, gc, [states[b] for b in early], early, half, True, local_bits + 1, lanes, False
    )
    late = (seq_bits - 1,)
    grad_x, gl, gb, gc = apply_states(
        *args, lam, (gx_all, gx_all), gl, gb, gc, [states[b] for b in late], late, half, False, local_bits + 1, lanes, True
    )
    return (grad_x, scatter_heads(gb), scatter_heads(gc), gl.reshape(level_weight.shape))


def solution(mesh):
    return jax.shard_map(
        local,
        mesh=mesh,
        in_specs=(
            P("seq", "head"),
            P("seq", "head"),
            P("seq", None),
            P("seq", None),
            P("head"),
            P(None, "head", "seq"),
            P("seq"),
        ),
        out_specs=(
            P("seq", "head"),
            P(("seq", "head"), None),
            P(("seq", "head"), None),
            P(None, "head", "seq"),
        ),
        check_vma=False,
    )
```

```python
import functools

import jax
import jax.numpy as jnp
from jax import lax
from jax.experimental import pallas as pl
from jax.experimental.pallas import tpu as pltpu
from jax.sharding import PartitionSpec as P

KERNELS = True
STRETCH = 64
WIDTH = 64
CHUNK = 256
LANES = 128
F32 = jnp.float32
BF16 = jnp.bfloat16


def partner(x, apart):
    return lax.ppermute(x, "seq", [(i, i ^ apart) for i in range(lax.axis_size("seq"))])


def gate_of(flags, device, level_bit):
    ids = jnp.arange(flags.shape[0])
    first = (device >> level_bit) << level_bit
    last = first + (1 << level_bit) - 1
    upper = ((device >> level_bit) & 1) == 1
    between = jnp.where(upper, (ids >= first) & (ids < device), (ids > device) & (ids <= last))
    return jnp.min(jnp.where(between, flags, 1.0))


def scatter_heads(x):
    count = lax.axis_size("head")
    me = lax.axis_index("head")
    bits = count.bit_length() - 1
    x = x.reshape((2,) * bits + (x.shape[0] // count,) + x.shape[1:])
    for bit in range(bits):
        axis = bits - 1 - bit
        high = (me >> bit) & 1
        away = lax.dynamic_index_in_dim(x, 1 - high, axis, keepdims=False)
        kept = lax.dynamic_index_in_dim(x, high, axis, keepdims=False)
        came = lax.ppermute(away, "head", [(i, i ^ (1 << bit)) for i in range(count)])
        x = kept + came
    return x


def split(a):
    hi = a.astype(BF16)
    return hi, (a - hi.astype(F32)).astype(BF16)


def dot(a, b):
    return lax.dot_general(a, b, (((1,), (0,)), ((), ())), preferred_element_type=F32)


def dot_nt(a, b):
    return lax.dot_general(a, b, (((1,), (1,)), ((), ())), preferred_element_type=F32)


def open_product(info, first, last):
    r = jnp.float32(1.0)
    for k in range(first, last + 1):
        r = r * (1 - info[1 + k]).astype(F32)
    return r


def query_open(info, level, i):
    mid = ((i >> level) << level) + (1 << (level - 1))
    return open_product(info, mid, i)


def key_open(info, level, j):
    mid = ((j >> level) << level) + (1 << (level - 1))
    return open_product(info, j + 1, mid - 1)


def scaled_rows(a, factors):
    return jnp.concatenate(
        [a[STRETCH * k : STRETCH * (k + 1)] * f for k, f in enumerate(factors)], 0
    )


def decays(rate_ref, chunk, base, sign, stretches):
    per = CHUNK // WIDTH
    lane_head = lax.broadcasted_iota(jnp.int32, (1, CHUNK), 1) // WIDTH
    row = jnp.zeros((1, CHUNK), F32)
    for k in range(per):
        row = jnp.where(lane_head == k, rate_ref[chunk * per + k], row)
    within = lax.broadcasted_iota(jnp.int32, (STRETCH, CHUNK), 0).astype(F32)
    across = lax.broadcasted_iota(jnp.int32, (stretches, CHUNK), 0).astype(F32) * STRETCH + base
    return jnp.exp(sign * within * row), jnp.exp(sign * across * row)


def decayed(a, tables, i, first=0):
    inner, outer = tables
    return a[STRETCH * i : STRETCH * (i + 1), :] * (inner * outer[first + i : first + i + 1, :])


def weight_of(lam, level, chunk, heads):
    rows = lam.shape[0]
    per = LANES // WIDTH
    lane = lax.broadcasted_iota(jnp.int32, (rows, LANES), 1) // WIDTH
    out = []
    for piece in range(CHUNK // LANES):
        at = lane + (level * heads + piece * per + chunk * (CHUNK // WIDTH))
        out.append(jnp.take_along_axis(lam, at, axis=1))
    return jnp.concatenate(out, 1)


def head_columns(columns):
    d = lax.broadcasted_iota(jnp.int32, (columns, LANES), 0) // WIDTH
    lane = lax.broadcasted_iota(jnp.int32, (columns, LANES), 1)
    return jnp.where(lane == d, 1.0, 0.0).astype(BF16)


def head_sums(ph, pl_, e, level, heads):
    r = dot(ph, e) + dot(pl_, e)
    return pltpu.roll(r, level * heads, 1) if level else r


def rs(a, count=1):
    return slice(STRETCH * a, STRETCH * (a + count))


def each_chunk(columns, body):
    for j in range(columns // CHUNK):
        body(j, slice(j * CHUNK, (j + 1) * CHUNK))


def weighted(cw_ref, lam_ref, i, cols, level, j, heads):
    return cw_ref[rs(i), cols] * weight_of(lam_ref[rs(i), :], level, j, heads)


VMEM = pl.BlockSpec(memory_space=pltpu.VMEM)
SMEM = pl.BlockSpec(memory_space=pltpu.SMEM)
ANY = pl.BlockSpec(memory_space=pl.ANY)


def call(kernel, name, inputs, specs, outs, out_specs, scratch, mib, flops, aliases=None):
    return pl.pallas_call(
        kernel,
        out_shape=[jax.ShapeDtypeStruct(*o) for o in outs],
        in_specs=specs,
        out_specs=out_specs,
        scratch_shapes=scratch,
        input_output_aliases=aliases or {},
        compiler_params=pltpu.CompilerParams(vmem_limit_bytes=mib * 2**20),
        cost_estimate=pl.CostEstimate(flops=flops, bytes_accessed=2**20, transcendentals=0),
        name=name,
    )(*inputs)


def level_scales(shape, axis, heads):
    shift = heads.bit_length() - 1
    level = (lax.broadcasted_iota(jnp.int32, shape, axis) >> shift).astype(F32)
    return jnp.exp2(-0.5 * level - 0.5 * (STRETCH.bit_length() - 1))


def state_of(info, upper, level, heads, b_ref, c_ref, lam_ref, cw_ref, xh, xl, v_ref, wt, zh, zl):
    rows, columns = xh.shape
    n = b_ref.shape[1]
    stretches = rows // STRETCH

    def put(w):
        t = w.T
        wt[:n], wt[n:] = split(t)

    def product(h, l):
        def one(j, cols):
            r = dot(wt[...], h[:, cols])
            v_ref[:, cols] = r[:n] + r[n:] + dot(wt[:n], l[:, cols])

        each_chunk(columns, one)

    @pl.when(upper)
    def _():
        put(scaled_rows(c_ref[...], [open_product(info, 0, i) for i in range(stretches)]))

        def one(j, cols):
            for i in range(stretches):
                zh[rs(i), cols], zl[rs(i), cols] = split(weighted(cw_ref, lam_ref, i, cols, level, j, heads))

        each_chunk(columns, one)
        product(zh, zl)

    @pl.when(jnp.logical_not(upper))
    def _():
        put(scaled_rows(b_ref[...], [open_product(info, i + 1, stretches - 1) for i in range(stretches)]))
        product(xh, xl)


def first_kernel(heads, level, bit, half, info, rate_ref, x_hbm, cot_hbm, b_ref, c_ref, raw_ref,
                 xh, xl, cw, lam_out, v_ref, xf, wt, zh, zl, sems):
    rows, columns = xh.shape
    stretches = rows // STRETCH
    pieces = sems.shape[1]
    size = rows // pieces
    me = info[0]
    base = (me * rows - half).astype(F32)
    copies = []
    for k in range(pieces):
        at = pl.ds(k * size, size)
        copies.append(
            (
                pltpu.make_async_copy(x_hbm.at[at], xf.at[at], sems.at[0, k]),
                pltpu.make_async_copy(cot_hbm.at[at], cw.at[at], sems.at[1, k]),
            )
        )
        for copy in copies[-1]:
            copy.start()
    lam_out[...] = (raw_ref[...] * level_scales((raw_ref.shape[0], 1), 0, heads)).T
    per = size // STRETCH
    for k in range(pieces):
        for copy in copies[k]:
            copy.wait()

        def one(j, cols):
            keys = decays(rate_ref, j, base, 1.0, stretches)
            queries = decays(rate_ref, j, base, -1.0, stretches)
            for i in range(k * per, (k + 1) * per):
                xh[rs(i), cols], xl[rs(i), cols] = split(xf[rs(i), cols] * (keys[0] * keys[1][i : i + 1, :]))
                cw[rs(i), cols] = cw[rs(i), cols] * (queries[0] * queries[1][i : i + 1, :])

        each_chunk(columns, one)
    upper = ((me >> bit) & 1) == 1
    state_of(info, upper, level, heads, b_ref, c_ref, lam_out, cw, xh, xl, v_ref, wt, zh, zl)


def first_state(info, rate, x, cot, b, c, raw, level, bit, half):
    rows, columns = x.shape
    n = b.shape[1]
    wide = ((rows, columns), BF16)
    return call(
        functools.partial(first_kernel, rate.shape[0], level, bit, half),
        f"send_level_{level}",
        (info, rate, x, cot, b, c, raw),
        [SMEM, SMEM, ANY, ANY, VMEM, VMEM, VMEM],
        [wide, wide, ((rows, columns), F32), ((rows, LANES), F32), ((n, columns), F32)],
        [VMEM] * 5,
        [
            pltpu.VMEM((rows, columns), F32),
            pltpu.VMEM((2 * n, rows), BF16),
            pltpu.VMEM((rows, columns), BF16),
            pltpu.VMEM((rows, columns), BF16),
            pltpu.SemaphoreType.DMA((2, 4)),
        ],
        16,
        10**9,
    )


def send_kernel(heads, level, bit, info, b_ref, c_ref, lam_ref, cw, xh, xl, v_ref, wt, zh, zl):
    upper = ((info[0] >> bit) & 1) == 1
    state_of(info, upper, level, heads, b_ref, c_ref, lam_ref, cw, xh, xl, v_ref, wt, zh, zl)


def send_state(info, heads, held, b, c, level, bit):
    xh, xl, cw, lam = held
    rows, columns = xh.shape
    n = b.shape[1]
    return call(
        functools.partial(send_kernel, heads, level, bit),
        f"send_level_{level}",
        (info, b, c, lam, cw, xh, xl),
        [SMEM] + [VMEM] * 6,
        [((n, columns), F32)],
        [VMEM],
        [
            pltpu.VMEM((2 * n, rows), BF16),
            pltpu.VMEM((rows, columns), BF16),
            pltpu.VMEM((rows, columns), BF16),
        ],
        12,
        10**9,
    )[0]


def split_rows(a):
    return jnp.concatenate(split(a), 1)


def spread(p, rh, rl, cols):
    n = rh.shape[0]
    h, l = rh[:, cols], rl[:, cols]
    return dot(p, jnp.concatenate([h, h], 0)) + dot(p[:, :n], l)


def gather(h, l, rh, rl):
    n = rh.shape[0]
    both = dot_nt(h, jnp.concatenate([rh[...], rl[...]], 0))
    return both[:, :n] + both[:, n:] + dot_nt(l, rh[...])


def local_kernel(heads, off, info, b_ref, c_ref, lam_ref, cw_ref, xh_ref, xl_ref,
                 gx_ref, gl_ref, gb_ref, gc_ref,
                 p0, p0t, p1, p1t, p2, p2t, s3, s3t, ph, pq, zh, zl, rh, rl):
    rows, columns = gx_ref.shape
    n = b_ref.shape[1]
    stretches = rows // STRETCH

    def own(a, count=1):
        return rs(off + a, count)

    def level_rows(level):
        span = 1 << (level - 1)
        return [(g, g << level, (g << level) + span, span) for g in range(stretches >> level)]

    def product(q, k):
        qh, ql = split(q)
        kh, kl = split(k)
        return dot_nt(jnp.concatenate([qh, ql], 1), jnp.concatenate([kh, kh], 1)) + dot_nt(qh, kl)

    for i in range(stretches):
        cq, bk = c_ref[own(i), :], b_ref[own(i), :]
        t = lax.broadcasted_iota(jnp.int32, (STRETCH, STRETCH), 0)
        s = lax.broadcasted_iota(jnp.int32, (STRETCH, STRETCH), 1)
        h, l = split(jnp.where(t >= s, product(cq, bk), 0.0))
        p0[i] = jnp.concatenate([h, l, h], 1)
        h, l = split(jnp.where(s >= t, product(bk, cq), 0.0))
        p0t[i] = jnp.concatenate([h, l, h], 1)
    scores = {1: (p1, p1t), 2: (p2, p2t), 3: (s3, s3t)}
    for level, ps in scores.items():
        for g, k0, q0, span in level_rows(level):
            cq = scaled_rows(c_ref[own(q0, span), :], [query_open(info, level, off + q0 + a) for a in range(span)])
            bk = scaled_rows(b_ref[own(k0, span), :], [key_open(info, level, off + k0 + a) for a in range(span)])
            for ref, (u, w) in zip(ps, ((cq, bk), (bk, cq))):
                h, l = split(product(u, w))
                ref[g] = jnp.concatenate([h, l, h], 1)

    def apply3(p, h, l):
        return dot(p, jnp.concatenate([h, h, l], 0))

    ones = head_columns(columns)
    mixed = {}
    for level in range(4):
        blocks = [(i, i, i, 1) for i in range(stretches)] if level == 0 else level_rows(level)
        ps, pst = (p0, p0t) if level == 0 else scores[level]

        def one(j, cols):
            at = 0
            for g, k0, q0, span in blocks:
                put = slice(at, at + span * STRETCH)
                for a in range(span):
                    z = weighted(cw_ref, lam_ref, off + q0 + a, cols, level, j, heads)
                    here = slice(at + a * STRETCH, at + (a + 1) * STRETCH)
                    zh[here, cols], zl[here, cols] = split(z)
                y = apply3(ps[g], xh_ref[own(k0, span), cols], xl_ref[own(k0, span), cols])
                ph[put, cols], pq[put, cols] = split(y * cw_ref[own(q0, span), cols])
                gx = apply3(pst[g], zh[put, cols], zl[put, cols])
                if level == 0:
                    gx_ref[rs(k0, span), cols] = gx
                else:
                    gx_ref[rs(k0, span), cols] += gx
                at += span * STRETCH

        each_chunk(columns, one)
        at = 0
        used = len(blocks) * blocks[0][3] * STRETCH
        sums = head_sums(ph[:used], pq[:used], ones, level, heads)
        for g, k0, q0, span in blocks:
            put = slice(at, at + span * STRETCH)
            if level == 0:
                gl_ref[rs(q0, span), :] = sums[put]
            else:
                gl_ref[rs(q0, span), :] += sums[put]
            at += span * STRETCH
        pairs = (
            [(2 * g, 2, 2 * g, 2) for g in range(stretches // 2)]
            if level == 0
            else [(g * span, span, k0, max(span, 2)) for g, k0, q0, span in blocks]
        )
        for key, (z0, zspan, k0, kspan) in enumerate(pairs):
            qh, ql = zh[rs(z0, zspan)], zl[rs(z0, zspan)]
            kh, kl = xh_ref[own(k0, kspan)], xl_ref[own(k0, kspan)]
            if kspan == 2:
                r = dot_nt(qh, jnp.concatenate([kh, kl], 0))
                mixed[level, key] = r[:, :LANES] + r[:, LANES:] + dot_nt(ql, kh)
            else:
                mixed[level, key] = dot_nt(qh, kh) + dot_nt(qh, kl) + dot_nt(ql, kh)

    level = stretches.bit_length()
    keys = [key_open(info, level, j) for j in range(stretches)]
    queries = [query_open(info, level, stretches + j) for j in range(stretches)]
    whole = slice(0, rows)

    def state(h, l, w):
        wh, wl = split(w.T)
        wt = jnp.concatenate([wh, wl], 0)

        def one(j, cols):
            r = dot(wt, h[:, cols])
            rh[:, cols], rl[:, cols] = split(r[:n] + r[n:] + dot(wh, l[:, cols]))

        each_chunk(columns, one)

    def query_z(first):
        def one(j, cols):
            for a in range(stretches):
                zh[rs(a), cols], zl[rs(a), cols] = split(weighted(cw_ref, lam_ref, first + a, cols, level, j, heads))

        each_chunk(columns, one)

    if off == 0:
        query_z(stretches)
        state(zh, zl, scaled_rows(c_ref[rs(stretches, stretches), :], queries))
        middle_rows = scaled_rows(gather(xh_ref[whole], xl_ref[whole], rh, rl), keys)
        pw = split_rows(scaled_rows(b_ref[whole, :], keys))

        def one(j, cols):
            for a in range(0, stretches, 4):
                gx_ref[rs(a, 4), cols] += spread(pw[rs(a, 4)], rh, rl, cols)

        each_chunk(columns, one)
    else:
        state(xh_ref.at[whole], xl_ref.at[whole], scaled_rows(b_ref[whole, :], keys))
        query_z(off)
        middle_rows = scaled_rows(gather(zh[...], zl[...], rh, rl), queries)
        pw = split_rows(scaled_rows(c_ref[own(0, stretches), :], queries))

        def one(j, cols):
            for a in range(0, stretches, 4):
                g = spread(pw[rs(a, 4)], rh, rl, cols)
                ph[rs(a, 4), cols], pq[rs(a, 4), cols] = split(g * cw_ref[own(a, 4), cols])

        each_chunk(columns, one)
        gl_ref[...] += head_sums(ph[...], pq[...], ones, level, heads)

    def times(m, w):
        mh, ml = split(m)
        wh, wl = split(w)
        r = dot(mh, jnp.concatenate([wh, wl], 1))
        return r[:, :n] + r[:, n:] + dot(ml, wh)

    wide = 2 * STRETCH
    t = lax.broadcasted_iota(jnp.int32, (wide, wide), 0)
    s = lax.broadcasted_iota(jnp.int32, (wide, wide), 1)
    for g in range(stretches // 4):
        rows4 = rs(4 * g, 4)
        blocks = []
        for d in range(2):
            at = 2 * g + d
            own_pair = jnp.where((t >= s) & (t // STRETCH == s // STRETCH), mixed[0, at], 0.0)
            valid = open_product(info, off + 2 * at + 1, off + 2 * at + 1)
            low = jnp.concatenate([jnp.zeros((STRETCH, wide), F32), mixed[1, at] * valid], 0)
            blocks.append(own_pair + jnp.where(s < STRETCH, low, 0.0))
        q = [query_open(info, 2, off + 4 * g + 2 + a) for a in range(2)]
        k = [key_open(info, 2, off + 4 * g + a) for a in range(2)]
        m_two = scaled_rows(mixed[2, g], q)
        m_two = jnp.where(s < STRETCH, m_two * k[0], m_two * k[1])
        m = jnp.concatenate(
            [
                jnp.concatenate([blocks[0], jnp.zeros((wide, wide), F32)], 1),
                jnp.concatenate([m_two, blocks[1]], 1),
            ],
            0,
        )
        gc_ref[rows4, :] = times(m, b_ref[own(4 * g, 4), :])
        gb_ref[rows4, :] = times(m.T, c_ref[own(4 * g, 4), :])
    q = [query_open(info, 3, off + 4 + a) for a in range(4)]
    k = [key_open(info, 3, off + a) for a in range(4)]
    m = mixed[3, 0]
    gc_ref[rs(4, 4), :] += scaled_rows(times(m, scaled_rows(b_ref[own(0, 4), :], k)), q)
    gb_ref[rs(0, 4), :] += scaled_rows(times(m.T, scaled_rows(c_ref[own(4, 4), :], q)), k)
    if off == 0:
        gb_ref[...] += middle_rows
    else:
        gc_ref[...] += middle_rows


def local_levels(info, heads, held, b, c, part):
    xh, xl, cw, lam = held
    rows, columns = xh.shape[0] // 2, xh.shape[1]
    n = b.shape[1]
    stretches = rows // STRETCH
    three, wide = 3 * STRETCH, 2 * STRETCH
    return call(
        functools.partial(local_kernel, heads, part * stretches),
        f"local_levels_{part}",
        (info, b, c, lam, cw, xh, xl),
        [SMEM] + [VMEM] * 6,
        [((rows, columns), F32), ((rows, LANES), F32), ((rows, n), F32), ((rows, n), F32)],
        [VMEM] * 4,
        [
            pltpu.VMEM((stretches, STRETCH, three), BF16),
            pltpu.VMEM((stretches, STRETCH, three), BF16),
            pltpu.VMEM((stretches // 2, STRETCH, three), BF16),
            pltpu.VMEM((stretches // 2, STRETCH, three), BF16),
            pltpu.VMEM((stretches // 4, wide, 3 * wide), BF16),
            pltpu.VMEM((stretches // 4, wide, 3 * wide), BF16),
            pltpu.VMEM((1, 2 * wide, 6 * wide), BF16),
            pltpu.VMEM((1, 2 * wide, 6 * wide), BF16),
            pltpu.VMEM((rows, columns), BF16),
            pltpu.VMEM((rows, columns), BF16),
            pltpu.VMEM((rows, columns), BF16),
            pltpu.VMEM((rows, columns), BF16),
            pltpu.VMEM((n, columns), BF16),
            pltpu.VMEM((n, columns), BF16),
        ],
        16,
        9 * 10**9,
    )


def masks(info, stretches):
    prefix = [open_product(info, 0, i) for i in range(stretches)]
    suffix = [open_product(info, i + 1, stretches - 1) for i in range(stretches)]
    return prefix, suffix


def level_sums(level, heads, p, cw, rh, rl, ph, pq, ones):
    rows, columns = cw.shape

    def one(j, cols):
        for a in range(0, rows // STRETCH, 4):
            g = spread(p[rs(a, 4)], rh, rl, cols)
            ph[rs(a, 4), cols], pq[rs(a, 4), cols] = split(g * cw[rs(a, 4), cols])

    each_chunk(columns, one)
    return head_sums(ph[...], pq[...], ones, level, heads)


def query_z(heads, level, lam_ref, cw, zh, zl):
    rows, columns = cw.shape

    def one(j, cols):
        for i in range(rows // STRETCH):
            zh[rs(i), cols], zl[rs(i), cols] = split(weighted(cw, lam_ref, i, cols, level, j, heads))

    each_chunk(columns, one)


def early_kernel(heads, level0, bits, top, info, gates, b_ref, c_ref, lam_ref, cw, xh, xl,
                 gla, glb, gba, gbb, gca, gcb, *rest):
    count = len(bits)
    states = rest[:count]
    low_ref, gl_ref, sel_ref, other_ref, pc, ph, pq, rh, rl, gbs, gcs = rest[count:]
    rows, columns = xh.shape
    stretches = rows // STRETCH
    mid = stretches // 2
    me = info[0]
    prefix, suffix = masks(info, stretches)
    uppers = [((me >> bit) & 1) == 1 for bit in bits]
    ones = head_columns(columns)
    for dst, (one, two) in ((gl_ref, (gla, glb)), (gbs, (gba, gbb)), (gcs, (gca, gcb))):
        dst[rs(0, mid), :], dst[rs(mid, mid), :] = one[...], two[...]
    pc[...] = split_rows(scaled_rows(c_ref[...], prefix))
    held = jnp.zeros(low_ref.shape, F32)
    for k, bit in enumerate(bits):
        held = held + states[k][...] * jnp.where(uppers[k], 0.0, gates[bit])
    low_ref[...] = held
    for k, bit in enumerate(bits):

        @pl.when(uppers[k])
        def _():
            rh[...], rl[...] = split(states[k][...] * gates[bit])
            query_z(heads, level0 + bit, lam_ref, cw, ph, pq)
            gcs[...] += scaled_rows(gather(ph[...], pq[...], rh, rl), prefix)
            gl_ref[...] += level_sums(level0 + bit, heads, pc, cw, rh, rl, ph, pq, ones)

    below = (1 << top) - 1

    @pl.when((me & below) != below)
    def _():
        rh[...], rl[...] = split(low_ref[...])
        gbs[...] += scaled_rows(gather(xh[...], xl[...], rh, rl), suffix)

    last = ((me >> top) & 1) == 1

    @pl.when(last)
    def _():
        sel_ref[...], other_ref[...] = gcs[...], gbs[...]

    @pl.when(jnp.logical_not(last))
    def _():
        sel_ref[...], other_ref[...] = gbs[...], gcs[...]


def early_states(info, gates, heads, held, b, c, sums, states, bits, top, level0):
    xh, xl, cw, lam = held
    rows, columns = xh.shape
    n = b.shape[1]
    inputs = (info, gates, b, c, lam, cw, xh, xl, *sums, *states)
    wide = pltpu.VMEM((rows, columns), BF16)
    state = pltpu.VMEM((n, columns), BF16)
    own = pltpu.VMEM((rows, n), F32)
    return call(
        functools.partial(early_kernel, heads, level0, bits, top),
        "apply_" + "_".join(str(level0 + b) for b in bits),
        inputs,
        [SMEM, SMEM] + [VMEM] * (len(inputs) - 2),
        [((n, columns), F32), ((rows, LANES), F32), ((rows, n), F32), ((rows, n), F32)],
        [VMEM] * 4,
        [pltpu.VMEM((rows, 2 * n), BF16), wide, wide, state, state, own, own],
        16,
        len(bits) * 2 * 10**9,
    )


def last_rows_kernel(heads, top, level, info, gates, lam_ref, cw, xh, xl, r_ref, sel_ref, out_ref, rh, rl, zh, zl):
    prefix, suffix = masks(info, xh.shape[0] // STRETCH)
    upper = ((info[0] >> top) & 1) == 1
    rh[...], rl[...] = split(r_ref[...] * gates[top])

    @pl.when(upper)
    def _():
        query_z(heads, level, lam_ref, cw, zh, zl)
        out_ref[...] = sel_ref[...] + scaled_rows(gather(zh[...], zl[...], rh, rl), prefix)

    @pl.when(jnp.logical_not(upper))
    def _():
        out_ref[...] = sel_ref[...] + scaled_rows(gather(xh[...], xl[...], rh, rl), suffix)


def last_rows(info, gates, heads, held, state, sel, top, level):
    xh, xl, cw, lam = held
    n = state.shape[0]
    rows, columns = xh.shape
    inputs = (info, gates, lam, cw, xh, xl, state, sel)
    return call(
        functools.partial(last_rows_kernel, heads, top, level),
        f"rows_{level}",
        inputs,
        [SMEM, SMEM] + [VMEM] * 6,
        [(sel.shape, F32)],
        [VMEM],
        [pltpu.VMEM((n, columns), BF16)] * 2 + [pltpu.VMEM((rows, columns), BF16)] * 2,
        12,
        10**9,
    )[0]


def last_kernel(heads, half, top, level, info, gates, rate_ref, b_ref, c_ref, cw, gxa, gxb, r_ref, low_ref, gl_in,
                gx_hbm, gl_ref, pw, ph, pq, rh, rl, of, gls, sems):
    rows, columns = cw.shape
    stretches = rows // STRETCH
    mid = stretches // 2
    me = info[0]
    base = (me * rows - half).astype(F32)
    prefix, suffix = masks(info, stretches)
    upper = ((me >> top) & 1) == 1
    gls[...] = gl_in[...]

    @pl.when(upper)
    def _():
        rh[...], rl[...] = split(r_ref[...] * gates[top])
        pw[...] = split_rows(scaled_rows(c_ref[...], prefix))
        gls[...] += level_sums(level, heads, pw, cw, rh, rl, ph, pq, head_columns(columns))

    pieces = sems.shape[0]
    per = stretches // pieces

    def copy(k):
        at = pl.ds(k * per * STRETCH, per * STRETCH)
        return pltpu.make_async_copy(of.at[at], gx_hbm.at[at], sems.at[k])

    def finish(any_low):
        if any_low:
            rh[...], rl[...] = split(low_ref[...] + r_ref[...] * jnp.where(upper, 0.0, gates[top]))
            pw[...] = split_rows(scaled_rows(b_ref[...], suffix))
        for k in range(pieces):

            def one(j, cols):
                inner, outer = decays(rate_ref, j, base, 1.0, stretches)
                extra = spread(pw[rs(k * per, per)], rh, rl, cols) if any_low else None
                for i in range(k * per, (k + 1) * per):
                    g = gxa[rs(i), cols] if i < mid else gxb[rs(i - mid), cols]
                    if any_low:
                        g = g + extra[rs(i - k * per)]
                    of[rs(i), cols] = g * (inner * outer[i : i + 1, :])

            each_chunk(columns, one)
            copy(k).start()

    below = (2 << top) - 1

    @pl.when((me & below) == below)
    def _():
        finish(False)

    @pl.when((me & below) != below)
    def _():
        finish(True)

    lanes = gl_ref.shape[0]
    gl_ref[...] = gls[...].T[:lanes] * level_scales((lanes, 1), 0, heads)
    for k in range(pieces):
        copy(k).wait()


def last_state(info, gates, rate, held, b, c, gx, state, low, gl, half, top, level, lanes):
    cw = held[2]
    rows, columns = cw.shape
    n = b.shape[1]
    wide = pltpu.VMEM((rows, columns), BF16)
    held_state = pltpu.VMEM((n, columns), BF16)
    return call(
        functools.partial(last_kernel, rate.shape[0], half, top, level),
        f"apply_{level}",
        (info, gates, rate, b, c, cw, *gx, state, low, gl),
        [SMEM] * 3 + [VMEM] * 8,
        [((rows, columns), F32), ((lanes, rows), F32)],
        [ANY, VMEM],
        [
            pltpu.VMEM((rows, 2 * n), BF16),
            wide,
            wide,
            held_state,
            held_state,
            pltpu.VMEM((rows, columns), F32),
            pltpu.VMEM((rows, LANES), F32),
            pltpu.SemaphoreType.DMA((4,)),
        ],
        20,
        3 * 10**9,
    )


def after(x, *others):
    return lax.optimization_barrier((x, *others))[0]


class Swap:
    def __init__(self, v, me, gates, level_bit, partner_gate):
        self.v, self.me, self.bit = v, me, level_bit
        self.own, self.other = gates[level_bit], partner_gate
        self.down = list(reversed(range(level_bit)))
        self.phase = 0
        self.begin()

    @property
    def steps(self):
        return 2 * self.bit + 1

    def high(self, bit):
        return (self.me >> bit) & 1

    def begin(self):
        k = self.phase
        if k < self.bit:
            bit = self.down[k]
            half = self.v.shape[0] // 2
            away = lax.dynamic_slice_in_dim(self.v, (1 - self.high(bit)) * half, half)
            self.kept = lax.dynamic_slice_in_dim(self.v, self.high(bit) * half, half)
            self.came = partner(away, 1 << bit)
        elif k == self.bit:
            self.came = partner(self.v, 1 << self.bit)
        elif k < self.steps:
            self.came = partner(self.v, 1 << (k - self.bit - 1))

    def step(self):
        k = self.phase
        if k < self.bit:
            if k == 0:
                self.v = self.own * self.kept + self.other * self.came
            else:
                self.v = self.kept + self.came
        elif k == self.bit:
            self.v = self.came
        else:
            high = self.high(k - self.bit - 1) == 1
            self.v = jnp.where(
                high, jnp.concatenate([self.came, self.v]), jnp.concatenate([self.v, self.came])
            )
        self.phase += 1
        self.begin()
        return self.v

    def finish(self):
        while self.phase < self.steps:
            self.step()
        return self.v


def local(inputs, cotangent, b_proj, c_proj, decay_rate, level_weight, starts):
    rows = inputs.shape[0]
    heads = decay_rate.shape[0]
    stretches = rows // STRETCH
    local_bits = stretches.bit_length() - 1
    seq_count = lax.axis_size("seq")
    seq_bits = seq_count.bit_length() - 1
    half = seq_count * rows // 2
    me = lax.axis_index("seq")
    lanes = level_weight.shape[0] * heads
    level0 = local_bits + 1
    top = seq_bits - 1
    info = jnp.concatenate([me.astype(jnp.int32).reshape(1), starts])
    raw_lam = level_weight.reshape(lanes, rows)
    if lanes < LANES:
        raw_lam = jnp.pad(raw_lam, ((0, LANES - lanes), (0, 0)))
    clean = jnp.where(jnp.max(starts) == 0, 1.0, 0.0)
    flags = jnp.where(jnp.arange(seq_count) == me, clean, 0.0)

    *held, v = first_state(info, decay_rate, inputs, cotangent, b_proj, c_proj, raw_lam, level0 + top, top, half)
    vs = {top: v}
    for k, b in enumerate(reversed(range(top))):
        flags = flags + partner(flags, 1 << k)
        tied = after(info, vs[b + 1], flags)
        vs[b] = send_state(tied, heads, held, b_proj, c_proj, level0 + b, b)
    flags = flags + partner(flags, 1 << top)
    gates = jnp.stack(
        [gate_of(flags, me, b) for b in range(seq_bits)] + [gate_of(flags, me ^ (1 << (b - 1)), b) for b in range(1, seq_bits)]
    )
    swaps = {b: Swap(vs[b], me, gates, b, gates[seq_bits + b - 1] if b else None) for b in reversed(range(seq_bits))}
    waits = []
    for b in reversed(range(1, seq_bits)):
        waits.append(swaps[b].step())
    tied = after(info, waits[0])
    part0 = local_levels(tied, heads, held, b_proj, c_proj, 0)
    for b in reversed(range(1, seq_bits)):
        swaps[b].v = after(swaps[b].v, part0[3])
    swaps[top].step()
    tied = after(info, part0[3], swaps[top].v)
    part1 = local_levels(tied, heads, held, b_proj, c_proj, 1)
    states = {b: swaps[b].finish() for b in range(seq_bits)}
    sums = [p[k] for k in range(1, 4) for p in (part0, part1)]
    early = tuple(range(top))
    low, gl, sel, other = early_states(
        info, gates, heads, held, b_proj, c_proj, sums, [states[b] for b in early], early, top, level0,
    )
    state = states[top]
    sel = last_rows(info, gates, heads, held, state, sel, top, level0 + top)
    grad_x, gl = last_state(
        info, gates, decay_rate, held, b_proj, c_proj, (part0[0], part1[0]), state, low, gl, half, top, level0 + top, lanes
    )
    sel, other = scatter_heads(sel), scatter_heads(other)
    upper = ((me >> top) & 1) == 1
    return (grad_x, jnp.where(upper, other, sel), jnp.where(upper, sel, other), gl.reshape(level_weight.shape))


def solution(mesh):
    return jax.shard_map(
        local,
        mesh=mesh,
        in_specs=(
            P("seq", "head"),
            P("seq", "head"),
            P("seq", None),
            P("seq", None),
            P("head"),
            P(None, "head", "seq"),
            P("seq"),
        ),
        out_specs=(
            P("seq", "head"),
            P(("seq", "head"), None),
            P(("seq", "head"), None),
            P(None, "head", "seq"),
        ),
        check_vma=False,
    )
```

```python
import functools

import jax
import jax.numpy as jnp
from jax import lax
from jax.experimental import pallas as pl
from jax.experimental.pallas import tpu as pltpu
from jax.sharding import PartitionSpec as P

KERNELS = True
STRETCH = 64
WIDTH = 64
CHUNK = 256
LANES = 128
F32 = jnp.float32
BF16 = jnp.bfloat16


def partner(x, apart):
    return lax.ppermute(x, "seq", [(i, i ^ apart) for i in range(lax.axis_size("seq"))])


def split(a):
    hi = a.astype(BF16)
    return hi, (a - hi.astype(F32)).astype(BF16)


def dot(a, b):
    return lax.dot_general(a, b, (((1,), (0,)), ((), ())), preferred_element_type=F32)


def dot_nt(a, b):
    return lax.dot_general(a, b, (((1,), (1,)), ((), ())), preferred_element_type=F32)


def open_product(info, first, last):
    r = jnp.float32(1.0)
    for k in range(first, last + 1):
        r = r * (1 - info[2 + k]).astype(F32)
    return r


def query_open(info, level, i):
    mid = ((i >> level) << level) + (1 << (level - 1))
    return open_product(info, mid, i)


def key_open(info, level, j):
    mid = ((j >> level) << level) + (1 << (level - 1))
    return open_product(info, j + 1, mid - 1)


def clean_flags(info, others):
    count = others[0].shape[0] if others else 0
    flags = [None]
    for ref in others:
        worst = ref[0]
        for k in range(1, count):
            worst = worst + ref[k]
        flags.append(jnp.where(worst == 0, 1.0, 0.0))
    worst = info[2]
    for k in range(1, count):
        worst = worst + info[2 + k]
    flags[0] = jnp.where(worst == 0, 1.0, 0.0)
    return flags


def gate_of(info, others, bit, apart=0):
    if bit == 0:
        return jnp.float32(1.0)
    flags = clean_flags(info, others)
    me = info[0]
    device = me ^ apart
    upper = ((device >> bit) & 1) == 1
    gate = jnp.float32(1.0)
    for k in range(len(flags)):
        if k != apart and (k ^ apart) < (1 << bit):
            one = me ^ k
            between = jnp.where(upper, one < device, one > device)
            gate = gate * jnp.where(between, flags[k], 1.0)
    return gate


def scaled_rows(a, factors):
    return jnp.concatenate(
        [a[STRETCH * k : STRETCH * (k + 1)] * f for k, f in enumerate(factors)], 0
    )


def decays(rate_ref, chunk, base, sign, stretches):
    per = CHUNK // WIDTH
    lane_head = lax.broadcasted_iota(jnp.int32, (1, CHUNK), 1) // WIDTH
    row = jnp.zeros((1, CHUNK), F32)
    for k in range(per):
        row = jnp.where(lane_head == k, rate_ref[chunk * per + k], row)
    within = lax.broadcasted_iota(jnp.int32, (STRETCH, CHUNK), 0).astype(F32)
    across = lax.broadcasted_iota(jnp.int32, (stretches, CHUNK), 0).astype(F32) * STRETCH + base
    return jnp.exp(sign * within * row), jnp.exp(sign * across * row)


def decayed(a, tables, i, first=0):
    inner, outer = tables
    return a[STRETCH * i : STRETCH * (i + 1), :] * (inner * outer[first + i : first + i + 1, :])


def weight_of(lam, level, chunk, heads):
    rows = lam.shape[0]
    per = LANES // WIDTH
    lane = lax.broadcasted_iota(jnp.int32, (rows, LANES), 1) // WIDTH
    out = []
    for piece in range(CHUNK // LANES):
        at = lane + (level * heads + piece * per + chunk * (CHUNK // WIDTH))
        out.append(jnp.take_along_axis(lam, at, axis=1))
    return jnp.concatenate(out, 1)


def head_columns(columns):
    d = lax.broadcasted_iota(jnp.int32, (columns, LANES), 0) // WIDTH
    lane = lax.broadcasted_iota(jnp.int32, (columns, LANES), 1)
    return jnp.where(lane == d, 1.0, 0.0).astype(BF16)


def head_sums(ph, pl_, e, level, heads):
    r = dot(ph, e) + dot(pl_, e)
    return pltpu.roll(r, level * heads, 1) if level else r


def rs(a, count=1):
    return slice(STRETCH * a, STRETCH * (a + count))


def each_chunk(columns, body):
    for j in range(columns // CHUNK):
        body(j, slice(j * CHUNK, (j + 1) * CHUNK))


def weighted(cw_ref, lam_ref, i, cols, level, j, heads):
    return cw_ref[rs(i), cols] * weight_of(lam_ref[rs(i), :], level, j, heads)


VMEM = pl.BlockSpec(memory_space=pltpu.VMEM)
SMEM = pl.BlockSpec(memory_space=pltpu.SMEM)
ANY = pl.BlockSpec(memory_space=pl.ANY)


def call(kernel, name, inputs, specs, outs, out_specs, scratch, mib, flops, aliases=None):
    return pl.pallas_call(
        kernel,
        out_shape=[jax.ShapeDtypeStruct(*o) for o in outs],
        in_specs=specs,
        out_specs=out_specs,
        scratch_shapes=scratch,
        input_output_aliases=aliases or {},
        compiler_params=pltpu.CompilerParams(vmem_limit_bytes=mib * 2**20),
        cost_estimate=pl.CostEstimate(flops=flops, bytes_accessed=2**20, transcendentals=0),
        name=name,
    )(*inputs)


def level_scales(shape, axis, heads):
    shift = heads.bit_length() - 1
    level = (lax.broadcasted_iota(jnp.int32, shape, axis) >> shift).astype(F32)
    return jnp.exp2(-0.5 * level - 0.5 * (STRETCH.bit_length() - 1))


def state_of(info, level, bit, heads, b_ref, c_ref, lam_ref, cw_ref, xh, xl, outs, wt, zh, zl):
    rows, columns = xh.shape
    n = b_ref.shape[1]
    stretches = rows // STRETCH
    upper = ((info[0] >> bit) & 1) == 1

    def put(w):
        t = w.T
        wt[:n], wt[n:] = split(t)

    def product(h, l):
        def one(j, cols):
            r = dot(wt[...], h[:, cols])
            v = r[:n] + r[n:] + dot(wt[:n], l[:, cols])
            if bit == 0:
                outs[0][:, cols] = v
            else:
                high = ((info[0] >> (bit - 1)) & 1) == 1
                low_half, high_half = v[: n // 2], v[n // 2 :]
                outs[0][:, cols] = jnp.where(high, low_half, high_half)
                outs[1][:, cols] = jnp.where(high, high_half, low_half)

        each_chunk(columns, one)

    @pl.when(upper)
    def _():
        put(scaled_rows(c_ref[...], [open_product(info, 0, i) for i in range(stretches)]))

        def one(j, cols):
            for i in range(stretches):
                zh[rs(i), cols], zl[rs(i), cols] = split(weighted(cw_ref, lam_ref, i, cols, level, j, heads))

        each_chunk(columns, one)
        product(zh, zl)

    @pl.when(jnp.logical_not(upper))
    def _():
        put(scaled_rows(b_ref[...], [open_product(info, i + 1, stretches - 1) for i in range(stretches)]))
        product(xh, xl)


def state_outs(n, columns, bit):
    return [((n, columns), F32)] if bit == 0 else [((n // 2, columns), F32)] * 2


def first_kernel(heads, level, bit, half, info, rate_ref, x_hbm, cot_hbm, b_hbm, c_hbm, raw_hbm,
                 xh, xl, cw, lam_out, b_ref, c_ref, *rest):
    outs, (xf, raw, wt, zh, zl, sems, more) = rest[:-7], rest[-7:]
    rows, columns = xh.shape
    stretches = rows // STRETCH
    pieces = sems.shape[1]
    size = rows // pieces
    base = (info[0] * rows - half).astype(F32)
    small = [
        pltpu.make_async_copy(src, dst, more.at[k])
        for k, (src, dst) in enumerate(((raw_hbm, raw), (b_hbm, b_ref), (c_hbm, c_ref)))
    ]
    small[0].start()
    copies = []
    for k in range(pieces):
        at = pl.ds(k * size, size)
        copies.append(pltpu.make_async_copy(x_hbm.at[at], xf.at[at], sems.at[0, k]))
        copies[-1].start()
    small[1].start()
    small[2].start()
    for k in range(pieces):
        at = pl.ds(k * size, size)
        copies.append(pltpu.make_async_copy(cot_hbm.at[at], cw.at[at], sems.at[1, k]))
        copies[-1].start()
    small[0].wait()
    lam_out[...] = (raw[...] * level_scales((raw.shape[0], 1), 0, heads)).T
    per = size // STRETCH
    for k in range(pieces):
        copies[k].wait()

        def one(j, cols):
            inner, outer = decays(rate_ref, j, base, 1.0, stretches)
            for i in range(k * per, (k + 1) * per):
                xh[rs(i), cols], xl[rs(i), cols] = split(xf[rs(i), cols] * (inner * outer[i : i + 1, :]))

        each_chunk(columns, one)
    for k in range(pieces):
        copies[pieces + k].wait()

        def one(j, cols):
            inner, outer = decays(rate_ref, j, base, -1.0, stretches)
            for i in range(k * per, (k + 1) * per):
                cw[rs(i), cols] = cw[rs(i), cols] * (inner * outer[i : i + 1, :])

        each_chunk(columns, one)
    small[1].wait()
    small[2].wait()
    state_of(info, level, bit, heads, b_ref, c_ref, lam_out, cw, xh, xl, outs, wt, zh, zl)


def first_state(info, rate, x, cot, b, c, raw, level, bit, half):
    rows, columns = x.shape
    n = b.shape[1]
    wide = ((rows, columns), BF16)
    outs = [wide, wide, ((rows, columns), F32), ((rows, LANES), F32), (b.shape, F32), (c.shape, F32)]
    outs += state_outs(n, columns, bit)
    return call(
        functools.partial(first_kernel, rate.shape[0], level, bit, half),
        f"send_level_{level}",
        (info, rate, x, cot, b, c, raw),
        [SMEM, SMEM, ANY, ANY, ANY, ANY, ANY],
        outs,
        [VMEM] * len(outs),
        [
            pltpu.VMEM((rows, columns), F32),
            pltpu.VMEM(raw.shape, F32),
            pltpu.VMEM((2 * n, rows), BF16),
            pltpu.VMEM((rows, columns), BF16),
            pltpu.VMEM((rows, columns), BF16),
            pltpu.SemaphoreType.DMA((2, 4)),
            pltpu.SemaphoreType.DMA((3,)),
        ],
        41,
        10**9,
    )


def send_kernel(heads, level, bit, info, b_ref, c_ref, lam_ref, cw, xh, xl, *rest):
    state_of(info, level, bit, heads, b_ref, c_ref, lam_ref, cw, xh, xl, rest[:-3], *rest[-3:])


def send_state(info, heads, held, b, c, level, bit):
    xh, xl, cw, lam = held
    rows, columns = xh.shape
    n = b.shape[1]
    outs = state_outs(n, columns, bit)
    return call(
        functools.partial(send_kernel, heads, level, bit),
        f"send_level_{level}",
        (info, b, c, lam, cw, xh, xl),
        [SMEM] + [VMEM] * 6,
        outs,
        [VMEM] * len(outs),
        [
            pltpu.VMEM((2 * n, rows), BF16),
            pltpu.VMEM((rows, columns), BF16),
            pltpu.VMEM((rows, columns), BF16),
        ],
        12,
        10**9,
    )


def sum_kernel(bit, gated, next_bit, info, *rest):
    others = rest[:gated]
    kept, came, *outs = rest[gated:]
    if gated:
        v = kept[...] * gate_of(info, others, bit) + came[...] * gate_of(info, others, bit, 1 << (bit - 1))
    else:
        v = kept[...] + came[...]
    if next_bit is None:
        outs[0][...] = v
    else:
        half = v.shape[0] // 2
        high = ((info[0] >> next_bit) & 1) == 1
        outs[0][...] = jnp.where(high, v[:half], v[half:])
        outs[1][...] = jnp.where(high, v[half:], v[:half])


def sum_step(info, others, kept, came, bit, gated, next_bit):
    rows, columns = kept.shape
    outs = [((rows, columns), F32)] if next_bit is None else [((rows // 2, columns), F32)] * 2
    others = list(others) if gated else []
    return call(
        functools.partial(sum_kernel, bit, len(others), next_bit),
        f"sum_{bit}_{rows}",
        (info, *others, kept, came),
        [SMEM] * (1 + len(others)) + [VMEM] * 2,
        outs,
        [VMEM] * len(outs),
        [],
        4,
        10**7,
    )


def head_halves(info, v, bit, bits):
    size = v.shape[0] >> (bits - bit)
    step = v.shape[0] // size
    mine = (info[1] >> bit) & 1
    away = [v[size * k : size * (k + 1)] for k in range(step)]
    pick = lambda side: jnp.concatenate(
        [jnp.where(side == 1, away[k + 1], away[k]) for k in range(0, step, 2)], 0
    )
    return pick(1 - mine), pick(mine)


def head_sum_kernel(bit, bits, info, kept, came, away_ref, kept_ref):
    away_ref[...], kept_ref[...] = head_halves(info, kept[...] + came[...], bit, bits)


def head_step(info, kept, came, bit, bits):
    rows, n = kept.shape
    return call(
        functools.partial(head_sum_kernel, bit, bits),
        f"heads_{bit}",
        (info, kept, came),
        [SMEM, VMEM, VMEM],
        [((rows // 2, n), F32)] * 2,
        [VMEM] * 2,
        [],
        4,
        10**7,
    )


def head_partner(x, bit):
    return lax.ppermute(x, "head", [(i, i ^ (1 << bit)) for i in range(lax.axis_size("head"))])


def split_rows(a):
    return jnp.concatenate(split(a), 1)


def spread(p, rh, rl, cols):
    n = rh.shape[0]
    h, l = rh[:, cols], rl[:, cols]
    return dot(p, jnp.concatenate([h, h], 0)) + dot(p[:, :n], l)


def gather(h, l, rh, rl):
    n = rh.shape[0]
    both = dot_nt(h, jnp.concatenate([rh[...], rl[...]], 0))
    return both[:, :n] + both[:, n:] + dot_nt(l, rh[...])


def local_kernel(heads, off, info, b_ref, c_ref, lam_ref, cw_ref, xh_ref, xl_ref,
                 gx_ref, gl_ref, gb_ref, gc_ref,
                 p0, p0t, p1, p1t, p2, p2t, s3, s3t, ph, pq, zh, zl, rh, rl):
    rows, columns = gx_ref.shape
    n = b_ref.shape[1]
    stretches = rows // STRETCH

    def own(a, count=1):
        return rs(off + a, count)

    def level_rows(level):
        span = 1 << (level - 1)
        return [(g, g << level, (g << level) + span, span) for g in range(stretches >> level)]

    def product(q, k):
        qh, ql = split(q)
        kh, kl = split(k)
        return dot_nt(jnp.concatenate([qh, ql], 1), jnp.concatenate([kh, kh], 1)) + dot_nt(qh, kl)

    for i in range(stretches):
        cq, bk = c_ref[own(i), :], b_ref[own(i), :]
        t = lax.broadcasted_iota(jnp.int32, (STRETCH, STRETCH), 0)
        s = lax.broadcasted_iota(jnp.int32, (STRETCH, STRETCH), 1)
        h, l = split(jnp.where(t >= s, product(cq, bk), 0.0))
        p0[i] = jnp.concatenate([h, l, h], 1)
        h, l = split(jnp.where(s >= t, product(bk, cq), 0.0))
        p0t[i] = jnp.concatenate([h, l, h], 1)
    scores = {1: (p1, p1t), 2: (p2, p2t), 3: (s3, s3t)}
    for level, ps in scores.items():
        for g, k0, q0, span in level_rows(level):
            cq = scaled_rows(c_ref[own(q0, span), :], [query_open(info, level, off + q0 + a) for a in range(span)])
            bk = scaled_rows(b_ref[own(k0, span), :], [key_open(info, level, off + k0 + a) for a in range(span)])
            for ref, (u, w) in zip(ps, ((cq, bk), (bk, cq))):
                h, l = split(product(u, w))
                ref[g] = jnp.concatenate([h, l, h], 1)

    def apply3(p, h, l):
        return dot(p, jnp.concatenate([h, h, l], 0))

    ones = head_columns(columns)
    mixed = {}
    for level in range(4):
        blocks = [(i, i, i, 1) for i in range(stretches)] if level == 0 else level_rows(level)
        ps, pst = (p0, p0t) if level == 0 else scores[level]

        def one(j, cols):
            at = 0
            for g, k0, q0, span in blocks:
                put = slice(at, at + span * STRETCH)
                for a in range(span):
                    z = weighted(cw_ref, lam_ref, off + q0 + a, cols, level, j, heads)
                    here = slice(at + a * STRETCH, at + (a + 1) * STRETCH)
                    zh[here, cols], zl[here, cols] = split(z)
                y = apply3(ps[g], xh_ref[own(k0, span), cols], xl_ref[own(k0, span), cols])
                ph[put, cols], pq[put, cols] = split(y * cw_ref[own(q0, span), cols])
                gx = apply3(pst[g], zh[put, cols], zl[put, cols])
                if level == 0:
                    gx_ref[rs(k0, span), cols] = gx
                else:
                    gx_ref[rs(k0, span), cols] += gx
                at += span * STRETCH

        each_chunk(columns, one)
        at = 0
        used = len(blocks) * blocks[0][3] * STRETCH
        sums = head_sums(ph[:used], pq[:used], ones, level, heads)
        for g, k0, q0, span in blocks:
            put = slice(at, at + span * STRETCH)
            if level == 0:
                gl_ref[rs(q0, span), :] = sums[put]
            else:
                gl_ref[rs(q0, span), :] += sums[put]
            at += span * STRETCH
        pairs = (
            [(2 * g, 2, 2 * g, 2) for g in range(stretches // 2)]
            if level == 0
            else [(g * span, span, k0, max(span, 2)) for g, k0, q0, span in blocks]
        )
        for key, (z0, zspan, k0, kspan) in enumerate(pairs):
            qh, ql = zh[rs(z0, zspan)], zl[rs(z0, zspan)]
            kh, kl = xh_ref[own(k0, kspan)], xl_ref[own(k0, kspan)]
            if kspan == 2:
                r = dot_nt(qh, jnp.concatenate([kh, kl], 0))
                mixed[level, key] = r[:, :LANES] + r[:, LANES:] + dot_nt(ql, kh)
            else:
                mixed[level, key] = dot_nt(qh, kh) + dot_nt(qh, kl) + dot_nt(ql, kh)

    level = stretches.bit_length()
    keys = [key_open(info, level, j) for j in range(stretches)]
    queries = [query_open(info, level, stretches + j) for j in range(stretches)]
    whole = slice(0, rows)

    def state(h, l, w):
        wh, wl = split(w.T)
        wt = jnp.concatenate([wh, wl], 0)

        def one(j, cols):
            r = dot(wt, h[:, cols])
            rh[:, cols], rl[:, cols] = split(r[:n] + r[n:] + dot(wh, l[:, cols]))

        each_chunk(columns, one)

    def query_z(first):
        def one(j, cols):
            for a in range(stretches):
                zh[rs(a), cols], zl[rs(a), cols] = split(weighted(cw_ref, lam_ref, first + a, cols, level, j, heads))

        each_chunk(columns, one)

    if off == 0:
        query_z(stretches)
        state(zh, zl, scaled_rows(c_ref[rs(stretches, stretches), :], queries))
        middle_rows = scaled_rows(gather(xh_ref[whole], xl_ref[whole], rh, rl), keys)
        pw = split_rows(scaled_rows(b_ref[whole, :], keys))

        def one(j, cols):
            for a in range(0, stretches, 4):
                gx_ref[rs(a, 4), cols] += spread(pw[rs(a, 4)], rh, rl, cols)

        each_chunk(columns, one)
    else:
        state(xh_ref.at[whole], xl_ref.at[whole], scaled_rows(b_ref[whole, :], keys))
        query_z(off)
        middle_rows = scaled_rows(gather(zh[...], zl[...], rh, rl), queries)
        pw = split_rows(scaled_rows(c_ref[own(0, stretches), :], queries))

        def one(j, cols):
            for a in range(0, stretches, 4):
                g = spread(pw[rs(a, 4)], rh, rl, cols)
                ph[rs(a, 4), cols], pq[rs(a, 4), cols] = split(g * cw_ref[own(a, 4), cols])

        each_chunk(columns, one)
        gl_ref[...] += head_sums(ph[...], pq[...], ones, level, heads)

    def times(m, w):
        mh, ml = split(m)
        wh, wl = split(w)
        r = dot(mh, jnp.concatenate([wh, wl], 1))
        return r[:, :n] + r[:, n:] + dot(ml, wh)

    wide = 2 * STRETCH
    t = lax.broadcasted_iota(jnp.int32, (wide, wide), 0)
    s = lax.broadcasted_iota(jnp.int32, (wide, wide), 1)
    for g in range(stretches // 4):
        rows4 = rs(4 * g, 4)
        blocks = []
        for d in range(2):
            at = 2 * g + d
            own_pair = jnp.where((t >= s) & (t // STRETCH == s // STRETCH), mixed[0, at], 0.0)
            valid = open_product(info, off + 2 * at + 1, off + 2 * at + 1)
            low = jnp.concatenate([jnp.zeros((STRETCH, wide), F32), mixed[1, at] * valid], 0)
            blocks.append(own_pair + jnp.where(s < STRETCH, low, 0.0))
        q = [query_open(info, 2, off + 4 * g + 2 + a) for a in range(2)]
        k = [key_open(info, 2, off + 4 * g + a) for a in range(2)]
        m_two = scaled_rows(mixed[2, g], q)
        m_two = jnp.where(s < STRETCH, m_two * k[0], m_two * k[1])
        m = jnp.concatenate(
            [
                jnp.concatenate([blocks[0], jnp.zeros((wide, wide), F32)], 1),
                jnp.concatenate([m_two, blocks[1]], 1),
            ],
            0,
        )
        gc_ref[rows4, :] = times(m, b_ref[own(4 * g, 4), :])
        gb_ref[rows4, :] = times(m.T, c_ref[own(4 * g, 4), :])
    q = [query_open(info, 3, off + 4 + a) for a in range(4)]
    k = [key_open(info, 3, off + a) for a in range(4)]
    m = mixed[3, 0]
    gc_ref[rs(4, 4), :] += scaled_rows(times(m, scaled_rows(b_ref[own(0, 4), :], k)), q)
    gb_ref[rs(0, 4), :] += scaled_rows(times(m.T, scaled_rows(c_ref[own(4, 4), :], q)), k)
    if off == 0:
        gb_ref[...] += middle_rows
    else:
        gc_ref[...] += middle_rows


def local_levels(info, heads, held, b, c, part):
    xh, xl, cw, lam = held
    rows, columns = xh.shape[0] // 2, xh.shape[1]
    n = b.shape[1]
    stretches = rows // STRETCH
    three, wide = 3 * STRETCH, 2 * STRETCH
    return call(
        functools.partial(local_kernel, heads, part * stretches),
        f"local_levels_{part}",
        (info, b, c, lam, cw, xh, xl),
        [SMEM] + [VMEM] * 6,
        [((rows, columns), F32), ((rows, LANES), F32), ((rows, n), F32), ((rows, n), F32)],
        [VMEM] * 4,
        [
            pltpu.VMEM((stretches, STRETCH, three), BF16),
            pltpu.VMEM((stretches, STRETCH, three), BF16),
            pltpu.VMEM((stretches // 2, STRETCH, three), BF16),
            pltpu.VMEM((stretches // 2, STRETCH, three), BF16),
            pltpu.VMEM((stretches // 4, wide, 3 * wide), BF16),
            pltpu.VMEM((stretches // 4, wide, 3 * wide), BF16),
            pltpu.VMEM((1, 2 * wide, 6 * wide), BF16),
            pltpu.VMEM((1, 2 * wide, 6 * wide), BF16),
            pltpu.VMEM((rows, columns), BF16),
            pltpu.VMEM((rows, columns), BF16),
            pltpu.VMEM((rows, columns), BF16),
            pltpu.VMEM((rows, columns), BF16),
            pltpu.VMEM((n, columns), BF16),
            pltpu.VMEM((n, columns), BF16),
        ],
        16,
        9 * 10**9,
    )


def masks(info, stretches):
    prefix = [open_product(info, 0, i) for i in range(stretches)]
    suffix = [open_product(info, i + 1, stretches - 1) for i in range(stretches)]
    return prefix, suffix


def assemble(info, bit, pieces, out):
    size = pieces[0].shape[0]
    for k, piece in enumerate(pieces):
        at = ((info[0] ^ k) & ((1 << bit) - 1)) * size
        out[pl.ds(pl.multiple_of(at, size), size), :] = piece[...]


def level_sums(level, heads, p, cw, rh, rl, ph, pq, ones):
    rows, columns = cw.shape

    def one(j, cols):
        for a in range(0, rows // STRETCH, 4):
            g = spread(p[rs(a, 4)], rh, rl, cols)
            ph[rs(a, 4), cols], pq[rs(a, 4), cols] = split(g * cw[rs(a, 4), cols])

    each_chunk(columns, one)
    return head_sums(ph[...], pq[...], ones, level, heads)


def query_z(heads, level, lam_ref, cw, zh, zl):
    rows, columns = cw.shape

    def one(j, cols):
        for i in range(rows // STRETCH):
            zh[rs(i), cols], zl[rs(i), cols] = split(weighted(cw, lam_ref, i, cols, level, j, heads))

    each_chunk(columns, one)


def early_kernel(heads, level0, bits, top, head_bits, known, info, *rest):
    others, rest = rest[:known], rest[known:]
    b_ref, c_ref, lam_ref, cw, xh, xl, gla, glb, gba, gbb, gca, gcb, *rest = rest
    states = []
    for bit in bits:
        states.append(rest[: 1 << bit])
        rest = rest[1 << bit :]
    low_ref, gl_ref, sel_ref, away_ref, kept_ref, pc, ph, pq, rh, rl, gbs, gcs, rf = rest
    rows, columns = xh.shape
    stretches = rows // STRETCH
    mid = stretches // 2
    me = info[0]
    prefix, suffix = masks(info, stretches)
    uppers = [((me >> bit) & 1) == 1 for bit in bits]
    gates = [gate_of(info, others, bit) for bit in bits]
    ones = head_columns(columns)
    for dst, (one, two) in ((gl_ref, (gla, glb)), (gbs, (gba, gbb)), (gcs, (gca, gcb))):
        dst[rs(0, mid), :], dst[rs(mid, mid), :] = one[...], two[...]
    pc[...] = split_rows(scaled_rows(c_ref[...], prefix))
    low_ref[...] = jnp.zeros_like(low_ref)
    for k, bit in enumerate(bits):
        assemble(info, bit, states[k], rf)

        @pl.when(jnp.logical_not(uppers[k]))
        def _():
            low_ref[...] += rf[...] * gates[k]

        @pl.when(uppers[k])
        def _():
            rh[...], rl[...] = split(rf[...] * gates[k])
            query_z(heads, level0 + bit, lam_ref, cw, ph, pq)
            gcs[...] += scaled_rows(gather(ph[...], pq[...], rh, rl), prefix)
            gl_ref[...] += level_sums(level0 + bit, heads, pc, cw, rh, rl, ph, pq, ones)

    below = (1 << top) - 1

    @pl.when((me & below) != below)
    def _():
        rh[...], rl[...] = split(low_ref[...])
        gbs[...] += scaled_rows(gather(xh[...], xl[...], rh, rl), suffix)

    last = ((me >> top) & 1) == 1

    def finish(sel, other):
        sel_ref[...] = sel[...]
        if head_bits:
            away_ref[...], kept_ref[...] = head_halves(info, other[...], 0, head_bits)
        else:
            away_ref[...] = other[...]
            kept_ref[...] = other[...]

    @pl.when(last)
    def _():
        finish(gcs, gbs)

    @pl.when(jnp.logical_not(last))
    def _():
        finish(gbs, gcs)


def half_rows(rows, n, head_bits):
    return ((rows // 2 if head_bits else rows, n), F32)


def early_states(info, others, heads, held, b, c, sums, states, bits, top, level0, head_bits):
    xh, xl, cw, lam = held
    rows, columns = xh.shape
    n = b.shape[1]
    inputs = (info, *others, b, c, lam, cw, xh, xl, *sums, *(p for q in states for p in q))
    wide = pltpu.VMEM((rows, columns), BF16)
    state = pltpu.VMEM((n, columns), BF16)
    own = pltpu.VMEM((rows, n), F32)
    return call(
        functools.partial(early_kernel, heads, level0, bits, top, head_bits, len(others)),
        "apply_" + "_".join(str(level0 + b) for b in bits),
        inputs,
        [SMEM] * (1 + len(others)) + [VMEM] * (len(inputs) - 1 - len(others)),
        [((n, columns), F32), ((rows, LANES), F32), ((rows, n), F32)] + [half_rows(rows, n, head_bits)] * 2,
        [VMEM] * 5,
        [pltpu.VMEM((rows, 2 * n), BF16), wide, wide, state, state, own, own, pltpu.VMEM((n, columns), F32)],
        16,
        len(bits) * 2 * 10**9,
    )


def last_rows_kernel(heads, top, level, head_bits, known, info, *rest):
    others, rest = rest[:known], rest[known:]
    lam_ref, cw, xh, xl, sel_ref, *rest = rest
    pieces, (away_ref, kept_ref, state_ref, rh, rl, zh, zl) = rest[: 1 << top], rest[1 << top :]
    prefix, suffix = masks(info, xh.shape[0] // STRETCH)
    upper = ((info[0] >> top) & 1) == 1
    assemble(info, top, pieces, state_ref)
    state_ref[...] = state_ref[...] * gate_of(info, others, top)
    rh[...], rl[...] = split(state_ref[...])

    def finish(v):
        if head_bits:
            away_ref[...], kept_ref[...] = head_halves(info, v, 0, head_bits)
        else:
            away_ref[...] = v
            kept_ref[...] = v

    @pl.when(upper)
    def _():
        query_z(heads, level, lam_ref, cw, zh, zl)
        finish(sel_ref[...] + scaled_rows(gather(zh[...], zl[...], rh, rl), prefix))

    @pl.when(jnp.logical_not(upper))
    def _():
        finish(sel_ref[...] + scaled_rows(gather(xh[...], xl[...], rh, rl), suffix))


def last_rows(info, others, heads, held, pieces, sel, top, level, head_bits):
    xh, xl, cw, lam = held
    rows, columns = xh.shape
    n = sel.shape[1]
    inputs = (info, *others, lam, cw, xh, xl, sel, *pieces)
    return call(
        functools.partial(last_rows_kernel, heads, top, level, head_bits, len(others)),
        f"rows_{level}",
        inputs,
        [SMEM] * (1 + len(others)) + [VMEM] * (len(inputs) - 1 - len(others)),
        [half_rows(rows, n, head_bits)] * 2 + [((n, columns), F32)],
        [VMEM] * 3,
        [pltpu.VMEM((n, columns), BF16)] * 2 + [pltpu.VMEM((rows, columns), BF16)] * 2,
        12,
        10**9,
    )


def last_kernel(heads, half, top, level, info, rate_ref, b_ref, c_ref, cw, gxa, gxb, r_ref, low_ref, gl_in,
                gx_hbm, gl_ref, pw, ph, pq, rh, rl, of, gls, sems):
    rows, columns = cw.shape
    stretches = rows // STRETCH
    mid = stretches // 2
    me = info[0]
    base = (me * rows - half).astype(F32)
    prefix, suffix = masks(info, stretches)
    upper = ((me >> top) & 1) == 1
    gls[...] = gl_in[...]

    @pl.when(upper)
    def _():
        rh[...], rl[...] = split(r_ref[...])
        pw[...] = split_rows(scaled_rows(c_ref[...], prefix))
        gls[...] += level_sums(level, heads, pw, cw, rh, rl, ph, pq, head_columns(columns))

    pieces = sems.shape[0]
    per = stretches // pieces

    def copy(k):
        at = pl.ds(k * per * STRETCH, per * STRETCH)
        return pltpu.make_async_copy(of.at[at], gx_hbm.at[at], sems.at[k])

    def finish(any_low):
        if any_low:
            rh[...], rl[...] = split(low_ref[...] + r_ref[...] * jnp.where(upper, 0.0, 1.0))
            pw[...] = split_rows(scaled_rows(b_ref[...], suffix))
        for k in range(pieces):

            def one(j, cols):
                inner, outer = decays(rate_ref, j, base, 1.0, stretches)
                extra = spread(pw[rs(k * per, per)], rh, rl, cols) if any_low else None
                for i in range(k * per, (k + 1) * per):
                    g = gxa[rs(i), cols] if i < mid else gxb[rs(i - mid), cols]
                    if any_low:
                        g = g + extra[rs(i - k * per)]
                    of[rs(i), cols] = g * (inner * outer[i : i + 1, :])

            each_chunk(columns, one)
            copy(k).start()

    below = (2 << top) - 1

    @pl.when((me & below) == below)
    def _():
        finish(False)

    @pl.when((me & below) != below)
    def _():
        finish(True)

    lanes = gl_ref.shape[0]
    gl_ref[...] = gls[...].T[:lanes] * level_scales((lanes, 1), 0, heads)
    for k in range(pieces):
        copy(k).wait()


def last_state(info, rate, held, b, c, gx, state, low, gl, half, top, level, lanes):
    cw = held[2]
    rows, columns = cw.shape
    n = b.shape[1]
    wide = pltpu.VMEM((rows, columns), BF16)
    held_state = pltpu.VMEM((n, columns), BF16)
    return call(
        functools.partial(last_kernel, rate.shape[0], half, top, level),
        f"apply_{level}",
        (info, rate, b, c, cw, *gx, state, low, gl),
        [SMEM] * 2 + [VMEM] * 8,
        [((rows, columns), F32), ((lanes, rows), F32)],
        [ANY, VMEM],
        [
            pltpu.VMEM((rows, 2 * n), BF16),
            wide,
            wide,
            held_state,
            held_state,
            pltpu.VMEM((rows, columns), F32),
            pltpu.VMEM((rows, LANES), F32),
            pltpu.SemaphoreType.DMA((4,)),
        ],
        20,
        3 * 10**9,
    )


def after(x, *others):
    return lax.optimization_barrier((x, *others))[0]


class Swap:
    def __init__(self, info, others, outs, bit):
        self.info, self.others, self.bit, self.phase = info, others, bit, 0
        if bit == 0:
            self.came = partner(outs[0], 1)
        else:
            self.away, self.kept = outs
            self.came = partner(self.away, 1 << (bit - 1))

    @property
    def done(self):
        return self.phase > self.bit

    def step(self):
        k, bit = self.phase, self.bit
        self.phase += 1
        if k < bit:
            next_bit = bit - 2 - k if k < bit - 1 else None
            outs = sum_step(self.info, self.others, self.kept, self.came, bit, k == 0, next_bit)
            if next_bit is None:
                self.came = partner(outs[0], 1 << bit)
            else:
                self.away, self.kept = outs
                self.came = partner(self.away, 1 << next_bit)
            return outs[0]
        own = self.came
        self.pieces = [own] + [partner(own, j) for j in range(1, 1 << bit)]
        return own


def local(inputs, cotangent, b_proj, c_proj, decay_rate, level_weight, starts):
    rows = inputs.shape[0]
    heads = decay_rate.shape[0]
    stretches = rows // STRETCH
    seq_count = lax.axis_size("seq")
    seq_bits = seq_count.bit_length() - 1
    head_bits = lax.axis_size("head").bit_length() - 1
    half = seq_count * rows // 2
    me = lax.axis_index("seq").astype(jnp.int32)
    lanes = level_weight.shape[0] * heads
    level0 = stretches.bit_length()
    top = seq_bits - 1
    others = [partner(starts, k) for k in range(1, 1 << top)]
    info = jnp.concatenate([me.reshape(1), lax.axis_index("head").astype(jnp.int32).reshape(1), starts])
    raw_lam = level_weight.reshape(lanes, rows)
    if lanes < LANES:
        raw_lam = jnp.pad(raw_lam, ((0, LANES - lanes), (0, 0)))

    order = [*range(1, seq_bits), 0]
    b = order[0]
    *held, bv, cv, away, kept = first_state(
        info, decay_rate, inputs, cotangent, b_proj, c_proj, raw_lam, level0 + b, b, half
    )
    swaps = {b: Swap(info, others, (away, kept), b)}
    tied = after(info, kept)
    for b in order[1:]:
        outs = send_state(tied, heads, held, bv, cv, level0 + b, b)
        swaps[b] = Swap(info, others, outs, b)
        tied = after(info, outs[-1])
    waits = [swaps[b].step() for b in range(1, seq_bits)]
    part0 = local_levels(after(tied, *waits), heads, held, bv, cv, 0)
    for b in range(1, seq_bits):
        swaps[b].info = after(info, part0[3])
        swaps[b].came = after(swaps[b].came, part0[3])
    waits = [swaps[b].step() for b in range(1, seq_bits)]
    part1 = local_levels(after(info, part0[3], *waits), heads, held, bv, cv, 1)
    waits = []
    for b in range(seq_bits):
        swaps[b].info = after(info, part1[3])
        swaps[b].came = after(swaps[b].came, part1[3])
        while not swaps[b].done:
            waits.append(swaps[b].step())
    sums = [p[k] for k in range(1, 4) for p in (part0, part1)]
    early = tuple(range(top))
    low, gl, sel, away, kept = early_states(
        after(info, *waits), others, heads, held, bv, cv, sums, [swaps[b].pieces for b in early], early, top, level0, head_bits
    )
    level = level0 + top
    came = head_partner(away, 0)
    pieces = [after(p, kept) for p in swaps[top].pieces]
    away, mine, state = last_rows(info, others, heads, held, pieces, sel, top, level, head_bits)
    sel_came = head_partner(away, 0)
    others_info = after(info, mine)
    other = (kept, came)
    sel = (mine, sel_came)
    waits = []
    for bit in range(1, head_bits):
        away, kept = head_step(others_info, *other, bit, head_bits)
        other = (kept, head_partner(away, bit))
        waits.append(kept)
        away, kept = head_step(others_info, *sel, bit, head_bits)
        sel = (kept, head_partner(away, bit))
        waits.append(kept)
    grad_x, gl = last_state(
        after(info, *waits), decay_rate, held, bv, cv, (part0[0], part1[0]), state, low, gl, half, top, level, lanes
    )
    other, sel = (after(u, gl) + after(v, gl) for u, v in (other, sel))
    upper = ((after(me, gl) >> top) & 1) == 1
    return (grad_x, jnp.where(upper, other, sel), jnp.where(upper, sel, other), gl.reshape(level_weight.shape))


def solution(mesh):
    return jax.shard_map(
        local,
        mesh=mesh,
        in_specs=(
            P("seq", "head"),
            P("seq", "head"),
            P("seq", None),
            P("seq", None),
            P("head"),
            P(None, "head", "seq"),
            P("seq"),
        ),
        out_specs=(
            P("seq", "head"),
            P(("seq", "head"), None),
            P(("seq", "head"), None),
            P(None, "head", "seq"),
        ),
        check_vma=False,
    )
```

```python
import functools

import jax
import jax.numpy as jnp
from jax import lax
from jax.experimental import pallas as pl
from jax.experimental.pallas import tpu as pltpu
from jax.sharding import PartitionSpec as P

KERNELS = True
STRETCH = 64
WIDTH = 64
CHUNK = 256
LANES = 128
F32 = jnp.float32
BF16 = jnp.bfloat16


def partner(x, apart):
    return lax.ppermute(x, "seq", [(i, i ^ apart) for i in range(lax.axis_size("seq"))])


def split(a):
    hi = a.astype(BF16)
    return hi, (a - hi.astype(F32)).astype(BF16)


def dot(a, b):
    return lax.dot_general(a, b, (((1,), (0,)), ((), ())), preferred_element_type=F32)


def dot_nt(a, b):
    return lax.dot_general(a, b, (((1,), (1,)), ((), ())), preferred_element_type=F32)


def open_product(info, first, last):
    r = jnp.float32(1.0)
    for k in range(first, last + 1):
        r = r * (1 - info[2 + k]).astype(F32)
    return r


def query_open(info, level, i):
    mid = ((i >> level) << level) + (1 << (level - 1))
    return open_product(info, mid, i)


def key_open(info, level, j):
    mid = ((j >> level) << level) + (1 << (level - 1))
    return open_product(info, j + 1, mid - 1)


def clean_flags(info, others):
    count = others[0].shape[0] if others else 0
    flags = [None]
    for ref in others:
        worst = ref[0]
        for k in range(1, count):
            worst = worst + ref[k]
        flags.append(jnp.where(worst == 0, 1.0, 0.0))
    worst = info[2]
    for k in range(1, count):
        worst = worst + info[2 + k]
    flags[0] = jnp.where(worst == 0, 1.0, 0.0)
    return flags


def gate_of(info, others, bit, apart=0):
    if bit == 0:
        return jnp.float32(1.0)
    flags = clean_flags(info, others)
    me = info[0]
    device = me ^ apart
    upper = ((device >> bit) & 1) == 1
    gate = jnp.float32(1.0)
    for k in range(len(flags)):
        if k != apart and (k ^ apart) < (1 << bit):
            one = me ^ k
            between = jnp.where(upper, one < device, one > device)
            gate = gate * jnp.where(between, flags[k], 1.0)
    return gate


def scaled_rows(a, factors):
    return jnp.concatenate(
        [a[STRETCH * k : STRETCH * (k + 1)] * f for k, f in enumerate(factors)], 0
    )


def decays(rate_ref, chunk, base, sign, stretches):
    per = CHUNK // WIDTH
    lane_head = lax.broadcasted_iota(jnp.int32, (1, CHUNK), 1) // WIDTH
    row = jnp.zeros((1, CHUNK), F32)
    for k in range(per):
        row = jnp.where(lane_head == k, rate_ref[chunk * per + k], row)
    within = lax.broadcasted_iota(jnp.int32, (STRETCH, CHUNK), 0).astype(F32)
    across = lax.broadcasted_iota(jnp.int32, (stretches, CHUNK), 0).astype(F32) * STRETCH + base
    return jnp.exp(sign * within * row), jnp.exp(sign * across * row)


def decayed(a, tables, i, first=0):
    inner, outer = tables
    return a[STRETCH * i : STRETCH * (i + 1), :] * (inner * outer[first + i : first + i + 1, :])


def weight_of(lam, level, chunk, heads):
    rows = lam.shape[0]
    per = LANES // WIDTH
    lane = lax.broadcasted_iota(jnp.int32, (rows, LANES), 1) // WIDTH
    out = []
    for piece in range(CHUNK // LANES):
        at = lane + (level * heads + piece * per + chunk * (CHUNK // WIDTH))
        out.append(jnp.take_along_axis(lam, at, axis=1))
    return jnp.concatenate(out, 1)


def head_columns(columns):
    d = lax.broadcasted_iota(jnp.int32, (columns, LANES), 0) // WIDTH
    lane = lax.broadcasted_iota(jnp.int32, (columns, LANES), 1)
    return jnp.where(lane == d, 1.0, 0.0).astype(BF16)


def head_sums(ph, pl_, e, level, heads):
    r = dot(ph, e) + dot(pl_, e)
    return pltpu.roll(r, level * heads, 1) if level else r


def rs(a, count=1):
    return slice(STRETCH * a, STRETCH * (a + count))


def each_chunk(columns, body):
    for j in range(columns // CHUNK):
        body(j, slice(j * CHUNK, (j + 1) * CHUNK))


def weighted(cw_ref, lam_ref, i, cols, level, j, heads):
    return cw_ref[rs(i), cols] * weight_of(lam_ref[rs(i), :], level, j, heads)


VMEM = pl.BlockSpec(memory_space=pltpu.VMEM)
SMEM = pl.BlockSpec(memory_space=pltpu.SMEM)
ANY = pl.BlockSpec(memory_space=pl.ANY)


def call(kernel, name, inputs, specs, outs, out_specs, scratch, mib, flops, aliases=None):
    return pl.pallas_call(
        kernel,
        out_shape=[jax.ShapeDtypeStruct(*o) for o in outs],
        in_specs=specs,
        out_specs=out_specs,
        scratch_shapes=scratch,
        input_output_aliases=aliases or {},
        compiler_params=pltpu.CompilerParams(vmem_limit_bytes=mib * 2**20),
        cost_estimate=pl.CostEstimate(flops=flops, bytes_accessed=2**20, transcendentals=0),
        name=name,
    )(*inputs)


def level_scales(shape, axis, heads):
    shift = heads.bit_length() - 1
    level = (lax.broadcasted_iota(jnp.int32, shape, axis) >> shift).astype(F32)
    return jnp.exp2(-0.5 * level - 0.5 * (STRETCH.bit_length() - 1))


def state_of(info, level, bit, heads, b_ref, c_ref, lam_ref, cw_ref, xh, xl, outs, wt, zh, zl):
    rows, columns = xh.shape
    n = b_ref.shape[1]
    stretches = rows // STRETCH
    upper = ((info[0] >> bit) & 1) == 1

    def put(w):
        t = w.T
        wt[:n], wt[n:] = split(t)

    def product(h, l):
        def one(j, cols):
            r = dot(wt[...], h[:, cols])
            v = r[:n] + r[n:] + dot(wt[:n], l[:, cols])
            if bit == 0:
                outs[0][:, cols] = v
            else:
                high = ((info[0] >> (bit - 1)) & 1) == 1
                low_half, high_half = v[: n // 2], v[n // 2 :]
                outs[0][:, cols] = jnp.where(high, low_half, high_half)
                outs[1][:, cols] = jnp.where(high, high_half, low_half)

        each_chunk(columns, one)

    @pl.when(upper)
    def _():
        put(scaled_rows(c_ref[...], [open_product(info, 0, i) for i in range(stretches)]))

        def one(j, cols):
            for i in range(stretches):
                zh[rs(i), cols], zl[rs(i), cols] = split(weighted(cw_ref, lam_ref, i, cols, level, j, heads))

        each_chunk(columns, one)
        product(zh, zl)

    @pl.when(jnp.logical_not(upper))
    def _():
        put(scaled_rows(b_ref[...], [open_product(info, i + 1, stretches - 1) for i in range(stretches)]))
        product(xh, xl)


def state_outs(n, columns, bit):
    return [((n, columns), F32)] if bit == 0 else [((n // 2, columns), F32)] * 2


def first_kernel(heads, level, bit, half, info, rate_ref, x_hbm, cot_hbm, b_hbm, c_hbm, raw_hbm,
                 xh, xl, cw, lam_out, b_ref, c_ref, *rest):
    zh, zl, *rest = rest
    outs, (xf, raw, wt, sems, more) = rest[:-5], rest[-5:]
    rows, columns = xh.shape
    stretches = rows // STRETCH
    pieces = sems.shape[1]
    size = rows // pieces
    base = (info[0] * rows - half).astype(F32)
    small = [
        pltpu.make_async_copy(src, dst, more.at[k])
        for k, (src, dst) in enumerate(((raw_hbm, raw), (b_hbm, b_ref), (c_hbm, c_ref)))
    ]
    small[0].start()
    copies = []
    for k in range(pieces):
        at = pl.ds(k * size, size)
        copies.append(pltpu.make_async_copy(x_hbm.at[at], xf.at[at], sems.at[0, k]))
        copies[-1].start()
    small[1].start()
    small[2].start()
    for k in range(pieces):
        at = pl.ds(k * size, size)
        copies.append(pltpu.make_async_copy(cot_hbm.at[at], cw.at[at], sems.at[1, k]))
        copies[-1].start()
    small[0].wait()
    lam_out[...] = (raw[...] * level_scales((raw.shape[0], 1), 0, heads)).T
    per = size // STRETCH
    for k in range(pieces):
        copies[k].wait()

        def one(j, cols):
            inner, outer = decays(rate_ref, j, base, 1.0, stretches)
            for i in range(k * per, (k + 1) * per):
                xh[rs(i), cols], xl[rs(i), cols] = split(xf[rs(i), cols] * (inner * outer[i : i + 1, :]))

        each_chunk(columns, one)
    for k in range(pieces):
        copies[pieces + k].wait()

        def one(j, cols):
            inner, outer = decays(rate_ref, j, base, -1.0, stretches)
            for i in range(k * per, (k + 1) * per):
                cw[rs(i), cols] = cw[rs(i), cols] * (inner * outer[i : i + 1, :])

        each_chunk(columns, one)
    small[1].wait()
    small[2].wait()
    state_of(info, level, bit, heads, b_ref, c_ref, lam_out, cw, xh, xl, outs, wt, zh, zl)


def first_state(info, rate, x, cot, b, c, raw, level, bit, half):
    rows, columns = x.shape
    n = b.shape[1]
    wide = ((rows, columns), BF16)
    outs = [wide, wide, ((rows, columns), F32), ((rows, LANES), F32), (b.shape, F32), (c.shape, F32), wide, wide]
    outs += state_outs(n, columns, bit)
    return call(
        functools.partial(first_kernel, rate.shape[0], level, bit, half),
        f"send_level_{level}",
        (info, rate, x, cot, b, c, raw),
        [SMEM, SMEM, ANY, ANY, ANY, ANY, ANY],
        outs,
        [VMEM] * len(outs),
        [
            pltpu.VMEM((rows, columns), F32),
            pltpu.VMEM(raw.shape, F32),
            pltpu.VMEM((2 * n, rows), BF16),
            pltpu.SemaphoreType.DMA((2, 4)),
            pltpu.SemaphoreType.DMA((3,)),
        ],
        37,
        10**9,
    )


def send_kernel(heads, level, bit, info, b_ref, c_ref, lam_ref, cw, xh, xl, *rest):
    zh, zl, *rest = rest
    state_of(info, level, bit, heads, b_ref, c_ref, lam_ref, cw, xh, xl, rest[:-1], rest[-1], zh, zl)


def send_state(info, heads, held, b, c, level, bit):
    xh, xl, cw, lam = held
    rows, columns = xh.shape
    n = b.shape[1]
    outs = [((rows, columns), BF16)] * 2 + state_outs(n, columns, bit)
    return call(
        functools.partial(send_kernel, heads, level, bit),
        f"send_level_{level}",
        (info, b, c, lam, cw, xh, xl),
        [SMEM] + [VMEM] * 6,
        outs,
        [VMEM] * len(outs),
        [pltpu.VMEM((2 * n, rows), BF16)],
        8,
        10**9,
    )


def sum_kernel(bit, gated, next_bit, info, *rest):
    others = rest[:gated]
    kept, came, *outs = rest[gated:]
    if gated:
        v = kept[...] * gate_of(info, others, bit) + came[...] * gate_of(info, others, bit, 1 << (bit - 1))
    else:
        v = kept[...] + came[...]
    if next_bit is None:
        outs[0][...] = v
    else:
        half = v.shape[0] // 2
        high = ((info[0] >> next_bit) & 1) == 1
        outs[0][...] = jnp.where(high, v[:half], v[half:])
        outs[1][...] = jnp.where(high, v[half:], v[:half])


def sum_step(info, others, kept, came, bit, gated, next_bit):
    rows, columns = kept.shape
    outs = [((rows, columns), F32)] if next_bit is None else [((rows // 2, columns), F32)] * 2
    others = list(others) if gated else []
    return call(
        functools.partial(sum_kernel, bit, len(others), next_bit),
        f"sum_{bit}_{rows}",
        (info, *others, kept, came),
        [SMEM] * (1 + len(others)) + [VMEM] * 2,
        outs,
        [VMEM] * len(outs),
        [],
        4,
        10**7,
    )


def head_halves(info, v, bit, bits):
    size = v.shape[0] >> (bits - bit)
    step = v.shape[0] // size
    mine = (info[1] >> bit) & 1
    away = [v[size * k : size * (k + 1)] for k in range(step)]
    pick = lambda side: jnp.concatenate(
        [jnp.where(side == 1, away[k + 1], away[k]) for k in range(0, step, 2)], 0
    )
    return pick(1 - mine), pick(mine)


def head_sum_kernel(bit, bits, info, kept, came, away_ref, kept_ref):
    size = away_ref.shape[0] // 2
    for k in range(2):
        part = slice(2 * size * k, 2 * size * (k + 1))
        at = slice(size * k, size * (k + 1))
        away_ref[at], kept_ref[at] = head_halves(info, kept[part] + came[part], bit, bits)


def head_step(info, kept, came, bit, bits):
    rows, n = kept.shape
    return call(
        functools.partial(head_sum_kernel, bit, bits),
        f"heads_{bit}",
        (info, kept, came),
        [SMEM, VMEM, VMEM],
        [((rows // 2, n), F32)] * 2,
        [VMEM] * 2,
        [],
        4,
        10**7,
    )


def head_partner(x, bit):
    return lax.ppermute(x, "head", [(i, i ^ (1 << bit)) for i in range(lax.axis_size("head"))])


def split_rows(a):
    return jnp.concatenate(split(a), 1)


def spread(p, rh, rl, cols):
    n = rh.shape[0]
    h, l = rh[:, cols], rl[:, cols]
    return dot(p, jnp.concatenate([h, h], 0)) + dot(p[:, :n], l)


def gather(h, l, rh, rl):
    n = rh.shape[0]
    both = dot_nt(h, jnp.concatenate([rh[...], rl[...]], 0))
    return both[:, :n] + both[:, n:] + dot_nt(l, rh[...])


def local_kernel(heads, off, info, b_ref, c_ref, lam_ref, cw_ref, xh_ref, xl_ref,
                 gx_ref, gl_ref, gb_ref, gc_ref,
                 p0, p0t, p1, p1t, p2, p2t, s3, s3t, ph, pq, zh, zl, rh, rl):
    rows, columns = gx_ref.shape
    n = b_ref.shape[1]
    stretches = rows // STRETCH

    def own(a, count=1):
        return rs(off + a, count)

    def level_rows(level):
        span = 1 << (level - 1)
        return [(g, g << level, (g << level) + span, span) for g in range(stretches >> level)]

    def product(q, k):
        qh, ql = split(q)
        kh, kl = split(k)
        return dot_nt(jnp.concatenate([qh, ql], 1), jnp.concatenate([kh, kh], 1)) + dot_nt(qh, kl)

    for i in range(stretches):
        cq, bk = c_ref[own(i), :], b_ref[own(i), :]
        t = lax.broadcasted_iota(jnp.int32, (STRETCH, STRETCH), 0)
        s = lax.broadcasted_iota(jnp.int32, (STRETCH, STRETCH), 1)
        h, l = split(jnp.where(t >= s, product(cq, bk), 0.0))
        p0[i] = jnp.concatenate([h, l, h], 1)
        h, l = split(jnp.where(s >= t, product(bk, cq), 0.0))
        p0t[i] = jnp.concatenate([h, l, h], 1)
    scores = {1: (p1, p1t), 2: (p2, p2t), 3: (s3, s3t)}
    for level, ps in scores.items():
        for g, k0, q0, span in level_rows(level):
            cq = scaled_rows(c_ref[own(q0, span), :], [query_open(info, level, off + q0 + a) for a in range(span)])
            bk = scaled_rows(b_ref[own(k0, span), :], [key_open(info, level, off + k0 + a) for a in range(span)])
            for ref, (u, w) in zip(ps, ((cq, bk), (bk, cq))):
                h, l = split(product(u, w))
                ref[g] = jnp.concatenate([h, l, h], 1)

    def apply3(p, h, l):
        return dot(p, jnp.concatenate([h, h, l], 0))

    ones = head_columns(columns)
    mixed = {}
    for level in range(4):
        blocks = [(i, i, i, 1) for i in range(stretches)] if level == 0 else level_rows(level)
        ps, pst = (p0, p0t) if level == 0 else scores[level]

        def one(j, cols):
            at = 0
            for g, k0, q0, span in blocks:
                put = slice(at, at + span * STRETCH)
                for a in range(span):
                    z = weighted(cw_ref, lam_ref, off + q0 + a, cols, level, j, heads)
                    here = slice(at + a * STRETCH, at + (a + 1) * STRETCH)
                    zh[here, cols], zl[here, cols] = split(z)
                y = apply3(ps[g], xh_ref[own(k0, span), cols], xl_ref[own(k0, span), cols])
                ph[put, cols], pq[put, cols] = split(y * cw_ref[own(q0, span), cols])
                gx = apply3(pst[g], zh[put, cols], zl[put, cols])
                if level == 0:
                    gx_ref[rs(k0, span), cols] = gx
                else:
                    gx_ref[rs(k0, span), cols] += gx
                at += span * STRETCH

        each_chunk(columns, one)
        at = 0
        used = len(blocks) * blocks[0][3] * STRETCH
        sums = head_sums(ph[:used], pq[:used], ones, level, heads)
        for g, k0, q0, span in blocks:
            put = slice(at, at + span * STRETCH)
            if level == 0:
                gl_ref[rs(q0, span), :] = sums[put]
            else:
                gl_ref[rs(q0, span), :] += sums[put]
            at += span * STRETCH
        pairs = (
            [(2 * g, 2, 2 * g, 2) for g in range(stretches // 2)]
            if level == 0
            else [(g * span, span, k0, max(span, 2)) for g, k0, q0, span in blocks]
        )
        for key, (z0, zspan, k0, kspan) in enumerate(pairs):
            qh, ql = zh[rs(z0, zspan)], zl[rs(z0, zspan)]
            kh, kl = xh_ref[own(k0, kspan)], xl_ref[own(k0, kspan)]
            if kspan == 2:
                r = dot_nt(qh, jnp.concatenate([kh, kl], 0))
                mixed[level, key] = r[:, :LANES] + r[:, LANES:] + dot_nt(ql, kh)
            else:
                mixed[level, key] = dot_nt(qh, kh) + dot_nt(qh, kl) + dot_nt(ql, kh)

    level = stretches.bit_length()
    keys = [key_open(info, level, j) for j in range(stretches)]
    queries = [query_open(info, level, stretches + j) for j in range(stretches)]
    whole = slice(0, rows)

    def state(h, l, w):
        wh, wl = split(w.T)
        wt = jnp.concatenate([wh, wl], 0)

        def one(j, cols):
            r = dot(wt, h[:, cols])
            rh[:, cols], rl[:, cols] = split(r[:n] + r[n:] + dot(wh, l[:, cols]))

        each_chunk(columns, one)

    def query_z(first):
        def one(j, cols):
            for a in range(stretches):
                zh[rs(a), cols], zl[rs(a), cols] = split(weighted(cw_ref, lam_ref, first + a, cols, level, j, heads))

        each_chunk(columns, one)

    if off == 0:
        query_z(stretches)
        state(zh, zl, scaled_rows(c_ref[rs(stretches, stretches), :], queries))
        middle_rows = scaled_rows(gather(xh_ref[whole], xl_ref[whole], rh, rl), keys)
        pw = split_rows(scaled_rows(b_ref[whole, :], keys))

        def one(j, cols):
            for a in range(0, stretches, 4):
                gx_ref[rs(a, 4), cols] += spread(pw[rs(a, 4)], rh, rl, cols)

        each_chunk(columns, one)
    else:
        state(xh_ref.at[whole], xl_ref.at[whole], scaled_rows(b_ref[whole, :], keys))
        query_z(off)
        middle_rows = scaled_rows(gather(zh[...], zl[...], rh, rl), queries)
        pw = split_rows(scaled_rows(c_ref[own(0, stretches), :], queries))

        def one(j, cols):
            for a in range(0, stretches, 4):
                g = spread(pw[rs(a, 4)], rh, rl, cols)
                ph[rs(a, 4), cols], pq[rs(a, 4), cols] = split(g * cw_ref[own(a, 4), cols])

        each_chunk(columns, one)
        gl_ref[...] += head_sums(ph[...], pq[...], ones, level, heads)

    def times(m, w):
        mh, ml = split(m)
        wh, wl = split(w)
        r = dot(mh, jnp.concatenate([wh, wl], 1))
        return r[:, :n] + r[:, n:] + dot(ml, wh)

    wide = 2 * STRETCH
    t = lax.broadcasted_iota(jnp.int32, (wide, wide), 0)
    s = lax.broadcasted_iota(jnp.int32, (wide, wide), 1)
    for g in range(stretches // 4):
        rows4 = rs(4 * g, 4)
        blocks = []
        for d in range(2):
            at = 2 * g + d
            own_pair = jnp.where((t >= s) & (t // STRETCH == s // STRETCH), mixed[0, at], 0.0)
            valid = open_product(info, off + 2 * at + 1, off + 2 * at + 1)
            low = jnp.concatenate([jnp.zeros((STRETCH, wide), F32), mixed[1, at] * valid], 0)
            blocks.append(own_pair + jnp.where(s < STRETCH, low, 0.0))
        q = [query_open(info, 2, off + 4 * g + 2 + a) for a in range(2)]
        k = [key_open(info, 2, off + 4 * g + a) for a in range(2)]
        m_two = scaled_rows(mixed[2, g], q)
        m_two = jnp.where(s < STRETCH, m_two * k[0], m_two * k[1])
        m = jnp.concatenate(
            [
                jnp.concatenate([blocks[0], jnp.zeros((wide, wide), F32)], 1),
                jnp.concatenate([m_two, blocks[1]], 1),
            ],
            0,
        )
        gc_ref[rows4, :] = times(m, b_ref[own(4 * g, 4), :])
        gb_ref[rows4, :] = times(m.T, c_ref[own(4 * g, 4), :])
    q = [query_open(info, 3, off + 4 + a) for a in range(4)]
    k = [key_open(info, 3, off + a) for a in range(4)]
    m = mixed[3, 0]
    gc_ref[rs(4, 4), :] += scaled_rows(times(m, scaled_rows(b_ref[own(0, 4), :], k)), q)
    gb_ref[rs(0, 4), :] += scaled_rows(times(m.T, scaled_rows(c_ref[own(4, 4), :], q)), k)
    if off == 0:
        gb_ref[...] += middle_rows
    else:
        gc_ref[...] += middle_rows


def local_levels(info, heads, held, b, c, part):
    xh, xl, cw, lam = held
    rows, columns = xh.shape[0] // 2, xh.shape[1]
    n = b.shape[1]
    stretches = rows // STRETCH
    three, wide = 3 * STRETCH, 2 * STRETCH
    return call(
        functools.partial(local_kernel, heads, part * stretches),
        f"local_levels_{part}",
        (info, b, c, lam, cw, xh, xl),
        [SMEM] + [VMEM] * 6,
        [((rows, columns), F32), ((rows, LANES), F32), ((rows, n), F32), ((rows, n), F32)],
        [VMEM] * 4,
        [
            pltpu.VMEM((stretches, STRETCH, three), BF16),
            pltpu.VMEM((stretches, STRETCH, three), BF16),
            pltpu.VMEM((stretches // 2, STRETCH, three), BF16),
            pltpu.VMEM((stretches // 2, STRETCH, three), BF16),
            pltpu.VMEM((stretches // 4, wide, 3 * wide), BF16),
            pltpu.VMEM((stretches // 4, wide, 3 * wide), BF16),
            pltpu.VMEM((1, 2 * wide, 6 * wide), BF16),
            pltpu.VMEM((1, 2 * wide, 6 * wide), BF16),
            pltpu.VMEM((rows, columns), BF16),
            pltpu.VMEM((rows, columns), BF16),
            pltpu.VMEM((rows, columns), BF16),
            pltpu.VMEM((rows, columns), BF16),
            pltpu.VMEM((n, columns), BF16),
            pltpu.VMEM((n, columns), BF16),
        ],
        16,
        9 * 10**9,
    )


def masks(info, stretches):
    prefix = [open_product(info, 0, i) for i in range(stretches)]
    suffix = [open_product(info, i + 1, stretches - 1) for i in range(stretches)]
    return prefix, suffix


def assemble(info, bit, pieces, out):
    size = pieces[0].shape[0]
    own = info[0] & ((1 << bit) - 1)
    own = own >> 1 if bit > 1 else own
    for k, piece in enumerate(pieces):
        at = (own ^ k) * size
        out[pl.ds(pl.multiple_of(at, size), size), :] = piece[...]


def level_sums(level, heads, p, cw, rh, rl, ph, pq, ones):
    rows, columns = cw.shape

    def one(j, cols):
        for a in range(0, rows // STRETCH, 4):
            g = spread(p[rs(a, 4)], rh, rl, cols)
            ph[rs(a, 4), cols], pq[rs(a, 4), cols] = split(g * cw[rs(a, 4), cols])

    each_chunk(columns, one)
    return head_sums(ph[...], pq[...], ones, level, heads)


def early_kernel(heads, level0, bits, top, known, info, *rest):
    others, rest = rest[:known], rest[known:]
    b_ref, c_ref, cw, xh, xl, gla, glb, gba, gbb, gca, gcb, *rest = rest
    zs, rest = rest[: 2 * len(bits)], rest[2 * len(bits) :]
    states = []
    for bit in bits:
        count = 1 << bit if bit <= 1 else 1 << (bit - 1)
        states.append(rest[:count])
        rest = rest[count:]
    low_ref, gl_ref, sel_ref, other_ref, pc, ph, pq, rh, rl, gbs, gcs, rf = rest
    rows, columns = xh.shape
    stretches = rows // STRETCH
    mid = stretches // 2
    me = info[0]
    prefix, suffix = masks(info, stretches)
    uppers = [((me >> bit) & 1) == 1 for bit in bits]
    gates = [gate_of(info, others, bit) for bit in bits]
    ones = head_columns(columns)
    for dst, (one, two) in ((gl_ref, (gla, glb)), (gbs, (gba, gbb)), (gcs, (gca, gcb))):
        dst[rs(0, mid), :], dst[rs(mid, mid), :] = one[...], two[...]
    pc[...] = split_rows(scaled_rows(c_ref[...], prefix))
    low_ref[...] = jnp.zeros_like(low_ref)
    for k, bit in enumerate(bits):
        assemble(info, bit, states[k], rf)

        @pl.when(jnp.logical_not(uppers[k]))
        def _():
            low_ref[...] += rf[...] * gates[k]

        @pl.when(uppers[k])
        def _():
            rh[...], rl[...] = split(rf[...] * gates[k])
            gcs[...] += scaled_rows(gather(zs[2 * k][...], zs[2 * k + 1][...], rh, rl), prefix)
            gl_ref[...] += level_sums(level0 + bit, heads, pc, cw, rh, rl, ph, pq, ones)

    below = (1 << top) - 1

    @pl.when((me & below) != below)
    def _():
        rh[...], rl[...] = split(low_ref[...])
        gbs[...] += scaled_rows(gather(xh[...], xl[...], rh, rl), suffix)

    last = ((me >> top) & 1) == 1

    @pl.when(last)
    def _():
        sel_ref[...], other_ref[...] = gcs[...], gbs[...]

    @pl.when(jnp.logical_not(last))
    def _():
        sel_ref[...], other_ref[...] = gbs[...], gcs[...]


def early_states(info, others, heads, held, b, c, sums, zs, states, bits, top, level0):
    xh, xl, cw, lam = held
    rows, columns = xh.shape
    n = b.shape[1]
    inputs = (info, *others, b, c, cw, xh, xl, *sums, *zs, *(p for q in states for p in q))
    wide = pltpu.VMEM((rows, columns), BF16)
    state = pltpu.VMEM((n, columns), BF16)
    own = pltpu.VMEM((rows, n), F32)
    return call(
        functools.partial(early_kernel, heads, level0, bits, top, len(others)),
        "apply_" + "_".join(str(level0 + b) for b in bits),
        inputs,
        [SMEM] * (1 + len(others)) + [VMEM] * (len(inputs) - 1 - len(others)),
        [((n, columns), F32), ((rows, LANES), F32), ((rows, n), F32), ((rows, n), F32)],
        [VMEM] * 4,
        [pltpu.VMEM((rows, 2 * n), BF16), wide, wide, state, state, own, own, pltpu.VMEM((n, columns), F32)],
        16,
        len(bits) * 2 * 10**9,
    )


def last_rows_kernel(top, head_bits, known, info, *rest):
    others, rest = rest[:known], rest[known:]
    xh, xl, zh, zl, sel_ref, other_ref, *rest = rest
    pieces, (away_ref, kept_ref, state_ref, rh, rl) = rest[:-5], rest[-5:]
    prefix, suffix = masks(info, xh.shape[0] // STRETCH)
    upper = ((info[0] >> top) & 1) == 1
    assemble(info, top, pieces, state_ref)
    state_ref[...] = state_ref[...] * gate_of(info, others, top)
    rh[...], rl[...] = split(state_ref[...])
    size = away_ref.shape[0] // 2

    def put(v, at):
        away_ref[at], kept_ref[at] = head_halves(info, v, 0, head_bits) if head_bits else (v, v)

    put(other_ref[...], slice(size, 2 * size))

    @pl.when(upper)
    def _():
        put(sel_ref[...] + scaled_rows(gather(zh[...], zl[...], rh, rl), prefix), slice(0, size))

    @pl.when(jnp.logical_not(upper))
    def _():
        put(sel_ref[...] + scaled_rows(gather(xh[...], xl[...], rh, rl), suffix), slice(0, size))


def last_rows(info, others, held, z, pieces, sel, other, top, level, head_bits):
    xh, xl = held[:2]
    rows, columns = xh.shape
    n = sel.shape[1]
    inputs = (info, *others, xh, xl, *z, sel, other, *pieces)
    halves = ((rows if head_bits else 2 * rows, n), F32)
    return call(
        functools.partial(last_rows_kernel, top, head_bits, len(others)),
        f"rows_{level}",
        inputs,
        [SMEM] * (1 + len(others)) + [VMEM] * (len(inputs) - 1 - len(others)),
        [halves, halves, ((n, columns), F32)],
        [VMEM] * 3,
        [pltpu.VMEM((n, columns), BF16)] * 2,
        12,
        10**9,
    )


def last_kernel(heads, half, top, level, info, rate_ref, b_ref, c_ref, cw, gxa, gxb, r_ref, low_ref, gl_in,
                gx_hbm, gl_ref, pw, ph, pq, rh, rl, of, gls, sems):
    rows, columns = cw.shape
    stretches = rows // STRETCH
    mid = stretches // 2
    me = info[0]
    base = (me * rows - half).astype(F32)
    prefix, suffix = masks(info, stretches)
    upper = ((me >> top) & 1) == 1
    gls[...] = gl_in[...]

    @pl.when(upper)
    def _():
        rh[...], rl[...] = split(r_ref[...])
        pw[...] = split_rows(scaled_rows(c_ref[...], prefix))
        gls[...] += level_sums(level, heads, pw, cw, rh, rl, ph, pq, head_columns(columns))

    pieces = sems.shape[0]
    per = stretches // pieces

    def copy(k):
        at = pl.ds(k * per * STRETCH, per * STRETCH)
        return pltpu.make_async_copy(of.at[at], gx_hbm.at[at], sems.at[k])

    def finish(any_low):
        if any_low:
            rh[...], rl[...] = split(low_ref[...] + r_ref[...] * jnp.where(upper, 0.0, 1.0))
            pw[...] = split_rows(scaled_rows(b_ref[...], suffix))
        for k in range(pieces):

            def one(j, cols):
                inner, outer = decays(rate_ref, j, base, 1.0, stretches)
                extra = spread(pw[rs(k * per, per)], rh, rl, cols) if any_low else None
                for i in range(k * per, (k + 1) * per):
                    g = gxa[rs(i), cols] if i < mid else gxb[rs(i - mid), cols]
                    if any_low:
                        g = g + extra[rs(i - k * per)]
                    of[rs(i), cols] = g * (inner * outer[i : i + 1, :])

            each_chunk(columns, one)
            copy(k).start()

    below = (2 << top) - 1

    @pl.when((me & below) == below)
    def _():
        finish(False)

    @pl.when((me & below) != below)
    def _():
        finish(True)

    lanes = gl_ref.shape[0]
    gl_ref[...] = gls[...].T[:lanes] * level_scales((lanes, 1), 0, heads)
    for k in range(pieces):
        copy(k).wait()


def last_state(info, rate, held, b, c, gx, state, low, gl, half, top, level, lanes):
    cw = held[2]
    rows, columns = cw.shape
    n = b.shape[1]
    wide = pltpu.VMEM((rows, columns), BF16)
    held_state = pltpu.VMEM((n, columns), BF16)
    return call(
        functools.partial(last_kernel, rate.shape[0], half, top, level),
        f"apply_{level}",
        (info, rate, b, c, cw, *gx, state, low, gl),
        [SMEM] * 2 + [VMEM] * 8,
        [((rows, columns), F32), ((lanes, rows), F32)],
        [ANY, VMEM],
        [
            pltpu.VMEM((rows, 2 * n), BF16),
            wide,
            wide,
            held_state,
            held_state,
            pltpu.VMEM((rows, columns), F32),
            pltpu.VMEM((rows, LANES), F32),
            pltpu.SemaphoreType.DMA((4,)),
        ],
        20,
        3 * 10**9,
    )


def after(x, *others):
    return lax.optimization_barrier((x, *others))[0]


class Swap:
    def __init__(self, info, others, outs, bit):
        self.info, self.others, self.bit, self.phase = info, others, bit, 0
        self.plan = list(reversed(range(bit)))
        if bit == 0:
            self.came = partner(outs[0], 1)
        else:
            self.away, self.kept = outs
            self.came = partner(self.away, 1 << (bit - 1))

    @property
    def done(self):
        return self.phase > self.bit

    def step(self):
        k, bit = self.phase, self.bit
        self.phase += 1
        if k < bit:
            next_bit = self.plan[k + 1] if k < bit - 1 else None
            whole = next_bit == 0
            outs = sum_step(
                self.info, self.others, self.kept, self.came, bit, k == 0, None if whole else next_bit
            )
            if whole:
                self.kept = outs[0]
                self.came = partner(outs[0], 1)
            elif next_bit is None:
                self.came = partner(outs[0], 1 << bit)
            else:
                self.away, self.kept = outs
                self.came = partner(self.away, 1 << next_bit)
            return outs[0]
        own = self.came
        apart = [j for j in range(1, 1 << bit) if bit <= 1 or j % 2 == 0]
        self.pieces = [own] + [partner(own, j) for j in apart]
        return own


def local(inputs, cotangent, b_proj, c_proj, decay_rate, level_weight, starts):
    rows = inputs.shape[0]
    heads = decay_rate.shape[0]
    stretches = rows // STRETCH
    seq_count = lax.axis_size("seq")
    seq_bits = seq_count.bit_length() - 1
    head_bits = lax.axis_size("head").bit_length() - 1
    half = seq_count * rows // 2
    me = lax.axis_index("seq").astype(jnp.int32)
    lanes = level_weight.shape[0] * heads
    level0 = stretches.bit_length()
    top = seq_bits - 1
    others = [partner(starts, k) for k in range(1, 1 << top)]
    info = jnp.concatenate([me.reshape(1), lax.axis_index("head").astype(jnp.int32).reshape(1), starts])
    raw_lam = level_weight.reshape(lanes, rows)
    if lanes < LANES:
        raw_lam = jnp.pad(raw_lam, ((0, LANES - lanes), (0, 0)))

    order = [*range(1, seq_bits), 0]
    b = order[0]
    *held, bv, cv, zh, zl, away, kept = first_state(
        info, decay_rate, inputs, cotangent, b_proj, c_proj, raw_lam, level0 + b, b, half
    )
    swaps = {b: Swap(info, others, (away, kept), b)}
    zs = {b: (zh, zl)}
    tied = after(info, kept)
    for b in order[1:]:
        zh, zl, *outs = send_state(tied, heads, held, bv, cv, level0 + b, b)
        zs[b] = (zh, zl)
        swaps[b] = Swap(info, others, outs, b)
        tied = after(info, outs[-1])
    waits = [swaps[b].step() for b in range(1, seq_bits)]
    part0 = local_levels(after(tied, *waits), heads, held, bv, cv, 0)
    for b in range(1, seq_bits):
        swaps[b].info = after(info, part0[3])
        swaps[b].came = after(swaps[b].came, part0[3])
    waits = [swaps[b].step() for b in range(1, seq_bits)]
    part1 = local_levels(after(info, part0[3], *waits), heads, held, bv, cv, 1)
    waits = []
    for b in range(seq_bits):
        swaps[b].info = after(info, part1[3])
        swaps[b].came = after(swaps[b].came, part1[3])
        while not swaps[b].done:
            waits.append(swaps[b].step())
    sums = [p[k] for k in range(1, 4) for p in (part0, part1)]
    early = tuple(range(top))
    low, gl, sel, other = early_states(
        after(info, *waits), others, heads, held, bv, cv, sums, [z for b in early for z in zs[b]],
        [swaps[b].pieces for b in early], early, top, level0,
    )
    level = level0 + top
    pieces = [after(p, other) for p in swaps[top].pieces]
    away, kept, state = last_rows(info, others, held, zs[top], pieces, sel, other, top, level, head_bits)
    came = head_partner(away, 0)
    for bit in range(1, head_bits):
        away, kept = head_step(info, kept, came, bit, head_bits)
        came = head_partner(away, bit)
    grad_x, gl = last_state(
        after(info, kept), decay_rate, held, bv, cv, (part0[0], part1[0]), state, low, gl, half, top, level, lanes
    )
    both = after(kept, gl) + after(came, gl)
    size = both.shape[0] // 2
    sel, other = both[:size], both[size:]
    upper = ((after(me, gl) >> top) & 1) == 1
    return (grad_x, jnp.where(upper, other, sel), jnp.where(upper, sel, other), gl.reshape(level_weight.shape))


def solution(mesh):
    return jax.shard_map(
        local,
        mesh=mesh,
        in_specs=(
            P("seq", "head"),
            P("seq", "head"),
            P("seq", None),
            P("seq", None),
            P("head"),
            P(None, "head", "seq"),
            P("seq"),
        ),
        out_specs=(
            P("seq", "head"),
            P(("seq", "head"), None),
            P(("seq", "head"), None),
            P(None, "head", "seq"),
        ),
        check_vma=False,
    )
```

```python
import functools

import jax
import jax.numpy as jnp
from jax import lax
from jax.experimental import pallas as pl
from jax.experimental.pallas import tpu as pltpu
from jax.sharding import PartitionSpec as P

KERNELS = True
STRETCH = 64
WIDTH = 64
CHUNK = 256
LANES = 128
F32 = jnp.float32
BF16 = jnp.bfloat16


def partner(x, apart):
    return lax.ppermute(x, "seq", [(i, i ^ apart) for i in range(lax.axis_size("seq"))])


def split(a):
    hi = a.astype(BF16)
    return hi, (a - hi.astype(F32)).astype(BF16)


def dot(a, b):
    return lax.dot_general(a, b, (((1,), (0,)), ((), ())), preferred_element_type=F32)


def dot_nt(a, b):
    return lax.dot_general(a, b, (((1,), (1,)), ((), ())), preferred_element_type=F32)


def open_product(info, first, last):
    r = jnp.float32(1.0)
    for k in range(first, last + 1):
        r = r * (1 - info[2 + k]).astype(F32)
    return r


def query_open(info, level, i):
    mid = ((i >> level) << level) + (1 << (level - 1))
    return open_product(info, mid, i)


def key_open(info, level, j):
    mid = ((j >> level) << level) + (1 << (level - 1))
    return open_product(info, j + 1, mid - 1)


def clean_flags(info, others):
    count = others[0].shape[0] if others else 0
    flags = [None]
    for ref in others:
        worst = ref[0]
        for k in range(1, count):
            worst = worst + ref[k]
        flags.append(jnp.where(worst == 0, 1.0, 0.0))
    worst = info[2]
    for k in range(1, count):
        worst = worst + info[2 + k]
    flags[0] = jnp.where(worst == 0, 1.0, 0.0)
    return flags


def gate_of(info, others, bit, apart=0):
    if bit == 0:
        return jnp.float32(1.0)
    flags = clean_flags(info, others)
    me = info[0]
    device = me ^ apart
    upper = ((device >> bit) & 1) == 1
    gate = jnp.float32(1.0)
    for k in range(len(flags)):
        if k != apart and (k ^ apart) < (1 << bit):
            one = me ^ k
            between = jnp.where(upper, one < device, one > device)
            gate = gate * jnp.where(between, flags[k], 1.0)
    return gate


def scaled_rows(a, factors):
    return jnp.concatenate(
        [a[STRETCH * k : STRETCH * (k + 1)] * f for k, f in enumerate(factors)], 0
    )


def decays(rate_ref, chunk, base, sign, stretches):
    per = CHUNK // WIDTH
    lane_head = lax.broadcasted_iota(jnp.int32, (1, CHUNK), 1) >> (WIDTH.bit_length() - 1)
    row = jnp.zeros((1, CHUNK), F32)
    for k in range(per):
        row = jnp.where(lane_head == k, rate_ref[chunk * per + k], row)
    within = lax.broadcasted_iota(jnp.int32, (STRETCH, CHUNK), 0).astype(F32)
    across = lax.broadcasted_iota(jnp.int32, (stretches, CHUNK), 0).astype(F32) * STRETCH + base
    return jnp.exp(sign * within * row), jnp.exp(sign * across * row)


def decayed(a, tables, i, first=0):
    inner, outer = tables
    return a[STRETCH * i : STRETCH * (i + 1), :] * (inner * outer[first + i : first + i + 1, :])


def weight_of(lam, level, chunk, heads):
    per = LANES // WIDTH
    lane = lax.broadcasted_iota(jnp.int32, (1, LANES), 1) >> (WIDTH.bit_length() - 1)
    out = []
    for piece in range(CHUNK // LANES):
        at = lane + (level * heads + piece * per + chunk * (CHUNK // WIDTH))
        out.append(jnp.take_along_axis(lam, jnp.broadcast_to(at, lam.shape), axis=1))
    return jnp.concatenate(out, 1)


def head_columns(columns):
    d = lax.broadcasted_iota(jnp.int32, (columns, LANES), 0) >> (WIDTH.bit_length() - 1)
    lane = lax.broadcasted_iota(jnp.int32, (columns, LANES), 1)
    return jnp.where(lane == d, 1.0, 0.0).astype(BF16)


def head_sums(ph, pl_, e, level, heads):
    r = jnp.concatenate(
        [dot(ph[k : k + 128], e) + dot(pl_[k : k + 128], e) for k in range(0, ph.shape[0], 128)], 0
    )
    return pltpu.roll(r, level * heads, 1) if level else r


def rs(a, count=1):
    return slice(STRETCH * a, STRETCH * (a + count))


def each_chunk(columns, body):
    for j in range(columns // CHUNK):
        body(j, slice(j * CHUNK, (j + 1) * CHUNK))


def weighted(cw_ref, lam_ref, i, cols, level, j, heads):
    return cw_ref[rs(i), cols] * weight_of(lam_ref[rs(i), :], level, j, heads)


VMEM = pl.BlockSpec(memory_space=pltpu.VMEM)
SMEM = pl.BlockSpec(memory_space=pltpu.SMEM)
ANY = pl.BlockSpec(memory_space=pl.ANY)


def call(kernel, name, inputs, specs, outs, out_specs, scratch, mib, flops, aliases=None):
    return pl.pallas_call(
        kernel,
        out_shape=[jax.ShapeDtypeStruct(*o) for o in outs],
        in_specs=specs,
        out_specs=out_specs,
        scratch_shapes=scratch,
        input_output_aliases=aliases or {},
        compiler_params=pltpu.CompilerParams(vmem_limit_bytes=mib * 2**20),
        cost_estimate=pl.CostEstimate(flops=flops, bytes_accessed=2**20, transcendentals=0),
        name=name,
    )(*inputs)


def level_scales(shape, axis, heads):
    shift = heads.bit_length() - 1
    level = (lax.broadcasted_iota(jnp.int32, shape, axis) >> shift).astype(F32)
    return jnp.exp2(-0.5 * level - 0.5 * (STRETCH.bit_length() - 1))


def state_of(info, level, bit, heads, b_ref, c_ref, lam_ref, cw_ref, xh, xl, outs, wt, zh, zl):
    rows, columns = xh.shape
    n = b_ref.shape[1]
    stretches = rows // STRETCH
    upper = ((info[0] >> bit) & 1) == 1

    def put(w):
        t = w.T
        wt[:n], wt[n:] = split(t)

    def product(h, l):
        def one(j, cols):
            r = dot(wt[...], h[:, cols])
            v = r[:n] + r[n:] + dot(wt[:n], l[:, cols])
            if bit == 0:
                outs[0][:, cols] = v
            else:
                high = ((info[0] >> (bit - 1)) & 1) == 1
                low_half, high_half = v[: n // 2], v[n // 2 :]
                outs[0][:, cols] = jnp.where(high, low_half, high_half)
                outs[1][:, cols] = jnp.where(high, high_half, low_half)

        each_chunk(columns, one)

    @pl.when(upper)
    def _():
        put(scaled_rows(c_ref[...], [open_product(info, 0, i) for i in range(stretches)]))

        def one(j, cols):
            for i in range(stretches):
                zh[rs(i), cols], zl[rs(i), cols] = split(weighted(cw_ref, lam_ref, i, cols, level, j, heads))

        each_chunk(columns, one)
        product(zh, zl)

    @pl.when(jnp.logical_not(upper))
    def _():
        put(scaled_rows(b_ref[...], [open_product(info, i + 1, stretches - 1) for i in range(stretches)]))
        product(xh, xl)


def state_outs(n, columns, bit):
    return [((n, columns), F32)] if bit == 0 else [((n // 2, columns), F32)] * 2


def first_kernel(heads, level, bit, half, info, rate_ref, x_hbm, cot_hbm, b_hbm, c_hbm, raw_hbm,
                 xh, xl, cw, lam_out, b_ref, c_ref, *rest):
    zh, zl, *rest = rest
    outs, (xf, raw, wt, sems, more) = rest[:-5], rest[-5:]
    rows, columns = xh.shape
    stretches = rows // STRETCH
    pieces = sems.shape[1]
    size = rows // pieces
    base = (info[0] * rows - half).astype(F32)
    small = [
        pltpu.make_async_copy(src, dst, more.at[k])
        for k, (src, dst) in enumerate(((raw_hbm, raw), (b_hbm, b_ref), (c_hbm, c_ref)))
    ]
    small[0].start()
    copies = []
    for k in range(pieces):
        at = pl.ds(k * size, size)
        copies.append(pltpu.make_async_copy(x_hbm.at[at], xf.at[at], sems.at[0, k]))
        copies[-1].start()
    small[1].start()
    small[2].start()
    for k in range(pieces):
        at = pl.ds(k * size, size)
        copies.append(pltpu.make_async_copy(cot_hbm.at[at], cw.at[at], sems.at[1, k]))
        copies[-1].start()
    small[0].wait()
    lam_out[...] = (raw[...] * level_scales((raw.shape[0], 1), 0, heads)).T
    per = size // STRETCH
    for k in range(pieces):
        copies[k].wait()

        def one(j, cols):
            inner, outer = decays(rate_ref, j, base, 1.0, stretches)
            for i in range(k * per, (k + 1) * per):
                xh[rs(i), cols], xl[rs(i), cols] = split(xf[rs(i), cols] * (inner * outer[i : i + 1, :]))

        each_chunk(columns, one)
    for k in range(pieces):
        copies[pieces + k].wait()

        def one(j, cols):
            inner, outer = decays(rate_ref, j, base, -1.0, stretches)
            for i in range(k * per, (k + 1) * per):
                cw[rs(i), cols] = cw[rs(i), cols] * (inner * outer[i : i + 1, :])

        each_chunk(columns, one)
    small[1].wait()
    small[2].wait()
    state_of(info, level, bit, heads, b_ref, c_ref, lam_out, cw, xh, xl, outs, wt, zh, zl)


def first_state(info, rate, x, cot, b, c, raw, level, bit, half):
    rows, columns = x.shape
    n = b.shape[1]
    wide = ((rows, columns), BF16)
    outs = [wide, wide, ((rows, columns), F32), ((rows, LANES), F32), (b.shape, F32), (c.shape, F32), wide, wide]
    outs += state_outs(n, columns, bit)
    return call(
        functools.partial(first_kernel, rate.shape[0], level, bit, half),
        f"send_level_{level}",
        (info, rate, x, cot, b, c, raw),
        [SMEM, SMEM, ANY, ANY, ANY, ANY, ANY],
        outs,
        [VMEM] * len(outs),
        [
            pltpu.VMEM((rows, columns), F32),
            pltpu.VMEM(raw.shape, F32),
            pltpu.VMEM((2 * n, rows), BF16),
            pltpu.SemaphoreType.DMA((2, 4)),
            pltpu.SemaphoreType.DMA((3,)),
        ],
        37,
        10**9,
    )


def send_kernel(heads, level, bit, info, b_ref, c_ref, lam_ref, cw, xh, xl, *rest):
    zh, zl, *rest = rest
    state_of(info, level, bit, heads, b_ref, c_ref, lam_ref, cw, xh, xl, rest[:-1], rest[-1], zh, zl)


def send_state(info, heads, held, b, c, level, bit):
    xh, xl, cw, lam = held
    rows, columns = xh.shape
    n = b.shape[1]
    outs = [((rows, columns), BF16)] * 2 + state_outs(n, columns, bit)
    return call(
        functools.partial(send_kernel, heads, level, bit),
        f"send_level_{level}",
        (info, b, c, lam, cw, xh, xl),
        [SMEM] + [VMEM] * 6,
        outs,
        [VMEM] * len(outs),
        [pltpu.VMEM((2 * n, rows), BF16)],
        8,
        10**9,
    )


def sum_kernel(bit, gated, next_bit, info, *rest):
    others = rest[:gated]
    kept, came, *outs = rest[gated:]
    if gated:
        v = kept[...] * gate_of(info, others, bit) + came[...] * gate_of(info, others, bit, 1 << (bit - 1))
    else:
        v = kept[...] + came[...]
    if next_bit is None:
        outs[0][...] = v
    else:
        half = v.shape[0] // 2
        high = ((info[0] >> next_bit) & 1) == 1
        outs[0][...] = jnp.where(high, v[:half], v[half:])
        outs[1][...] = jnp.where(high, v[half:], v[:half])


def sum_step(info, others, kept, came, bit, gated, next_bit):
    rows, columns = kept.shape
    outs = [((rows, columns), F32)] if next_bit is None else [((rows // 2, columns), F32)] * 2
    others = list(others) if gated else []
    return call(
        functools.partial(sum_kernel, bit, len(others), next_bit),
        f"sum_{bit}_{rows}",
        (info, *others, kept, came),
        [SMEM] * (1 + len(others)) + [VMEM] * 2,
        outs,
        [VMEM] * len(outs),
        [],
        4,
        10**7,
    )


def head_halves(info, v, bit, bits):
    size = v.shape[0] >> (bits - bit)
    step = v.shape[0] // size
    mine = (info[1] >> bit) & 1
    away = [v[size * k : size * (k + 1)] for k in range(step)]
    pick = lambda side: jnp.concatenate(
        [jnp.where(side == 1, away[k + 1], away[k]) for k in range(0, step, 2)], 0
    )
    return pick(1 - mine), pick(mine)


def head_sum_kernel(bit, bits, info, kept, came, away_ref, kept_ref):
    size = away_ref.shape[0] // 2
    for k in range(2):
        part = slice(2 * size * k, 2 * size * (k + 1))
        at = slice(size * k, size * (k + 1))
        away_ref[at], kept_ref[at] = head_halves(info, kept[part] + came[part], bit, bits)


def head_step(info, kept, came, bit, bits):
    rows, n = kept.shape
    return call(
        functools.partial(head_sum_kernel, bit, bits),
        f"heads_{bit}",
        (info, kept, came),
        [SMEM, VMEM, VMEM],
        [((rows // 2, n), F32)] * 2,
        [VMEM] * 2,
        [],
        4,
        10**7,
    )


def head_partner(x, bit):
    return lax.ppermute(x, "head", [(i, i ^ (1 << bit)) for i in range(lax.axis_size("head"))])


def split_rows(a):
    return jnp.concatenate(split(a), 1)


def spread(p, rh, rl, cols):
    n = rh.shape[0]
    h, l = rh[:, cols], rl[:, cols]
    return dot(p, jnp.concatenate([h, h], 0)) + dot(p[:, :n], l)


def gather(h, l, rh, rl):
    n = rh.shape[0]
    both = dot_nt(h, jnp.concatenate([rh[...], rl[...]], 0))
    return both[:, :n] + both[:, n:] + dot_nt(l, rh[...])


def local_kernel(heads, off, info, b_ref, c_ref, lam_ref, cw_ref, xh_ref, xl_ref,
                 gx_ref, gl_ref, gb_ref, gc_ref,
                 p0, p0t, p1, p1t, p2, p2t, s3, s3t, ph, pq, zh, zl, rh, rl):
    rows, columns = gx_ref.shape
    n = b_ref.shape[1]
    stretches = rows // STRETCH

    def own(a, count=1):
        return rs(off + a, count)

    def level_rows(level):
        span = 1 << (level - 1)
        return [(g, g << level, (g << level) + span, span) for g in range(stretches >> level)]

    def product(q, k):
        qh, ql = split(q)
        kh, kl = split(k)
        return dot_nt(jnp.concatenate([qh, ql], 1), jnp.concatenate([kh, kh], 1)) + dot_nt(qh, kl)

    for i in range(stretches):
        cq, bk = c_ref[own(i), :], b_ref[own(i), :]
        t = lax.broadcasted_iota(jnp.int32, (STRETCH, STRETCH), 0)
        s = lax.broadcasted_iota(jnp.int32, (STRETCH, STRETCH), 1)
        h, l = split(jnp.where(t >= s, product(cq, bk), 0.0))
        p0[i] = jnp.concatenate([h, l, h], 1)
        h, l = split(jnp.where(s >= t, product(bk, cq), 0.0))
        p0t[i] = jnp.concatenate([h, l, h], 1)
    scores = {1: (p1, p1t), 2: (p2, p2t), 3: (s3, s3t)}
    for level, ps in scores.items():
        for g, k0, q0, span in level_rows(level):
            cq = scaled_rows(c_ref[own(q0, span), :], [query_open(info, level, off + q0 + a) for a in range(span)])
            bk = scaled_rows(b_ref[own(k0, span), :], [key_open(info, level, off + k0 + a) for a in range(span)])
            for ref, (u, w) in zip(ps, ((cq, bk), (bk, cq))):
                h, l = split(product(u, w))
                ref[g] = jnp.concatenate([h, l, h], 1)

    def apply3(p, h, l):
        return dot(p, jnp.concatenate([h, h, l], 0))

    ones = head_columns(columns)
    mixed = {}
    for level in range(4):
        blocks = [(i, i, i, 1) for i in range(stretches)] if level == 0 else level_rows(level)
        ps, pst = (p0, p0t) if level == 0 else scores[level]

        def one(j, cols):
            at = 0
            for g, k0, q0, span in blocks:
                put = slice(at, at + span * STRETCH)
                for a in range(span):
                    z = weighted(cw_ref, lam_ref, off + q0 + a, cols, level, j, heads)
                    here = slice(at + a * STRETCH, at + (a + 1) * STRETCH)
                    zh[here, cols], zl[here, cols] = split(z)
                y = apply3(ps[g], xh_ref[own(k0, span), cols], xl_ref[own(k0, span), cols])
                ph[put, cols], pq[put, cols] = split(y * cw_ref[own(q0, span), cols])
                gx = apply3(pst[g], zh[put, cols], zl[put, cols])
                if level == 0:
                    gx_ref[rs(k0, span), cols] = gx
                else:
                    gx_ref[rs(k0, span), cols] += gx
                at += span * STRETCH

        each_chunk(columns, one)
        at = 0
        used = len(blocks) * blocks[0][3] * STRETCH
        sums = head_sums(ph[:used], pq[:used], ones, level, heads)
        for g, k0, q0, span in blocks:
            put = slice(at, at + span * STRETCH)
            if level == 0:
                gl_ref[rs(q0, span), :] = sums[put]
            else:
                gl_ref[rs(q0, span), :] += sums[put]
            at += span * STRETCH
        pairs = (
            [(2 * g, 2, 2 * g, 2) for g in range(stretches // 2)]
            if level == 0
            else [(g * span, span, k0, max(span, 2)) for g, k0, q0, span in blocks]
        )
        for key, (z0, zspan, k0, kspan) in enumerate(pairs):
            qh, ql = zh[rs(z0, zspan)], zl[rs(z0, zspan)]
            kh, kl = xh_ref[own(k0, kspan)], xl_ref[own(k0, kspan)]
            if kspan == 2:
                r = dot_nt(qh, jnp.concatenate([kh, kl], 0))
                mixed[level, key] = r[:, :LANES] + r[:, LANES:] + dot_nt(ql, kh)
            else:
                mixed[level, key] = dot_nt(qh, kh) + dot_nt(qh, kl) + dot_nt(ql, kh)

    level = stretches.bit_length()
    keys = [key_open(info, level, j) for j in range(stretches)]
    queries = [query_open(info, level, stretches + j) for j in range(stretches)]
    whole = slice(0, rows)

    def state(h, l, w):
        wh, wl = split(w.T)
        wt = jnp.concatenate([wh, wl], 0)

        def one(j, cols):
            r = dot(wt, h[:, cols])
            rh[:, cols], rl[:, cols] = split(r[:n] + r[n:] + dot(wh, l[:, cols]))

        each_chunk(columns, one)

    def query_z(first):
        def one(j, cols):
            for a in range(stretches):
                zh[rs(a), cols], zl[rs(a), cols] = split(weighted(cw_ref, lam_ref, first + a, cols, level, j, heads))

        each_chunk(columns, one)

    if off == 0:
        query_z(stretches)
        state(zh, zl, scaled_rows(c_ref[rs(stretches, stretches), :], queries))
        middle_rows = scaled_rows(gather(xh_ref[whole], xl_ref[whole], rh, rl), keys)
        pw = split_rows(scaled_rows(b_ref[whole, :], keys))

        def one(j, cols):
            for a in range(0, stretches, 4):
                gx_ref[rs(a, 4), cols] += spread(pw[rs(a, 4)], rh, rl, cols)

        each_chunk(columns, one)
    else:
        state(xh_ref.at[whole], xl_ref.at[whole], scaled_rows(b_ref[whole, :], keys))
        query_z(off)
        middle_rows = scaled_rows(gather(zh[...], zl[...], rh, rl), queries)
        pw = split_rows(scaled_rows(c_ref[own(0, stretches), :], queries))

        def one(j, cols):
            for a in range(0, stretches, 4):
                g = spread(pw[rs(a, 4)], rh, rl, cols)
                ph[rs(a, 4), cols], pq[rs(a, 4), cols] = split(g * cw_ref[own(a, 4), cols])

        each_chunk(columns, one)
        gl_ref[...] += head_sums(ph[...], pq[...], ones, level, heads)

    def times(m, w):
        mh, ml = split(m)
        wh, wl = split(w)
        r = dot(mh, jnp.concatenate([wh, wl], 1))
        return r[:, :n] + r[:, n:] + dot(ml, wh)

    wide = 2 * STRETCH
    t = lax.broadcasted_iota(jnp.int32, (wide, wide), 0)
    s = lax.broadcasted_iota(jnp.int32, (wide, wide), 1)
    for g in range(stretches // 4):
        rows4 = rs(4 * g, 4)
        blocks = []
        for d in range(2):
            at = 2 * g + d
            own_pair = jnp.where((t >= s) & ((t < STRETCH) == (s < STRETCH)), mixed[0, at], 0.0)
            valid = open_product(info, off + 2 * at + 1, off + 2 * at + 1)
            low = jnp.concatenate([jnp.zeros((STRETCH, wide), F32), mixed[1, at] * valid], 0)
            blocks.append(own_pair + jnp.where(s < STRETCH, low, 0.0))
        q = [query_open(info, 2, off + 4 * g + 2 + a) for a in range(2)]
        k = [key_open(info, 2, off + 4 * g + a) for a in range(2)]
        m_two = scaled_rows(mixed[2, g], q)
        m_two = jnp.where(s < STRETCH, m_two * k[0], m_two * k[1])
        m = jnp.concatenate(
            [
                jnp.concatenate([blocks[0], jnp.zeros((wide, wide), F32)], 1),
                jnp.concatenate([m_two, blocks[1]], 1),
            ],
            0,
        )
        gc_ref[rows4, :] = times(m, b_ref[own(4 * g, 4), :])
        gb_ref[rows4, :] = times(m.T, c_ref[own(4 * g, 4), :])
    q = [query_open(info, 3, off + 4 + a) for a in range(4)]
    k = [key_open(info, 3, off + a) for a in range(4)]
    m = mixed[3, 0]
    gc_ref[rs(4, 4), :] += scaled_rows(times(m, scaled_rows(b_ref[own(0, 4), :], k)), q)
    gb_ref[rs(0, 4), :] += scaled_rows(times(m.T, scaled_rows(c_ref[own(4, 4), :], q)), k)
    if off == 0:
        gb_ref[...] += middle_rows
    else:
        gc_ref[...] += middle_rows


def local_levels(info, heads, held, b, c, part):
    xh, xl, cw, lam = held
    rows, columns = xh.shape[0] // 2, xh.shape[1]
    n = b.shape[1]
    stretches = rows // STRETCH
    three, wide = 3 * STRETCH, 2 * STRETCH
    return call(
        functools.partial(local_kernel, heads, part * stretches),
        f"local_levels_{part}",
        (info, b, c, lam, cw, xh, xl),
        [SMEM] + [VMEM] * 6,
        [((rows, columns), F32), ((rows, LANES), F32), ((rows, n), F32), ((rows, n), F32)],
        [VMEM] * 4,
        [
            pltpu.VMEM((stretches, STRETCH, three), BF16),
            pltpu.VMEM((stretches, STRETCH, three), BF16),
            pltpu.VMEM((stretches // 2, STRETCH, three), BF16),
            pltpu.VMEM((stretches // 2, STRETCH, three), BF16),
            pltpu.VMEM((stretches // 4, wide, 3 * wide), BF16),
            pltpu.VMEM((stretches // 4, wide, 3 * wide), BF16),
            pltpu.VMEM((1, 2 * wide, 6 * wide), BF16),
            pltpu.VMEM((1, 2 * wide, 6 * wide), BF16),
            pltpu.VMEM((rows, columns), BF16),
            pltpu.VMEM((rows, columns), BF16),
            pltpu.VMEM((rows, columns), BF16),
            pltpu.VMEM((rows, columns), BF16),
            pltpu.VMEM((n, columns), BF16),
            pltpu.VMEM((n, columns), BF16),
        ],
        16,
        9 * 10**9,
    )


def masks(info, stretches):
    prefix = [open_product(info, 0, i) for i in range(stretches)]
    suffix = [open_product(info, i + 1, stretches - 1) for i in range(stretches)]
    return prefix, suffix


def assemble(info, bit, pieces, out):
    size = pieces[0].shape[0]
    own = info[0] & ((1 << bit) - 1)
    own = own >> 1 if bit > 1 else own
    for k, piece in enumerate(pieces):
        at = (own ^ k) * size
        out[pl.ds(pl.multiple_of(at, size), size), :] = piece[...]


def level_sums(level, heads, p, cw, rh, rl, ph, pq, ones):
    rows, columns = cw.shape

    def one(j, cols):
        for a in range(0, rows // STRETCH, 4):
            g = spread(p[rs(a, 4)], rh, rl, cols)
            ph[rs(a, 4), cols], pq[rs(a, 4), cols] = split(g * cw[rs(a, 4), cols])

    each_chunk(columns, one)
    return head_sums(ph[...], pq[...], ones, level, heads)


def early_kernel(heads, level0, bits, top, known, info, *rest):
    others, rest = rest[:known], rest[known:]
    b_ref, c_ref, cw, xh, xl, gla, glb, gba, gbb, gca, gcb, *rest = rest
    zs, rest = rest[: 2 * len(bits)], rest[2 * len(bits) :]
    states = []
    for bit in bits:
        count = 1 << bit if bit <= 1 else 1 << (bit - 1)
        states.append(rest[:count])
        rest = rest[count:]
    low_ref, gl_ref, sel_ref, other_ref, pc, ph, pq, rh, rl, gbs, gcs, rf = rest
    rows, columns = xh.shape
    stretches = rows // STRETCH
    mid = stretches // 2
    me = info[0]
    prefix, suffix = masks(info, stretches)
    uppers = [((me >> bit) & 1) == 1 for bit in bits]
    gates = [gate_of(info, others, bit) for bit in bits]
    ones = head_columns(columns)
    for dst, (one, two) in ((gl_ref, (gla, glb)), (gbs, (gba, gbb)), (gcs, (gca, gcb))):
        dst[rs(0, mid), :], dst[rs(mid, mid), :] = one[...], two[...]
    pc[...] = split_rows(scaled_rows(c_ref[...], prefix))
    low_ref[...] = jnp.zeros_like(low_ref)
    for k, bit in enumerate(bits):
        assemble(info, bit, states[k], rf)

        @pl.when(jnp.logical_not(uppers[k]))
        def _():
            low_ref[...] += rf[...] * gates[k]

        @pl.when(uppers[k])
        def _():
            rh[...], rl[...] = split(rf[...] * gates[k])
            gcs[...] += scaled_rows(gather(zs[2 * k][...], zs[2 * k + 1][...], rh, rl), prefix)
            gl_ref[...] += level_sums(level0 + bit, heads, pc, cw, rh, rl, ph, pq, ones)

    below = (1 << top) - 1

    @pl.when((me & below) != below)
    def _():
        rh[...], rl[...] = split(low_ref[...])
        gbs[...] += scaled_rows(gather(xh[...], xl[...], rh, rl), suffix)

    last = ((me >> top) & 1) == 1

    @pl.when(last)
    def _():
        sel_ref[...], other_ref[...] = gcs[...], gbs[...]

    @pl.when(jnp.logical_not(last))
    def _():
        sel_ref[...], other_ref[...] = gbs[...], gcs[...]


def early_states(info, others, heads, held, b, c, sums, zs, states, bits, top, level0):
    xh, xl, cw, lam = held
    rows, columns = xh.shape
    n = b.shape[1]
    inputs = (info, *others, b, c, cw, xh, xl, *sums, *zs, *(p for q in states for p in q))
    wide = pltpu.VMEM((rows, columns), BF16)
    state = pltpu.VMEM((n, columns), BF16)
    own = pltpu.VMEM((rows, n), F32)
    return call(
        functools.partial(early_kernel, heads, level0, bits, top, len(others)),
        "apply_" + "_".join(str(level0 + b) for b in bits),
        inputs,
        [SMEM] * (1 + len(others)) + [VMEM] * (len(inputs) - 1 - len(others)),
        [((n, columns), F32), ((rows, LANES), F32), ((rows, n), F32), ((rows, n), F32)],
        [VMEM] * 4,
        [pltpu.VMEM((rows, 2 * n), BF16), wide, wide, state, state, own, own, pltpu.VMEM((n, columns), F32)],
        16,
        len(bits) * 2 * 10**9,
    )


def last_rows_kernel(top, head_bits, known, info, *rest):
    others, rest = rest[:known], rest[known:]
    xh, xl, zh, zl, sel_ref, other_ref, *rest = rest
    pieces, (away_ref, kept_ref, state_ref, rh, rl) = rest[:-5], rest[-5:]
    prefix, suffix = masks(info, xh.shape[0] // STRETCH)
    upper = ((info[0] >> top) & 1) == 1
    assemble(info, top, pieces, state_ref)
    state_ref[...] = state_ref[...] * gate_of(info, others, top)
    rh[...], rl[...] = split(state_ref[...])
    size = away_ref.shape[0] // 2

    def put(v, at):
        away_ref[at], kept_ref[at] = head_halves(info, v, 0, head_bits) if head_bits else (v, v)

    put(other_ref[...], slice(size, 2 * size))

    @pl.when(upper)
    def _():
        put(sel_ref[...] + scaled_rows(gather(zh[...], zl[...], rh, rl), prefix), slice(0, size))

    @pl.when(jnp.logical_not(upper))
    def _():
        put(sel_ref[...] + scaled_rows(gather(xh[...], xl[...], rh, rl), suffix), slice(0, size))


def last_rows(info, others, held, z, pieces, sel, other, top, level, head_bits):
    xh, xl = held[:2]
    rows, columns = xh.shape
    n = sel.shape[1]
    inputs = (info, *others, xh, xl, *z, sel, other, *pieces)
    halves = ((rows if head_bits else 2 * rows, n), F32)
    return call(
        functools.partial(last_rows_kernel, top, head_bits, len(others)),
        f"rows_{level}",
        inputs,
        [SMEM] * (1 + len(others)) + [VMEM] * (len(inputs) - 1 - len(others)),
        [halves, halves, ((n, columns), F32)],
        [VMEM] * 3,
        [pltpu.VMEM((n, columns), BF16)] * 2,
        12,
        10**9,
    )


def last_kernel(heads, half, top, level, info, rate_ref, b_ref, c_ref, cw, gxa, gxb, r_ref, low_ref, gl_in,
                gx_hbm, gl_ref, pw, ph, pq, rh, rl, of, gls, sems):
    rows, columns = cw.shape
    stretches = rows // STRETCH
    mid = stretches // 2
    me = info[0]
    base = (me * rows - half).astype(F32)
    prefix, suffix = masks(info, stretches)
    upper = ((me >> top) & 1) == 1
    gls[...] = gl_in[...]

    @pl.when(upper)
    def _():
        rh[...], rl[...] = split(r_ref[...])
        pw[...] = split_rows(scaled_rows(c_ref[...], prefix))
        gls[...] += level_sums(level, heads, pw, cw, rh, rl, ph, pq, head_columns(columns))

    pieces = sems.shape[0]
    per = stretches // pieces

    def copy(k):
        at = pl.ds(k * per * STRETCH, per * STRETCH)
        return pltpu.make_async_copy(of.at[at], gx_hbm.at[at], sems.at[k])

    def finish(any_low):
        if any_low:
            rh[...], rl[...] = split(low_ref[...] + r_ref[...] * jnp.where(upper, 0.0, 1.0))
            pw[...] = split_rows(scaled_rows(b_ref[...], suffix))
        for k in range(pieces):

            def one(j, cols):
                inner, outer = decays(rate_ref, j, base, 1.0, stretches)
                extra = spread(pw[rs(k * per, per)], rh, rl, cols) if any_low else None
                for i in range(k * per, (k + 1) * per):
                    g = gxa[rs(i), cols] if i < mid else gxb[rs(i - mid), cols]
                    if any_low:
                        g = g + extra[rs(i - k * per)]
                    of[rs(i), cols] = g * (inner * outer[i : i + 1, :])

            each_chunk(columns, one)
            copy(k).start()

    below = (2 << top) - 1

    @pl.when((me & below) == below)
    def _():
        finish(False)

    @pl.when((me & below) != below)
    def _():
        finish(True)

    lanes = gl_ref.shape[0]
    gl_ref[...] = gls[...].T[:lanes] * level_scales((lanes, 1), 0, heads)
    for k in range(pieces):
        copy(k).wait()


def last_state(info, rate, held, b, c, gx, state, low, gl, half, top, level, lanes):
    cw = held[2]
    rows, columns = cw.shape
    n = b.shape[1]
    wide = pltpu.VMEM((rows, columns), BF16)
    held_state = pltpu.VMEM((n, columns), BF16)
    return call(
        functools.partial(last_kernel, rate.shape[0], half, top, level),
        f"apply_{level}",
        (info, rate, b, c, cw, *gx, state, low, gl),
        [SMEM] * 2 + [VMEM] * 8,
        [((rows, columns), F32), ((lanes, rows), F32)],
        [ANY, VMEM],
        [
            pltpu.VMEM((rows, 2 * n), BF16),
            wide,
            wide,
            held_state,
            held_state,
            pltpu.VMEM((rows, columns), F32),
            pltpu.VMEM((rows, LANES), F32),
            pltpu.SemaphoreType.DMA((4,)),
        ],
        20,
        3 * 10**9,
    )


def after(x, *others):
    return lax.optimization_barrier((x, *others))[0]


class Swap:
    def __init__(self, info, others, outs, bit):
        self.info, self.others, self.bit, self.phase = info, others, bit, 0
        self.plan = list(reversed(range(bit)))
        if bit == 0:
            self.came = partner(outs[0], 1)
        else:
            self.away, self.kept = outs
            self.came = partner(self.away, 1 << (bit - 1))

    @property
    def done(self):
        return self.phase > self.bit

    def step(self):
        k, bit = self.phase, self.bit
        self.phase += 1
        if k < bit:
            next_bit = self.plan[k + 1] if k < bit - 1 else None
            whole = next_bit == 0
            outs = sum_step(
                self.info, self.others, self.kept, self.came, bit, k == 0, None if whole else next_bit
            )
            if whole:
                self.kept = outs[0]
                self.came = partner(outs[0], 1)
            elif next_bit is None:
                self.came = partner(outs[0], 1 << bit)
            else:
                self.away, self.kept = outs
                self.came = partner(self.away, 1 << next_bit)
            return outs[0]
        own = self.came
        apart = [j for j in range(1, 1 << bit) if bit <= 1 or j % 2 == 0]
        self.pieces = [own] + [partner(own, j) for j in apart]
        return own


def local(inputs, cotangent, b_proj, c_proj, decay_rate, level_weight, starts):
    rows = inputs.shape[0]
    heads = decay_rate.shape[0]
    stretches = rows // STRETCH
    seq_count = lax.axis_size("seq")
    seq_bits = seq_count.bit_length() - 1
    head_bits = lax.axis_size("head").bit_length() - 1
    half = seq_count * rows // 2
    me = lax.axis_index("seq").astype(jnp.int32)
    lanes = level_weight.shape[0] * heads
    level0 = stretches.bit_length()
    top = seq_bits - 1
    others = [partner(starts, k) for k in range(1, 1 << top)]
    info = jnp.concatenate([me.reshape(1), lax.axis_index("head").astype(jnp.int32).reshape(1), starts])
    raw_lam = level_weight.reshape(lanes, rows)
    if lanes < LANES:
        raw_lam = jnp.pad(raw_lam, ((0, LANES - lanes), (0, 0)))

    order = [*range(1, seq_bits), 0]
    b = order[0]
    *held, bv, cv, zh, zl, away, kept = first_state(
        info, decay_rate, inputs, cotangent, b_proj, c_proj, raw_lam, level0 + b, b, half
    )
    swaps = {b: Swap(info, others, (away, kept), b)}
    zs = {b: (zh, zl)}
    tied = after(info, kept)
    for b in order[1:]:
        zh, zl, *outs = send_state(tied, heads, held, bv, cv, level0 + b, b)
        zs[b] = (zh, zl)
        swaps[b] = Swap(info, others, outs, b)
        tied = after(info, outs[-1])
    waits = [swaps[b].step() for b in range(1, seq_bits)]
    part0 = local_levels(after(tied, *waits), heads, held, bv, cv, 0)
    for b in range(1, seq_bits):
        swaps[b].info = after(info, part0[3])
        swaps[b].came = after(swaps[b].came, part0[3])
    waits = [swaps[b].step() for b in range(1, seq_bits)]
    part1 = local_levels(after(info, part0[3], *waits), heads, held, bv, cv, 1)
    waits = []
    for b in range(seq_bits):
        swaps[b].info = after(info, part1[3])
        swaps[b].came = after(swaps[b].came, part1[3])
        while not swaps[b].done:
            waits.append(swaps[b].step())
    sums = [p[k] for k in range(1, 4) for p in (part0, part1)]
    early = tuple(range(top))
    low, gl, sel, other = early_states(
        after(info, *waits), others, heads, held, bv, cv, sums, [z for b in early for z in zs[b]],
        [swaps[b].pieces for b in early], early, top, level0,
    )
    level = level0 + top
    pieces = [after(p, other) for p in swaps[top].pieces]
    away, kept, state = last_rows(info, others, held, zs[top], pieces, sel, other, top, level, head_bits)
    came = head_partner(away, 0)
    for bit in range(1, head_bits):
        away, kept = head_step(info, kept, came, bit, head_bits)
        came = head_partner(away, bit)
    grad_x, gl = last_state(
        after(info, kept), decay_rate, held, bv, cv, (part0[0], part1[0]), state, low, gl, half, top, level, lanes
    )
    both = after(kept, gl) + after(came, gl)
    size = both.shape[0] // 2
    sel, other = both[:size], both[size:]
    upper = ((after(me, gl) >> top) & 1) == 1
    return (grad_x, jnp.where(upper, other, sel), jnp.where(upper, sel, other), gl.reshape(level_weight.shape))


def solution(mesh):
    return jax.shard_map(
        local,
        mesh=mesh,
        in_specs=(
            P("seq", "head"),
            P("seq", "head"),
            P("seq", None),
            P("seq", None),
            P("head"),
            P(None, "head", "seq"),
            P("seq"),
        ),
        out_specs=(
            P("seq", "head"),
            P(("seq", "head"), None),
            P(("seq", "head"), None),
            P(None, "head", "seq"),
        ),
        check_vma=False,
    )
```

```python
import functools

import jax
import jax.numpy as jnp
from jax import lax
from jax.experimental import pallas as pl
from jax.experimental.pallas import tpu as pltpu
from jax.sharding import PartitionSpec as P

KERNELS = True
STRETCH = 64
WIDTH = 64
CHUNK = 256
LANES = 128
CODE_ROWS = 8
F32 = jnp.float32
BF16 = jnp.bfloat16


def partner(x, apart):
    return lax.ppermute(x, "seq", [(i, i ^ apart) for i in range(lax.axis_size("seq"))])


def split(a):
    hi = a.astype(BF16)
    return hi, (a - hi.astype(F32)).astype(BF16)


def dot(a, b):
    return lax.dot_general(a, b, (((1,), (0,)), ((), ())), preferred_element_type=F32)


def dot_nt(a, b):
    return lax.dot_general(a, b, (((1,), (1,)), ((), ())), preferred_element_type=F32)


def open_product(info, first, last):
    r = jnp.float32(1.0)
    for k in range(first, last + 1):
        r = r * (1 - info[2 + k]).astype(F32)
    return r


def query_open(info, level, i):
    mid = ((i >> level) << level) + (1 << (level - 1))
    return open_product(info, mid, i)


def key_open(info, level, j):
    mid = ((j >> level) << level) + (1 << (level - 1))
    return open_product(info, j + 1, mid - 1)


def clean_flags(info, others):
    count = others[0].shape[0] if others else 0
    flags = [None]
    for ref in others:
        worst = ref[0]
        for k in range(1, count):
            worst = worst + ref[k]
        flags.append(jnp.where(worst == 0, 1.0, 0.0))
    worst = info[2]
    for k in range(1, count):
        worst = worst + info[2 + k]
    flags[0] = jnp.where(worst == 0, 1.0, 0.0)
    return flags


def gate_of(info, others, bit, apart=0):
    if bit == 0:
        return jnp.float32(1.0)
    flags = others if isinstance(others, list) else clean_flags(info, others)
    me = info[0]
    device = me ^ apart
    upper = ((device >> bit) & 1) == 1
    gate = jnp.float32(1.0)
    for k in range(len(flags)):
        if k != apart and (k ^ apart) < (1 << bit):
            one = me ^ k
            between = jnp.where(upper, one < device, one > device)
            gate = gate * jnp.where(between, flags[k], 1.0)
    return gate


def pair_code(info, others):
    flags = clean_flags(info, others)
    return flags[0] + 2.0 * flags[1]


def quad_flags(info, others, came):
    code = jnp.max(came[came.shape[0] - CODE_ROWS :, :])
    second = jnp.where(code >= 2.0, 1.0, 0.0)
    return clean_flags(info, others) + [code - 2.0 * second, second]


def scaled_rows(a, factors):
    return jnp.concatenate(
        [a[STRETCH * k : STRETCH * (k + 1)] * f for k, f in enumerate(factors)], 0
    )


def decays(rate_ref, chunk, base, sign, stretches):
    per = CHUNK // WIDTH
    lane_head = lax.broadcasted_iota(jnp.int32, (1, CHUNK), 1) >> (WIDTH.bit_length() - 1)
    row = jnp.zeros((1, CHUNK), F32)
    for k in range(per):
        row = jnp.where(lane_head == k, rate_ref[chunk * per + k], row)
    within = lax.broadcasted_iota(jnp.int32, (STRETCH, CHUNK), 0).astype(F32)
    across = lax.broadcasted_iota(jnp.int32, (stretches, CHUNK), 0).astype(F32) * STRETCH + base
    return jnp.exp(sign * within * row), jnp.exp(sign * across * row)


def decayed(a, tables, i, first=0):
    inner, outer = tables
    return a[STRETCH * i : STRETCH * (i + 1), :] * (inner * outer[first + i : first + i + 1, :])


def weight_of(lam, level, chunk, heads):
    per = LANES // WIDTH
    lane = lax.broadcasted_iota(jnp.int32, (1, LANES), 1) >> (WIDTH.bit_length() - 1)
    out = []
    for piece in range(CHUNK // LANES):
        at = lane + (level * heads + piece * per + chunk * (CHUNK // WIDTH))
        out.append(jnp.take_along_axis(lam, jnp.broadcast_to(at, lam.shape), axis=1))
    return jnp.concatenate(out, 1)


def head_columns(columns):
    d = lax.broadcasted_iota(jnp.int32, (columns, LANES), 0) >> (WIDTH.bit_length() - 1)
    lane = lax.broadcasted_iota(jnp.int32, (columns, LANES), 1)
    return jnp.where(lane == d, 1.0, 0.0).astype(BF16)


def head_sums(ph, pl_, e, level, heads):
    r = jnp.concatenate(
        [dot(ph[k : k + 128], e) + dot(pl_[k : k + 128], e) for k in range(0, ph.shape[0], 128)], 0
    )
    return pltpu.roll(r, level * heads, 1) if level else r


def rs(a, count=1):
    return slice(STRETCH * a, STRETCH * (a + count))


def each_chunk(columns, body):
    for j in range(columns // CHUNK):
        body(j, slice(j * CHUNK, (j + 1) * CHUNK))


def weighted(cw_ref, lam_ref, i, cols, level, j, heads):
    return cw_ref[rs(i), cols] * weight_of(lam_ref[rs(i), :], level, j, heads)


VMEM = pl.BlockSpec(memory_space=pltpu.VMEM)
SMEM = pl.BlockSpec(memory_space=pltpu.SMEM)
ANY = pl.BlockSpec(memory_space=pl.ANY)


def call(kernel, name, inputs, specs, outs, out_specs, scratch, mib, flops, aliases=None):
    return pl.pallas_call(
        kernel,
        out_shape=[jax.ShapeDtypeStruct(*o) for o in outs],
        in_specs=specs,
        out_specs=out_specs,
        scratch_shapes=scratch,
        input_output_aliases=aliases or {},
        compiler_params=pltpu.CompilerParams(vmem_limit_bytes=mib * 2**20),
        cost_estimate=pl.CostEstimate(flops=flops, bytes_accessed=2**20, transcendentals=0),
        name=name,
    )(*inputs)


def level_scales(shape, axis, heads):
    shift = heads.bit_length() - 1
    level = (lax.broadcasted_iota(jnp.int32, shape, axis) >> shift).astype(F32)
    return jnp.exp2(-0.5 * level - 0.5 * (STRETCH.bit_length() - 1))


def state_of(info, level, bit, heads, b_ref, c_ref, lam_ref, cw_ref, xh, xl, outs, wt, zh, zl):
    rows, columns = xh.shape
    n = b_ref.shape[1]
    stretches = rows // STRETCH
    upper = ((info[0] >> bit) & 1) == 1

    def put(w):
        t = w.T
        wt[:n], wt[n:] = split(t)

    def product(h, l):
        def one(j, cols):
            r = dot(wt[...], h[:, cols])
            v = r[:n] + r[n:] + dot(wt[:n], l[:, cols])
            if bit == 0:
                outs[0][:, cols] = v
            else:
                high = ((info[0] >> (bit - 1)) & 1) == 1
                low_half, high_half = v[: n // 2], v[n // 2 :]
                outs[0][: n // 2, cols] = jnp.where(high, low_half, high_half)
                outs[1][:, cols] = jnp.where(high, high_half, low_half)

        each_chunk(columns, one)

    @pl.when(upper)
    def _():
        put(scaled_rows(c_ref[...], [open_product(info, 0, i) for i in range(stretches)]))

        def one(j, cols):
            for i in range(stretches):
                zh[rs(i), cols], zl[rs(i), cols] = split(weighted(cw_ref, lam_ref, i, cols, level, j, heads))

        each_chunk(columns, one)
        product(zh, zl)

    @pl.when(jnp.logical_not(upper))
    def _():
        put(scaled_rows(b_ref[...], [open_product(info, i + 1, stretches - 1) for i in range(stretches)]))
        product(xh, xl)


def state_outs(n, columns, bit):
    return [((n, columns), F32)] if bit == 0 else [((n // 2, columns), F32)] * 2


def first_kernel(heads, level, bit, half, info, rate_ref, x_hbm, cot_hbm, b_hbm, c_hbm, raw_hbm,
                 xh, xl, cw, lam_out, b_ref, c_ref, *rest):
    zh, zl, *rest = rest
    outs, (xf, raw, wt, sems, more) = rest[:-5], rest[-5:]
    rows, columns = xh.shape
    stretches = rows // STRETCH
    pieces = sems.shape[1]
    size = rows // pieces
    base = (info[0] * rows - half).astype(F32)
    small = [
        pltpu.make_async_copy(src, dst, more.at[k])
        for k, (src, dst) in enumerate(((raw_hbm, raw), (b_hbm, b_ref), (c_hbm, c_ref)))
    ]
    small[0].start()
    copies = []
    for k in range(pieces):
        at = pl.ds(k * size, size)
        copies.append(pltpu.make_async_copy(x_hbm.at[at], xf.at[at], sems.at[0, k]))
        copies[-1].start()
    small[1].start()
    small[2].start()
    for k in range(pieces):
        at = pl.ds(k * size, size)
        copies.append(pltpu.make_async_copy(cot_hbm.at[at], cw.at[at], sems.at[1, k]))
        copies[-1].start()
    small[0].wait()
    lam_out[...] = (raw[...] * level_scales((raw.shape[0], 1), 0, heads)).T
    per = size // STRETCH
    for k in range(pieces):
        copies[k].wait()

        def one(j, cols):
            inner, outer = decays(rate_ref, j, base, 1.0, stretches)
            for i in range(k * per, (k + 1) * per):
                xh[rs(i), cols], xl[rs(i), cols] = split(xf[rs(i), cols] * (inner * outer[i : i + 1, :]))

        each_chunk(columns, one)
    for k in range(pieces):
        copies[pieces + k].wait()

        def one(j, cols):
            inner, outer = decays(rate_ref, j, base, -1.0, stretches)
            for i in range(k * per, (k + 1) * per):
                cw[rs(i), cols] = cw[rs(i), cols] * (inner * outer[i : i + 1, :])

        each_chunk(columns, one)
    small[1].wait()
    small[2].wait()
    state_of(info, level, bit, heads, b_ref, c_ref, lam_out, cw, xh, xl, outs, wt, zh, zl)


def first_state(info, rate, x, cot, b, c, raw, level, bit, half):
    rows, columns = x.shape
    n = b.shape[1]
    wide = ((rows, columns), BF16)
    outs = [wide, wide, ((rows, columns), F32), ((rows, LANES), F32), (b.shape, F32), (c.shape, F32), wide, wide]
    outs += state_outs(n, columns, bit)
    return call(
        functools.partial(first_kernel, rate.shape[0], level, bit, half),
        f"send_level_{level}",
        (info, rate, x, cot, b, c, raw),
        [SMEM, SMEM, ANY, ANY, ANY, ANY, ANY],
        outs,
        [VMEM] * len(outs),
        [
            pltpu.VMEM((rows, columns), F32),
            pltpu.VMEM(raw.shape, F32),
            pltpu.VMEM((2 * n, rows), BF16),
            pltpu.SemaphoreType.DMA((2, 4)),
            pltpu.SemaphoreType.DMA((3,)),
        ],
        37,
        10**9,
    )


def send_kernel(heads, level, bit, known, info, *rest):
    others, rest = tuple(rest[:known]), rest[known:]
    b_ref, c_ref, lam_ref, cw, xh, xl, zh, zl, *rest = rest
    if known:
        away, half = rest[0], b_ref.shape[1] // 2
        away[half:, :] = jnp.full((CODE_ROWS, away.shape[1]), pair_code(info, others), F32)
    state_of(info, level, bit, heads, b_ref, c_ref, lam_ref, cw, xh, xl, rest[:-1], rest[-1], zh, zl)


def send_state(info, heads, held, b, c, level, bit, others=()):
    xh, xl, cw, lam = held
    rows, columns = xh.shape
    n = b.shape[1]
    outs = [((rows, columns), BF16)] * 2 + state_outs(n, columns, bit)
    if others:
        outs[2] = ((n // 2 + CODE_ROWS, columns), F32)
    return call(
        functools.partial(send_kernel, heads, level, bit, len(others)),
        f"send_level_{level}",
        (info, *others, b, c, lam, cw, xh, xl),
        [SMEM] * (1 + len(others)) + [VMEM] * 6,
        outs,
        [VMEM] * len(outs),
        [pltpu.VMEM((2 * n, rows), BF16)],
        8,
        10**9,
    )


def sum_kernel(bit, gated, next_bit, info, *rest):
    others = tuple(rest[:gated])
    kept, came, *outs = rest[gated:]
    if came.shape[0] > kept.shape[0]:
        flags = quad_flags(info, others, came)
        gate = gate_of(info, flags, bit)
        outs.pop()[0] = gate
        v = kept[...] * gate + came[: kept.shape[0], :] * gate_of(info, flags, bit, 1 << (bit - 1))
    elif gated:
        v = kept[...] * gate_of(info, others, bit) + came[...] * gate_of(info, others, bit, 1 << (bit - 1))
    else:
        v = kept[...] + came[...]
    if next_bit is None:
        outs[0][...] = v
    else:
        half = v.shape[0] // 2
        high = ((info[0] >> next_bit) & 1) == 1
        outs[0][...] = jnp.where(high, v[:half], v[half:])
        outs[1][...] = jnp.where(high, v[half:], v[:half])


def sum_step(info, others, kept, came, bit, gated, next_bit):
    rows, columns = kept.shape
    outs = [((rows, columns), F32)] if next_bit is None else [((rows // 2, columns), F32)] * 2
    others = list(others) if gated else []
    out_specs = [VMEM] * len(outs)
    if came.shape[0] > rows:
        outs = outs + [((1,), F32)]
        out_specs = out_specs + [SMEM]
    return call(
        functools.partial(sum_kernel, bit, len(others), next_bit),
        f"sum_{bit}_{rows}",
        (info, *others, kept, came),
        [SMEM] * (1 + len(others)) + [VMEM] * 2,
        outs,
        out_specs,
        [],
        4,
        10**7,
    )


def head_halves(info, v, bit, bits):
    size = v.shape[0] >> (bits - bit)
    step = v.shape[0] // size
    mine = (info[1] >> bit) & 1
    away = [v[size * k : size * (k + 1)] for k in range(step)]
    pick = lambda side: jnp.concatenate(
        [jnp.where(side == 1, away[k + 1], away[k]) for k in range(0, step, 2)], 0
    )
    return pick(1 - mine), pick(mine)


def head_sum_kernel(bit, bits, info, kept, came, away_ref, kept_ref):
    size = away_ref.shape[0] // 2
    for k in range(2):
        part = slice(2 * size * k, 2 * size * (k + 1))
        at = slice(size * k, size * (k + 1))
        away_ref[at], kept_ref[at] = head_halves(info, kept[part] + came[part], bit, bits)


def head_step(info, kept, came, bit, bits):
    rows, n = kept.shape
    return call(
        functools.partial(head_sum_kernel, bit, bits),
        f"heads_{bit}",
        (info, kept, came),
        [SMEM, VMEM, VMEM],
        [((rows // 2, n), F32)] * 2,
        [VMEM] * 2,
        [],
        4,
        10**7,
    )


def head_partner(x, bit):
    return lax.ppermute(x, "head", [(i, i ^ (1 << bit)) for i in range(lax.axis_size("head"))])


def split_rows(a):
    return jnp.concatenate(split(a), 1)


def spread(p, rh, rl, cols):
    n = rh.shape[0]
    h, l = rh[:, cols], rl[:, cols]
    return dot(p, jnp.concatenate([h, h], 0)) + dot(p[:, :n], l)


def gather(h, l, rh, rl):
    n = rh.shape[0]
    both = dot_nt(h, jnp.concatenate([rh[...], rl[...]], 0))
    return both[:, :n] + both[:, n:] + dot_nt(l, rh[...])


def local_kernel(heads, off, info, b_ref, c_ref, lam_ref, cw_ref, xh_ref, xl_ref,
                 gx_ref, gl_ref, gb_ref, gc_ref,
                 p0, p0t, p1, p1t, p2, p2t, s3, s3t, ph, pq, zh, zl, rh, rl):
    rows, columns = gx_ref.shape
    n = b_ref.shape[1]
    stretches = rows // STRETCH

    def own(a, count=1):
        return rs(off + a, count)

    def level_rows(level):
        span = 1 << (level - 1)
        return [(g, g << level, (g << level) + span, span) for g in range(stretches >> level)]

    def product(q, k):
        qh, ql = split(q)
        kh, kl = split(k)
        return dot_nt(jnp.concatenate([qh, ql], 1), jnp.concatenate([kh, kh], 1)) + dot_nt(qh, kl)

    for i in range(stretches):
        cq, bk = c_ref[own(i), :], b_ref[own(i), :]
        t = lax.broadcasted_iota(jnp.int32, (STRETCH, STRETCH), 0)
        s = lax.broadcasted_iota(jnp.int32, (STRETCH, STRETCH), 1)
        h, l = split(jnp.where(t >= s, product(cq, bk), 0.0))
        p0[i] = jnp.concatenate([h, l, h], 1)
        h, l = split(jnp.where(s >= t, product(bk, cq), 0.0))
        p0t[i] = jnp.concatenate([h, l, h], 1)
    scores = {1: (p1, p1t), 2: (p2, p2t), 3: (s3, s3t)}
    for level, ps in scores.items():
        for g, k0, q0, span in level_rows(level):
            cq = scaled_rows(c_ref[own(q0, span), :], [query_open(info, level, off + q0 + a) for a in range(span)])
            bk = scaled_rows(b_ref[own(k0, span), :], [key_open(info, level, off + k0 + a) for a in range(span)])
            for ref, (u, w) in zip(ps, ((cq, bk), (bk, cq))):
                h, l = split(product(u, w))
                ref[g] = jnp.concatenate([h, l, h], 1)

    def apply3(p, h, l):
        return dot(p, jnp.concatenate([h, h, l], 0))

    ones = head_columns(columns)
    mixed = {}
    for level in range(4):
        blocks = [(i, i, i, 1) for i in range(stretches)] if level == 0 else level_rows(level)
        ps, pst = (p0, p0t) if level == 0 else scores[level]

        def one(j, cols):
            at = 0
            for g, k0, q0, span in blocks:
                put = slice(at, at + span * STRETCH)
                for a in range(span):
                    z = weighted(cw_ref, lam_ref, off + q0 + a, cols, level, j, heads)
                    here = slice(at + a * STRETCH, at + (a + 1) * STRETCH)
                    zh[here, cols], zl[here, cols] = split(z)
                y = apply3(ps[g], xh_ref[own(k0, span), cols], xl_ref[own(k0, span), cols])
                ph[put, cols], pq[put, cols] = split(y * cw_ref[own(q0, span), cols])
                gx = apply3(pst[g], zh[put, cols], zl[put, cols])
                if level == 0:
                    gx_ref[rs(k0, span), cols] = gx
                else:
                    gx_ref[rs(k0, span), cols] += gx
                at += span * STRETCH

        each_chunk(columns, one)
        at = 0
        used = len(blocks) * blocks[0][3] * STRETCH
        sums = head_sums(ph[:used], pq[:used], ones, level, heads)
        for g, k0, q0, span in blocks:
            put = slice(at, at + span * STRETCH)
            if level == 0:
                gl_ref[rs(q0, span), :] = sums[put]
            else:
                gl_ref[rs(q0, span), :] += sums[put]
            at += span * STRETCH
        pairs = (
            [(2 * g, 2, 2 * g, 2) for g in range(stretches // 2)]
            if level == 0
            else [(g * span, span, k0, max(span, 2)) for g, k0, q0, span in blocks]
        )
        for key, (z0, zspan, k0, kspan) in enumerate(pairs):
            qh, ql = zh[rs(z0, zspan)], zl[rs(z0, zspan)]
            kh, kl = xh_ref[own(k0, kspan)], xl_ref[own(k0, kspan)]
            if kspan == 2:
                r = dot_nt(qh, jnp.concatenate([kh, kl], 0))
                mixed[level, key] = r[:, :LANES] + r[:, LANES:] + dot_nt(ql, kh)
            else:
                mixed[level, key] = dot_nt(qh, kh) + dot_nt(qh, kl) + dot_nt(ql, kh)

    level = stretches.bit_length()
    keys = [key_open(info, level, j) for j in range(stretches)]
    queries = [query_open(info, level, stretches + j) for j in range(stretches)]
    whole = slice(0, rows)

    def state(h, l, w):
        wh, wl = split(w.T)
        wt = jnp.concatenate([wh, wl], 0)

        def one(j, cols):
            r = dot(wt, h[:, cols])
            rh[:, cols], rl[:, cols] = split(r[:n] + r[n:] + dot(wh, l[:, cols]))

        each_chunk(columns, one)

    def query_z(first):
        def one(j, cols):
            for a in range(stretches):
                zh[rs(a), cols], zl[rs(a), cols] = split(weighted(cw_ref, lam_ref, first + a, cols, level, j, heads))

        each_chunk(columns, one)

    if off == 0:
        query_z(stretches)
        state(zh, zl, scaled_rows(c_ref[rs(stretches, stretches), :], queries))
        middle_rows = scaled_rows(gather(xh_ref[whole], xl_ref[whole], rh, rl), keys)
        pw = split_rows(scaled_rows(b_ref[whole, :], keys))

        def one(j, cols):
            for a in range(0, stretches, 4):
                gx_ref[rs(a, 4), cols] += spread(pw[rs(a, 4)], rh, rl, cols)

        each_chunk(columns, one)
    else:
        state(xh_ref.at[whole], xl_ref.at[whole], scaled_rows(b_ref[whole, :], keys))
        query_z(off)
        middle_rows = scaled_rows(gather(zh[...], zl[...], rh, rl), queries)
        pw = split_rows(scaled_rows(c_ref[own(0, stretches), :], queries))

        def one(j, cols):
            for a in range(0, stretches, 4):
                g = spread(pw[rs(a, 4)], rh, rl, cols)
                ph[rs(a, 4), cols], pq[rs(a, 4), cols] = split(g * cw_ref[own(a, 4), cols])

        each_chunk(columns, one)
        gl_ref[...] += head_sums(ph[...], pq[...], ones, level, heads)

    def times(m, w):
        mh, ml = split(m)
        wh, wl = split(w)
        r = dot(mh, jnp.concatenate([wh, wl], 1))
        return r[:, :n] + r[:, n:] + dot(ml, wh)

    wide = 2 * STRETCH
    t = lax.broadcasted_iota(jnp.int32, (wide, wide), 0)
    s = lax.broadcasted_iota(jnp.int32, (wide, wide), 1)
    for g in range(stretches // 4):
        rows4 = rs(4 * g, 4)
        blocks = []
        for d in range(2):
            at = 2 * g + d
            own_pair = jnp.where((t >= s) & ((t < STRETCH) == (s < STRETCH)), mixed[0, at], 0.0)
            valid = open_product(info, off + 2 * at + 1, off + 2 * at + 1)
            low = jnp.concatenate([jnp.zeros((STRETCH, wide), F32), mixed[1, at] * valid], 0)
            blocks.append(own_pair + jnp.where(s < STRETCH, low, 0.0))
        q = [query_open(info, 2, off + 4 * g + 2 + a) for a in range(2)]
        k = [key_open(info, 2, off + 4 * g + a) for a in range(2)]
        m_two = scaled_rows(mixed[2, g], q)
        m_two = jnp.where(s < STRETCH, m_two * k[0], m_two * k[1])
        m = jnp.concatenate(
            [
                jnp.concatenate([blocks[0], jnp.zeros((wide, wide), F32)], 1),
                jnp.concatenate([m_two, blocks[1]], 1),
            ],
            0,
        )
        gc_ref[rows4, :] = times(m, b_ref[own(4 * g, 4), :])
        gb_ref[rows4, :] = times(m.T, c_ref[own(4 * g, 4), :])
    q = [query_open(info, 3, off + 4 + a) for a in range(4)]
    k = [key_open(info, 3, off + a) for a in range(4)]
    m = mixed[3, 0]
    gc_ref[rs(4, 4), :] += scaled_rows(times(m, scaled_rows(b_ref[own(0, 4), :], k)), q)
    gb_ref[rs(0, 4), :] += scaled_rows(times(m.T, scaled_rows(c_ref[own(4, 4), :], q)), k)
    if off == 0:
        gb_ref[...] += middle_rows
    else:
        gc_ref[...] += middle_rows


def local_levels(info, heads, held, b, c, part):
    xh, xl, cw, lam = held
    rows, columns = xh.shape[0] // 2, xh.shape[1]
    n = b.shape[1]
    stretches = rows // STRETCH
    three, wide = 3 * STRETCH, 2 * STRETCH
    return call(
        functools.partial(local_kernel, heads, part * stretches),
        f"local_levels_{part}",
        (info, b, c, lam, cw, xh, xl),
        [SMEM] + [VMEM] * 6,
        [((rows, columns), F32), ((rows, LANES), F32), ((rows, n), F32), ((rows, n), F32)],
        [VMEM] * 4,
        [
            pltpu.VMEM((stretches, STRETCH, three), BF16),
            pltpu.VMEM((stretches, STRETCH, three), BF16),
            pltpu.VMEM((stretches // 2, STRETCH, three), BF16),
            pltpu.VMEM((stretches // 2, STRETCH, three), BF16),
            pltpu.VMEM((stretches // 4, wide, 3 * wide), BF16),
            pltpu.VMEM((stretches // 4, wide, 3 * wide), BF16),
            pltpu.VMEM((1, 2 * wide, 6 * wide), BF16),
            pltpu.VMEM((1, 2 * wide, 6 * wide), BF16),
            pltpu.VMEM((rows, columns), BF16),
            pltpu.VMEM((rows, columns), BF16),
            pltpu.VMEM((rows, columns), BF16),
            pltpu.VMEM((rows, columns), BF16),
            pltpu.VMEM((n, columns), BF16),
            pltpu.VMEM((n, columns), BF16),
        ],
        16,
        9 * 10**9,
    )


def masks(info, stretches):
    prefix = [open_product(info, 0, i) for i in range(stretches)]
    suffix = [open_product(info, i + 1, stretches - 1) for i in range(stretches)]
    return prefix, suffix


def assemble(info, bit, pieces, out):
    size = pieces[0].shape[0]
    own = info[0] & ((1 << bit) - 1)
    own = own >> 1 if bit > 1 else own
    for k, piece in enumerate(pieces):
        at = (own ^ k) * size
        out[pl.ds(pl.multiple_of(at, size), size), :] = piece[...]


def level_sums(level, heads, p, cw, rh, rl, ph, pq, ones):
    rows, columns = cw.shape

    def one(j, cols):
        for a in range(0, rows // STRETCH, 4):
            g = spread(p[rs(a, 4)], rh, rl, cols)
            ph[rs(a, 4), cols], pq[rs(a, 4), cols] = split(g * cw[rs(a, 4), cols])

    each_chunk(columns, one)
    return head_sums(ph[...], pq[...], ones, level, heads)


def early_kernel(heads, level0, bits, top, known, info, *rest):
    others, rest = tuple(rest[:known]), rest[known:]
    b_ref, c_ref, cw, xh, xl, gla, glb, gba, gbb, gca, gcb, *rest = rest
    zs, rest = rest[: 2 * len(bits)], rest[2 * len(bits) :]
    states = []
    for bit in bits:
        count = 1 << bit if bit <= 1 else 1 << (bit - 1)
        states.append(rest[:count])
        rest = rest[count:]
    low_ref, gl_ref, sel_ref, other_ref, pc, ph, pq, rh, rl, gbs, gcs, rf = rest
    rows, columns = xh.shape
    stretches = rows // STRETCH
    mid = stretches // 2
    me = info[0]
    prefix, suffix = masks(info, stretches)
    uppers = [((me >> bit) & 1) == 1 for bit in bits]
    gates = [gate_of(info, others, bit) for bit in bits]
    ones = head_columns(columns)
    for dst, (one, two) in ((gl_ref, (gla, glb)), (gbs, (gba, gbb)), (gcs, (gca, gcb))):
        dst[rs(0, mid), :], dst[rs(mid, mid), :] = one[...], two[...]
    pc[...] = split_rows(scaled_rows(c_ref[...], prefix))
    low_ref[...] = jnp.zeros_like(low_ref)
    for k, bit in enumerate(bits):
        assemble(info, bit, states[k], rf)

        @pl.when(jnp.logical_not(uppers[k]))
        def _():
            low_ref[...] += rf[...] * gates[k]

        @pl.when(uppers[k])
        def _():
            rh[...], rl[...] = split(rf[...] * gates[k])
            gcs[...] += scaled_rows(gather(zs[2 * k][...], zs[2 * k + 1][...], rh, rl), prefix)
            gl_ref[...] += level_sums(level0 + bit, heads, pc, cw, rh, rl, ph, pq, ones)

    below = (1 << top) - 1

    @pl.when((me & below) != below)
    def _():
        rh[...], rl[...] = split(low_ref[...])
        gbs[...] += scaled_rows(gather(xh[...], xl[...], rh, rl), suffix)

    last = ((me >> top) & 1) == 1

    @pl.when(last)
    def _():
        sel_ref[...], other_ref[...] = gcs[...], gbs[...]

    @pl.when(jnp.logical_not(last))
    def _():
        sel_ref[...], other_ref[...] = gbs[...], gcs[...]


def early_states(info, others, heads, held, b, c, sums, zs, states, bits, top, level0):
    xh, xl, cw, lam = held
    rows, columns = xh.shape
    n = b.shape[1]
    inputs = (info, *others, b, c, cw, xh, xl, *sums, *zs, *(p for q in states for p in q))
    wide = pltpu.VMEM((rows, columns), BF16)
    state = pltpu.VMEM((n, columns), BF16)
    own = pltpu.VMEM((rows, n), F32)
    return call(
        functools.partial(early_kernel, heads, level0, bits, top, len(others)),
        "apply_" + "_".join(str(level0 + b) for b in bits),
        inputs,
        [SMEM] * (1 + len(others)) + [VMEM] * (len(inputs) - 1 - len(others)),
        [((n, columns), F32), ((rows, LANES), F32), ((rows, n), F32), ((rows, n), F32)],
        [VMEM] * 4,
        [pltpu.VMEM((rows, 2 * n), BF16), wide, wide, state, state, own, own, pltpu.VMEM((n, columns), F32)],
        16,
        len(bits) * 2 * 10**9,
    )


def last_rows_kernel(top, head_bits, known, info, *rest):
    others, rest = tuple(rest[:known]), rest[known:]
    xh, xl, zh, zl, sel_ref, other_ref, *rest = rest
    pieces, (away_ref, kept_ref, state_ref, rh, rl) = rest[:-5], rest[-5:]
    prefix, suffix = masks(info, xh.shape[0] // STRETCH)
    upper = ((info[0] >> top) & 1) == 1
    assemble(info, top, pieces, state_ref)
    gate = others[0][0] if others[0].shape[0] == 1 else gate_of(info, others, top)
    state_ref[...] = state_ref[...] * gate
    rh[...], rl[...] = split(state_ref[...])
    size = away_ref.shape[0] // 2

    def put(v, at):
        away_ref[at], kept_ref[at] = head_halves(info, v, 0, head_bits) if head_bits else (v, v)

    put(other_ref[...], slice(size, 2 * size))

    @pl.when(upper)
    def _():
        put(sel_ref[...] + scaled_rows(gather(zh[...], zl[...], rh, rl), prefix), slice(0, size))

    @pl.when(jnp.logical_not(upper))
    def _():
        put(sel_ref[...] + scaled_rows(gather(xh[...], xl[...], rh, rl), suffix), slice(0, size))


def last_rows(info, others, held, z, pieces, sel, other, top, level, head_bits):
    xh, xl = held[:2]
    rows, columns = xh.shape
    n = sel.shape[1]
    inputs = (info, *others, xh, xl, *z, sel, other, *pieces)
    halves = ((rows if head_bits else 2 * rows, n), F32)
    return call(
        functools.partial(last_rows_kernel, top, head_bits, len(others)),
        f"rows_{level}",
        inputs,
        [SMEM] * (1 + len(others)) + [VMEM] * (len(inputs) - 1 - len(others)),
        [halves, halves, ((n, columns), F32)],
        [VMEM] * 3,
        [pltpu.VMEM((n, columns), BF16)] * 2,
        12,
        10**9,
    )


def last_kernel(heads, half, top, level, info, rate_ref, b_ref, c_ref, cw, gxa, gxb, r_ref, low_ref, gl_in,
                gx_hbm, gl_ref, pw, ph, pq, rh, rl, of, gls, sems):
    rows, columns = cw.shape
    stretches = rows // STRETCH
    mid = stretches // 2
    me = info[0]
    base = (me * rows - half).astype(F32)
    prefix, suffix = masks(info, stretches)
    upper = ((me >> top) & 1) == 1
    gls[...] = gl_in[...]

    pieces = sems.shape[0]
    per = stretches // pieces

    def copy(k):
        at = pl.ds(k * per * STRETCH, per * STRETCH)
        return pltpu.make_async_copy(of.at[at], gx_hbm.at[at], sems.at[k])

    def finish(any_low):
        if any_low:
            rh[...], rl[...] = split(low_ref[...] + r_ref[...] * jnp.where(upper, 0.0, 1.0))
            pw[...] = split_rows(scaled_rows(b_ref[...], suffix))
        for k in range(pieces):

            def one(j, cols):
                inner, outer = decays(rate_ref, j, base, 1.0, stretches)
                extra = spread(pw[rs(k * per, per)], rh, rl, cols) if any_low else None
                for i in range(k * per, (k + 1) * per):
                    g = gxa[rs(i), cols] if i < mid else gxb[rs(i - mid), cols]
                    if any_low:
                        g = g + extra[rs(i - k * per)]
                    of[rs(i), cols] = g * (inner * outer[i : i + 1, :])

            each_chunk(columns, one)
            copy(k).start()

    below = (2 << top) - 1

    @pl.when((me & below) == below)
    def _():
        finish(False)

    @pl.when((me & below) != below)
    def _():
        finish(True)

    @pl.when(upper)
    def _():
        rh[...], rl[...] = split(r_ref[...])
        pw[...] = split_rows(scaled_rows(c_ref[...], prefix))
        gls[...] += level_sums(level, heads, pw, cw, rh, rl, ph, pq, head_columns(columns))

    lanes = gl_ref.shape[0]
    gl_ref[...] = gls[...].T[:lanes] * level_scales((lanes, 1), 0, heads)
    for k in range(pieces):
        copy(k).wait()


def last_state(info, rate, held, b, c, gx, state, low, gl, half, top, level, lanes):
    cw = held[2]
    rows, columns = cw.shape
    n = b.shape[1]
    wide = pltpu.VMEM((rows, columns), BF16)
    held_state = pltpu.VMEM((n, columns), BF16)
    return call(
        functools.partial(last_kernel, rate.shape[0], half, top, level),
        f"apply_{level}",
        (info, rate, b, c, cw, *gx, state, low, gl),
        [SMEM] * 2 + [VMEM] * 8,
        [((rows, columns), F32), ((lanes, rows), F32)],
        [ANY, VMEM],
        [
            pltpu.VMEM((rows, 2 * n), BF16),
            wide,
            wide,
            held_state,
            held_state,
            pltpu.VMEM((rows, columns), F32),
            pltpu.VMEM((rows, LANES), F32),
            pltpu.SemaphoreType.DMA((4,)),
        ],
        20,
        3 * 10**9,
    )


def after(x, *others):
    return lax.optimization_barrier((x, *others))[0]


class Swap:
    def __init__(self, info, others, outs, bit):
        self.info, self.others, self.bit, self.phase = info, others, bit, 0
        self.plan = list(reversed(range(bit)))
        if bit == 0:
            self.came = partner(outs[0], 1)
        else:
            self.away, self.kept = outs
            self.came = partner(self.away, 1 << (bit - 1))

    @property
    def done(self):
        return self.phase > self.bit

    def step(self):
        k, bit = self.phase, self.bit
        self.phase += 1
        if k < bit:
            next_bit = self.plan[k + 1] if k < bit - 1 else None
            whole = next_bit == 0
            coded = self.came.shape[0] > self.kept.shape[0]
            outs = sum_step(
                self.info, self.others, self.kept, self.came, bit, k == 0, None if whole else next_bit
            )
            if coded:
                self.gate = outs[-1]
            if whole:
                self.kept = outs[0]
                self.came = partner(outs[0], 1)
            elif next_bit is None:
                self.came = partner(outs[0], 1 << bit)
            else:
                self.away, self.kept = outs
                self.came = partner(self.away, 1 << next_bit)
            return outs[0]
        own = self.came
        apart = [j for j in range(1, 1 << bit) if bit <= 1 or j % 2 == 0]
        self.pieces = [own] + [partner(own, j) for j in apart]
        return own


def local(inputs, cotangent, b_proj, c_proj, decay_rate, level_weight, starts):
    rows = inputs.shape[0]
    heads = decay_rate.shape[0]
    stretches = rows // STRETCH
    seq_count = lax.axis_size("seq")
    seq_bits = seq_count.bit_length() - 1
    head_bits = lax.axis_size("head").bit_length() - 1
    half = seq_count * rows // 2
    me = lax.axis_index("seq").astype(jnp.int32)
    lanes = level_weight.shape[0] * heads
    level0 = stretches.bit_length()
    top = seq_bits - 1
    coded = seq_bits == 3
    others = [partner(starts, k) for k in range(1, 2 if coded else 1 << top)]
    info = jnp.concatenate([me.reshape(1), lax.axis_index("head").astype(jnp.int32).reshape(1), starts])
    raw_lam = level_weight.reshape(lanes, rows)
    if lanes < LANES:
        raw_lam = jnp.pad(raw_lam, ((0, LANES - lanes), (0, 0)))

    order = [*range(1, seq_bits), 0]
    b = order[0]
    *held, bv, cv, zh, zl, away, kept = first_state(
        info, decay_rate, inputs, cotangent, b_proj, c_proj, raw_lam, level0 + b, b, half
    )
    swaps = {b: Swap(info, others, (away, kept), b)}
    zs = {b: (zh, zl)}
    tied = after(info, kept)
    for b in order[1:]:
        zh, zl, *outs = send_state(
            tied, heads, held, bv, cv, level0 + b, b, others if coded and b == top else ()
        )
        zs[b] = (zh, zl)
        swaps[b] = Swap(info, others, outs, b)
        tied = after(info, outs[-1])
    waits = [swaps[b].step() for b in range(1, seq_bits)]
    part0 = local_levels(after(tied, *waits), heads, held, bv, cv, 0)
    for b in range(1, seq_bits):
        swaps[b].info = after(info, part0[3])
        swaps[b].came = after(swaps[b].came, part0[3])
    waits = [swaps[b].step() for b in range(1, seq_bits)]
    part1 = local_levels(after(info, part0[3], *waits), heads, held, bv, cv, 1)
    waits = []
    for b in range(seq_bits):
        swaps[b].info = after(info, part1[3])
        swaps[b].came = after(swaps[b].came, part1[3])
        while not swaps[b].done:
            waits.append(swaps[b].step())
    sums = [p[k] for k in range(1, 4) for p in (part0, part1)]
    early = tuple(range(top))
    low, gl, sel, other = early_states(
        after(info, *waits), others, heads, held, bv, cv, sums, [z for b in early for z in zs[b]],
        [swaps[b].pieces for b in early], early, top, level0,
    )
    level = level0 + top
    pieces = [after(p, other) for p in swaps[top].pieces]
    known = [swaps[top].gate] if coded else others
    away, kept, state = last_rows(info, known, held, zs[top], pieces, sel, other, top, level, head_bits)
    came = head_partner(away, 0)
    for bit in range(1, head_bits):
        away, kept = head_step(info, kept, came, bit, head_bits)
        came = head_partner(away, bit)
    grad_x, gl = last_state(
        after(info, kept), decay_rate, held, bv, cv, (part0[0], part1[0]), state, low, gl, half, top, level, lanes
    )
    both = after(kept, gl) + after(came, gl)
    size = both.shape[0] // 2
    sel, other = both[:size], both[size:]
    upper = ((after(me, gl) >> top) & 1) == 1
    return (grad_x, jnp.where(upper, other, sel), jnp.where(upper, sel, other), gl.reshape(level_weight.shape))


def solution(mesh):
    return jax.shard_map(
        local,
        mesh=mesh,
        in_specs=(
            P("seq", "head"),
            P("seq", "head"),
            P("seq", None),
            P("seq", None),
            P("head"),
            P(None, "head", "seq"),
            P("seq"),
        ),
        out_specs=(
            P("seq", "head"),
            P(("seq", "head"), None),
            P(("seq", "head"), None),
            P(None, "head", "seq"),
        ),
        check_vma=False,
    )
```
